32 devices in a mesh: pairs: 8 (over z, y), orb: 4 (over x, core).
Axes of the slice: x: 2, y: 2, z: 4, core: 2. Of those that a mesh axis runs over, the one named last changes fastest.
Arguments:
- amplitudes: float32 [128, 128, 128], P(('pairs', 'orb')), may hold values from -4 to 4
- integrals: bfloat16 [128, 128, 128], P(('pairs', 'orb')), may hold values from -6 to 6
- energies: float32 [128, 128], P(('pairs', 'orb')), may hold values from 0.5 to 4
- intersections: bfloat16 [128, 16, 128, 128], P(('pairs', 'orb')), may hold values from -0.5 to 0.5
- couplings: float32 [128, 16], P(('pairs', 'orb')), may hold values from -2 to 2
- projector: float32 [128, 128], P(('pairs', 'orb')), may hold values from -0.5 to 0.5
- pair_orbitals: int32 [128, 2], P(('pairs', 'orb')), may hold values from 0 to 3
- coupled: int32 [128, 16], replicated, may hold values from 0 to 127, as said below
- pair_slot: int32 [128], replicated, may hold values from 0 to 127, as said below
Outputs:
- final_amplitudes: float32 [128, 128, 128], P(('pairs', 'orb'))
- residual: float32 [128, 128, 128], P(('pairs', 'orb'))
The draws below stay inside these ranges and needn't reach their ends.
Inputs may be any that keep to these rules, and one draw needn't show every extreme that they name: `coupled`: each row holds 16 different pair ids, never the id of the pair held in that row's slot. The rows of one device name at most 3 different pairs held by the devices of any one pairs index, and exactly 3 held by the devices of the next pairs index. `pair_slot`: A permutation of the pair ids.
All inputs are finite; a program needn't handle non-finite values.
Results may differ from the reference program's by a relative error of at most 0.00037.
Values may be sent and summed in bfloat16 or wider, within the bound.
No kernel may reach another device: no remote copies, remote signals or barrier semaphores. Data moves between devices by JAX's collectives and lax.ppermute only.
A program may use at most 64 MiB of HBM per device.

```python
import math
import jax
import jax.numpy as jnp
from jax import lax

NV = 128
NB = 16
ITERS = 2
PAIRS_DEV = 4
TOTAL = 128
NOCC = 4
CAP = 3
N_PAIRS = 8
N_ORB = 4


def plan_coupling(key):
    base_key = jax.random.fold_in(key, 31)
    key_perm, key_pick, key_score = jax.random.split(base_key, 3)
    devices = TOTAL // PAIRS_DEV
    group = PAIRS_DEV * N_ORB
    slot_of = jax.random.permutation(key_perm, TOTAL).astype(jnp.int32)
    pair_of = jnp.argsort(slot_of).astype(jnp.int32)
    jitter = jax.random.randint(key_pick, (devices, N_PAIRS, group), 0, 2 ** 20) * group + jnp.arange(group)
    chosen = jnp.argsort(jitter, axis=2)[:, :, :CAP].astype(jnp.int32)
    candidate = (jnp.arange(N_PAIRS)[None, :, None] * group + chosen).reshape(devices, N_PAIRS * CAP)
    columns = N_PAIRS * CAP
    scores = jax.random.randint(key_score, (TOTAL, columns), 0, 2 ** 20) * columns + jnp.arange(columns)
    row_ids = jnp.arange(TOTAL)
    owner_dev = row_ids // PAIRS_DEV
    owner_group = owner_dev // N_ORB
    row_cand = candidate[owner_dev]
    source = jnp.arange(columns) // CAP
    forced = (row_ids % PAIRS_DEV == 0)[:, None] & (source[None, :] == ((owner_group + 1) % N_PAIRS)[:, None])
    scores = jnp.where(forced, scores + 2 ** 30, scores)
    scores = jnp.where(row_cand == row_ids[:, None], -1, scores)
    top_vals, picked = lax.top_k(scores, NB)
    neighbour = jnp.take_along_axis(row_cand, picked, axis=1)
    return (slot_of, pair_of[neighbour].astype(jnp.int32))


def draw_coupled(key, part):
    return plan_coupling(key)[1]


def draw_pair_slot(key, part):
    return plan_coupling(key)[0]


def place_ends(result, stream_key, low, high):
    index_at = [jax.random.randint(jax.random.fold_in(stream_key, axis), (), 0, length) for axis, length in enumerate(result.shape)]
    widest = result.shape.index(max(result.shape))
    beside = index_at[:widest] + [(index_at[widest] + 1) % result.shape[widest]] + index_at[widest + 1:]
    return result.at[tuple(index_at)].set(low).at[tuple(beside)].set(high)


def block_scale(key, extent, cuts, low, largest):
    loudness, own = 1.0, jax.random.fold_in(key, 6)
    for dim, parts in cuts:
        heights = jnp.exp(jax.random.uniform(jax.random.fold_in(own, dim), (parts,), jnp.float32, low / len(cuts), largest / len(cuts)))
        loudness = loudness * jnp.repeat(heights, extent[dim] // parts).reshape([-1 if axis == dim else 1 for axis in range(len(extent))])
    return loudness


def normal_values(rng, dims, deviation, reach, shards=(), held_as=jnp.bfloat16):
    level = block_scale(rng, dims, shards, -0.22, 0.18) if shards else 1.0
    entries = jax.random.normal(rng, dims, jnp.float32) * deviation * level
    return jnp.minimum(jnp.maximum(entries, -reach), reach).astype(held_as)


def setup_inputs(seed: int = 0) -> dict:
    keys = jax.random.split(jax.random.key(seed), 10)
    return {
        "amplitudes": normal_values(keys[0], (TOTAL, NV, NV), 0.3, 4.0, ((0, 32),), jnp.float32),
        "integrals": normal_values(keys[1], (TOTAL, NV, NV), 1.0, 6.0, ((0, 32),)),
        "energies": jnp.clip(jnp.exp(math.log(4.0) - 2.0794415 * jax.random.uniform(keys[2], (TOTAL, NV), jnp.float32) ** block_scale(keys[2], (TOTAL, NV), ((0, 32),), -0.2, 0.2)), 0.5, 4.0),
        "intersections": normal_values(keys[3], (TOTAL, NB, NV, NV), NV ** -0.5, 0.5, ((0, 32),)),
        "couplings": normal_values(keys[4], (TOTAL, NB), 0.15, 2.0, ((0, 32),), jnp.float32),
        "projector": normal_values(keys[5], (TOTAL, NV), NV ** -0.5, 0.5, ((0, 32),), jnp.float32),
        "pair_orbitals": place_ends(jax.random.randint(keys[6], (TOTAL, 2), 0, NOCC), jax.random.fold_in(keys[6], 1), 0, NOCC - 1).astype(jnp.int32),
        "coupled": draw_coupled(jax.random.fold_in(keys[9], 71), 0),
        "pair_slot": draw_pair_slot(jax.random.fold_in(keys[9], 71), 0),
    }


def reference(amplitudes, integrals, energies, intersections, couplings, projector, pair_orbitals, coupled, pair_slot):
    highest = lax.Precision.HIGHEST
    neighbour = pair_slot[coupled].astype(jnp.int32)
    orbital_ids = jnp.arange(NOCC).astype(jnp.int32)
    first_hot = (pair_orbitals[:, 0:1] == orbital_ids[None, :]).astype(jnp.float32)
    second_hot = (pair_orbitals[:, 1:2] == orbital_ids[None, :]).astype(jnp.float32)
    denom = energies[:, :, None] + energies[:, None, :]
    state = amplitudes
    residual = amplitudes
    for step in range(ITERS):
        blocks = state.astype(jnp.bfloat16)
        blocks = lax.optimization_barrier(blocks)

        def couple_one(items):
            intersection, coeff, index = items
            near = blocks[index].astype(jnp.float32)
            wide = intersection.astype(jnp.float32)
            lifted = jnp.einsum("kab,kbc->kac", wide, near, precision=highest)
            scaled = (coeff[:, None, None] * lifted).astype(jnp.bfloat16)
            scaled = lax.optimization_barrier(scaled).astype(jnp.float32)
            return jnp.einsum("kac,kdc->ad", scaled, wide, precision=highest)

        coupling = lax.map(couple_one, (intersections, couplings, neighbour))
        projected = jnp.einsum("pab,pb->pa", state, projector, precision=highest)
        singles = jnp.dot(first_hot.T, projected, precision=highest) + jnp.dot(second_hot.T, projected, precision=highest)
        left = jnp.dot(first_hot, singles, precision=highest)
        right = jnp.dot(second_hot, singles, precision=highest)
        residual = (integrals.astype(jnp.float32) + energies[:, :, None] * state + state * energies[:, None, :]
                    - coupling + left[:, :, None] * projector[:, None, :] + projector[:, :, None] * right[:, None, :])
        state = state - residual / denom
    return state, residual
```

```python
import functools

import jax
import jax.numpy as jnp
from jax import lax
from jax.experimental import pallas as pl
from jax.experimental.pallas import tpu as pltpu
from jax.sharding import PartitionSpec as P

PAIRS_ORB = 32
ITERS = 2
ROWS = 16
PARTS = 3

F32 = jnp.float32
BF16 = jnp.bfloat16
VMEM = pl.BlockSpec(memory_space=pltpu.VMEM)
SMEM = pl.BlockSpec(memory_space=pltpu.SMEM)
ANY = pl.BlockSpec(memory_space=pl.ANY)
LIMIT = 40 * 1024 * 1024


def eye_mask(width):
    rows = lax.broadcasted_iota(jnp.int32, (width, width), 0)
    cols = lax.broadcasted_iota(jnp.int32, (width, width), 1)
    return rows == cols


def to_row(column, eye):
    return jnp.sum(jnp.where(eye, column, 0.0), axis=0, keepdims=True)


def to_column(row, eye):
    return jnp.sum(jnp.where(eye, row, 0.0), axis=1, keepdims=True)


def split_parts(value):
    parts = []
    for _ in range(PARTS):
        part = value.astype(BF16)
        parts.append(part)
        value = value - part.astype(F32)
    return parts


def tail_rows(value, rows):
    parts = split_parts(value)
    missing = rows - sum(part.shape[0] for part in parts)
    if missing:
        parts.append(jnp.zeros((missing, value.shape[1]), BF16))
    return jnp.concatenate([part.astype(F32) for part in parts], axis=0).astype(BF16)


def join_parts(rows, orbitals):
    rows = rows.astype(F32)
    value = rows[:orbitals]
    for part in range(1, PARTS):
        value = value + rows[part * orbitals : (part + 1) * orbitals]
    return value


def singles_terms(state, projector_row, orbital_a, orbital_b, orbitals, eye):
    projected = to_row(jnp.sum(state * projector_row, axis=1, keepdims=True), eye)
    ids = lax.broadcasted_iota(jnp.int32, (orbitals, 1), 0)
    count = (ids == orbital_a).astype(F32) + (ids == orbital_b).astype(F32)
    return count * projected


def setup_kernel(
    capacity, group, stride, orbitals,
    position, ends, state, projector, dest_rows, own_row, slot_row, slot_col,
    payload, send_index, entry_row,
):
    per_device, width = state.shape[0], state.shape[1]
    eye = eye_mask(width)
    total = jnp.zeros((orbitals, width), F32)
    for s in range(per_device):
        block = state[s]
        payload[pl.ds(s * width, width), :] = block.astype(BF16)
        total += singles_terms(block, projector[pl.ds(s, 1), :], ends[s, 0], ends[s, 1], orbitals, eye)
    payload[pl.ds(per_device * width, payload.shape[0] - per_device * width), :] = tail_rows(
        total, payload.shape[0] - per_device * width
    )

    count = slot_row.shape[1]
    pair_idx = position[0]
    slots = slot_row[...]
    lanes = lax.broadcasted_iota(jnp.int32, (1, count), 1)
    wanted = dest_rows[...]
    run = jnp.zeros((wanted.shape[0], 1), jnp.int32)
    picked = [jnp.zeros((wanted.shape[0], 1), jnp.int32) for _ in range(capacity)]
    for g in range(group):
        pair = jnp.sum(jnp.where(slots == pair_idx * group + g, lanes, 0), axis=1, keepdims=True)
        hit = jnp.max((wanted == pair).astype(jnp.int32), axis=1, keepdims=True)
        for c in range(capacity):
            picked[c] = picked[c] + jnp.where((hit == 1) & (run == c), g, 0)
        run = run + hit
    column = lax.broadcasted_iota(jnp.int32, send_index.shape, 1)
    index = jnp.zeros(send_index.shape, jnp.int32)
    for c in range(capacity):
        index = jnp.where(column == c, picked[c], index)
    send_index[...] = index

    own = own_row[...]
    ids = lax.broadcasted_iota(jnp.int32, (count, own.shape[1]), 0)
    entry = (ids == own).astype(F32)
    mine = jnp.max(entry, axis=1, keepdims=True)
    slots_c = slot_col[...]
    before = (slots_c // group == slots // group) & (slots_c < slots)
    rank = jnp.sum(jnp.where(before, mine, 0.0), axis=0, keepdims=True)
    place = (slots // group).astype(F32) * (stride // ROWS) + rank * (width // ROWS)
    found = jnp.dot(place, entry, precision=lax.Precision.HIGHEST, preferred_element_type=F32)
    entry_row[...] = found.astype(jnp.int32) * ROWS


def select_kernel(capacity, per_device, orbitals, width, send_index, gathered, outgoing):
    blocks = per_device * width
    tail = gathered.shape[1] - blocks
    total = join_parts(gathered[0, pl.ds(blocks, tail), :], orbitals)
    for d in range(1, gathered.shape[0]):
        total += join_parts(gathered[d, pl.ds(blocks, tail), :], orbitals)
    rows = tail_rows(total, tail)
    for p in range(outgoing.shape[0]):
        for c in range(capacity):
            j = send_index[p, c]
            first = pl.multiple_of((j % per_device) * width, ROWS)
            outgoing[p, pl.ds(c * width, width), :] = gathered[j // per_device, pl.ds(first, width), :]
        outgoing[p, pl.ds(capacity * width, tail), :] = rows


def update_kernel(
    last, capacity, orbitals,
    entry_row, couplings, ends, arrived, intersections, state, integrals, energies, projector,
    out_a, out_b, held, sems,
):
    per_device, count, width = intersections.shape[0], intersections.shape[1], intersections.shape[2]
    stride = capacity * width + tail_size(orbitals)
    copies = [
        pltpu.make_async_copy(intersections.at[s], held.at[s], sems.at[s]) for s in range(per_device)
    ]
    for copy in copies:
        copy.start()
    eye = eye_mask(width)
    singles = None
    for p in range(arrived.shape[0] // stride):
        part = join_parts(
            arrived[pl.ds(p * stride + capacity * width, stride - capacity * width), :], orbitals
        )
        singles = part if singles is None else singles + part
    ids = lax.broadcasted_iota(jnp.int32, (orbitals, 1), 0)
    total = jnp.zeros((orbitals, width), F32)
    for s in range(per_device):
        copies[s].wait()
        coupling = jnp.zeros((width, width), F32)
        for k in range(0, count, 2):
            wide = jnp.concatenate([held[s, k], held[s, k + 1]], axis=1)
            scaled = []
            for m in (k, k + 1):
                first = pl.multiple_of(entry_row[0, s * count + m], ROWS)
                near = arrived[pl.ds(first, width), :]
                lifted = jnp.dot(held[s, m], near, preferred_element_type=F32)
                scaled.append((couplings[s, m] * lifted).astype(BF16))
            coupling += lax.dot_general(
                jnp.concatenate(scaled, axis=1), wide, (((1,), (1,)), ((), ())),
                preferred_element_type=F32,
            )
        old = state[s]
        energy = energies[pl.ds(s, 1), :]
        energy_c = to_column(energy, eye)
        proj = projector[pl.ds(s, 1), :]
        proj_c = to_column(proj, eye)
        left = jnp.sum(jnp.where(ids == ends[s, 0], singles, 0.0), axis=0, keepdims=True)
        right = jnp.sum(jnp.where(ids == ends[s, 1], singles, 0.0), axis=0, keepdims=True)
        residual = (
            integrals[s].astype(F32) + energy_c * old + old * energy - coupling
            + to_column(left, eye) * proj + proj_c * right
        )
        new = old - residual / (energy_c + energy)
        if last:
            out_a[s] = new
            out_b[s] = residual
        else:
            out_a[s] = new
            out_b[pl.ds(s * width, width), :] = new.astype(BF16)
            total += singles_terms(new, proj, ends[s, 0], ends[s, 1], orbitals, eye)
    if not last:
        tail = out_b.shape[0] - per_device * width
        out_b[pl.ds(per_device * width, tail), :] = tail_rows(total, tail)


def tail_size(orbitals):
    return -(-PARTS * orbitals // ROWS) * ROWS


def body(
    amplitudes, integrals, energies, intersections, couplings, projector, pair_orbitals, coupled, pair_slot,
):
    pair_count = lax.axis_size("pairs")
    orb_count = lax.axis_size("orb")
    per_device, width = amplitudes.shape[0], amplitudes.shape[1]
    total, near = coupled.shape
    capacity = 1 + near // pair_count
    group = orb_count * per_device
    orbitals = total // PAIRS_ORB
    tail = tail_size(orbitals)
    stride = capacity * width + tail
    pair_idx = lax.axis_index("pairs")
    orb_idx = lax.axis_index("orb")
    params = pltpu.CompilerParams(vmem_limit_bytes=LIMIT)

    by_device = coupled.reshape(pair_count, orb_count, per_device * near)
    dest_rows = lax.dynamic_index_in_dim(by_device, orb_idx, 1, keepdims=False)
    own_row = lax.dynamic_slice_in_dim(dest_rows, pair_idx, 1, 0)
    position = pair_idx.reshape(1).astype(jnp.int32)
    payload, send_index, entry_row = pl.pallas_call(
        functools.partial(setup_kernel, capacity, group, stride, orbitals),
        out_shape=(
            jax.ShapeDtypeStruct((per_device * width + tail, width), BF16),
            jax.ShapeDtypeStruct((pair_count, 128), jnp.int32),
            jax.ShapeDtypeStruct((1, per_device * near), jnp.int32),
        ),
        in_specs=[SMEM, SMEM, VMEM, VMEM, VMEM, VMEM, VMEM, VMEM],
        out_specs=(VMEM, VMEM, VMEM),
        compiler_params=params,
        name="setup",
    )(
        position, pair_orbitals, amplitudes, projector, dest_rows, own_row,
        pair_slot.reshape(1, total), pair_slot.reshape(total, 1),
    )
    state = amplitudes
    for step in range(ITERS):
        last = step == ITERS - 1
        gathered = lax.all_gather(payload, "orb", axis=0, tiled=False)
        outgoing = pl.pallas_call(
            functools.partial(select_kernel, capacity, per_device, orbitals, width),
            out_shape=jax.ShapeDtypeStruct((pair_count, stride, width), BF16),
            in_specs=[SMEM, VMEM],
            out_specs=VMEM,
            compiler_params=params,
            name="select",
        )(send_index, gathered)
        arrived = lax.all_to_all(outgoing, "pairs", split_axis=0, concat_axis=0, tiled=True)
        arrived = arrived.reshape(pair_count * stride, width)
        second = (
            jax.ShapeDtypeStruct(amplitudes.shape, F32)
            if last
            else jax.ShapeDtypeStruct((per_device * width + tail, width), BF16)
        )
        state, payload = pl.pallas_call(
            functools.partial(update_kernel, last, capacity, orbitals),
            out_shape=(jax.ShapeDtypeStruct(amplitudes.shape, F32), second),
            in_specs=[SMEM, SMEM, SMEM, VMEM, ANY, VMEM, VMEM, VMEM, VMEM],
            out_specs=(VMEM, VMEM),
            scratch_shapes=[
                pltpu.VMEM(intersections.shape, BF16),
                pltpu.SemaphoreType.DMA((per_device,)),
            ],
            compiler_params=params,
            name="update",
        )(entry_row, couplings, pair_orbitals, arrived, intersections, state, integrals, energies, projector)
    return state, payload


def solution(mesh):
    split = ("pairs", "orb")
    return jax.shard_map(
        body,
        mesh=mesh,
        in_specs=(
            P(split, None, None),
            P(split, None, None),
            P(split, None),
            P(split, None, None, None),
            P(split, None),
            P(split, None),
            P(split, None),
            P(),
            P(),
        ),
        out_specs=(P(split, None, None), P(split, None, None)),
        check_vma=False,
    )
```

```python
import functools

import jax
import jax.numpy as jnp
from jax import lax
from jax.experimental import pallas as pl
from jax.experimental.pallas import tpu as pltpu
from jax.sharding import PartitionSpec as P

PAIRS_ORB = 32
ITERS = 2
ROWS = 16
PARTS = 3

F32 = jnp.float32
BF16 = jnp.bfloat16
VMEM = pl.BlockSpec(memory_space=pltpu.VMEM)
SMEM = pl.BlockSpec(memory_space=pltpu.SMEM)
ANY = pl.BlockSpec(memory_space=pl.ANY)
HBM = pl.BlockSpec(memory_space=pltpu.HBM)
LIMIT = 40 * 1024 * 1024


def eye_mask(width):
    rows = lax.broadcasted_iota(jnp.int32, (width, width), 0)
    cols = lax.broadcasted_iota(jnp.int32, (width, width), 1)
    return rows == cols


def to_row(column, eye):
    return jnp.sum(jnp.where(eye, column, 0.0), axis=0, keepdims=True)


def to_column(row, eye):
    return jnp.sum(jnp.where(eye, row, 0.0), axis=1, keepdims=True)


def split_parts(value):
    parts = []
    for _ in range(PARTS):
        part = value.astype(BF16)
        parts.append(part)
        value = value - part.astype(F32)
    return parts


def tail_rows(value, rows):
    parts = split_parts(value)
    missing = rows - sum(part.shape[0] for part in parts)
    if missing:
        parts.append(jnp.zeros((missing, value.shape[1]), BF16))
    return jnp.concatenate([part.astype(F32) for part in parts], axis=0).astype(BF16)


def join_parts(rows, orbitals):
    rows = rows.astype(F32)
    value = rows[:orbitals]
    for part in range(1, PARTS):
        value = value + rows[part * orbitals : (part + 1) * orbitals]
    return value


def singles_terms(state, projector_row, orbital_a, orbital_b, orbitals, eye):
    projected = to_row(jnp.sum(state * projector_row, axis=1, keepdims=True), eye)
    ids = lax.broadcasted_iota(jnp.int32, (orbitals, 1), 0)
    count = (ids == orbital_a).astype(F32) + (ids == orbital_b).astype(F32)
    return count * projected


def setup_kernel(
    capacity, stride, orbitals, near,
    ends, state_hbm, projector_hbm, coupled_hbm, slot_hbm,
    payload, send_index, entry_index,
    state, projector, coupled, slot, sems,
):
    copies = [
        pltpu.make_async_copy(src, dst, sems.at[i])
        for i, (src, dst) in enumerate(
            ((coupled_hbm, coupled), (slot_hbm, slot), (projector_hbm, projector), (state_hbm, state))
        )
    ]
    for copy in copies:
        copy.start()
    per_device, width = state.shape[0], state.shape[1]
    count = slot.shape[1]
    pair_count, orb_count = lax.axis_size("pairs"), lax.axis_size("orb")
    pair_idx, orb_idx = lax.axis_index("pairs"), lax.axis_index("orb")
    group = orb_count * per_device
    copies[0].wait()
    copies[1].wait()
    slots = slot[...]
    wanted = coupled[...]
    lanes = lax.broadcasted_iota(jnp.int32, (1, count), 1)

    members = lax.broadcasted_iota(jnp.int32, (group, 1), 0)
    pairs = jnp.sum(jnp.where(slots == pair_idx * group + members, lanes, 0), axis=1, keepdims=True)
    hits = jnp.zeros((group, count), F32)
    for g in range(group):
        hit = jnp.max((wanted == pairs[g : g + 1, :]).astype(F32), axis=0, keepdims=True)
        hits = jnp.where(members == g, hit, hits)
    slot_ids = lax.broadcasted_iota(jnp.int32, (count, 128), 0)
    dest = lax.broadcasted_iota(jnp.int32, (count, 128), 1)
    owner = (slot_ids // per_device == dest * orb_count + orb_idx) & (dest < pair_count)
    needed = jnp.dot(hits, owner.astype(F32), preferred_element_type=F32) > 0.5
    run = jnp.zeros((1, 128), jnp.int32)
    picked = [jnp.zeros((1, 128), jnp.int32) for _ in range(capacity)]
    for g in range(group):
        hit = needed[g : g + 1, :].astype(jnp.int32)
        for c in range(capacity):
            picked[c] = picked[c] + jnp.where((hit == 1) & (run == c), g, 0)
        run = run + hit
    send_index[...] = jnp.concatenate(picked, axis=0)

    eye = eye_mask(count)
    slots_c = jnp.sum(jnp.where(eye, slots, 0), axis=1, keepdims=True)
    first = (pair_idx * orb_count + orb_idx) * per_device
    entries = []
    mine = jnp.zeros((1, count), F32)
    for i in range(per_device):
        own = jnp.sum(jnp.where(lanes == first + i, wanted, 0), axis=1, keepdims=True)
        entries.append((own == lanes).astype(F32))
        mine = jnp.maximum(mine, jnp.max(entries[i], axis=0, keepdims=True))
    mine_c = to_column(mine, eye)
    before = (slots_c // group == slots // group) & (slots_c < slots)
    rank = jnp.sum(jnp.where(before, mine_c, 0.0), axis=0, keepdims=True).astype(jnp.int32)
    place = ((slots // group) ^ (pair_idx & ~(near - 1))) * stride + rank * width
    place = place.astype(F32)
    column = lax.broadcasted_iota(jnp.int32, entry_index.shape, 1)
    index = jnp.zeros(entry_index.shape, F32)
    for i in range(per_device):
        found = jnp.sum(entries[i] * place, axis=1, keepdims=True)
        index = jnp.where(column == i, found, index)
    entry_index[...] = index.astype(jnp.int32)

    eye = eye_mask(width)
    copies[2].wait()
    copies[3].wait()
    total = jnp.zeros((orbitals, width), F32)
    for s in range(per_device):
        block = state[s]
        payload[pl.ds(s * width, width), :] = block.astype(BF16)
        total += singles_terms(block, projector[pl.ds(s, 1), :], ends[0, s], ends[1, s], orbitals, eye)
    tail = payload.shape[0] - per_device * width
    payload[pl.ds(per_device * width, tail), :] = tail_rows(total, tail)


def select_kernel(capacity, per_device, orbitals, width, near, send_index, gathered, out_near, *out_far):
    blocks = per_device * width
    tail = gathered.shape[1] - blocks
    base = lax.axis_index("pairs") & ~(near - 1)
    total = join_parts(gathered[0, pl.ds(blocks, tail), :], orbitals)
    for d in range(1, gathered.shape[0]):
        total += join_parts(gathered[d, pl.ds(blocks, tail), :], orbitals)
    rows = tail_rows(total, tail)
    outs = [(base + i, out_near.at[i]) for i in range(near)]
    outs += [(lax.axis_index("pairs") ^ (near + i), out) for i, out in enumerate(out_far)]
    for dest, out in outs:
        for c in range(capacity):
            j = send_index[c, dest]
            first = pl.multiple_of((j % per_device) * width, ROWS)
            out[pl.ds(c * width, width), :] = gathered[j // per_device, pl.ds(first, width), :]
        out[pl.ds(capacity * width, tail), :] = rows


def update_kernel(
    last, capacity, orbitals, sources,
    entry_index, couplings, ends, *refs,
):
    near, far = refs[0], refs[1:sources]
    intersections, state, integrals, energies, projector, out_a, out_b, held, arrived, sems = refs[sources:]
    per_device, count, width = intersections.shape[0], intersections.shape[1], intersections.shape[2]
    stride = capacity * width + tail_size(orbitals)
    copies = [
        pltpu.make_async_copy(intersections.at[s], held.at[s], sems.at[s]) for s in range(per_device)
    ]
    for copy in copies:
        copy.start()
    half = near.shape[0]
    for i in range(half):
        arrived[pl.ds(i * stride, stride), :] = near[i]
    for i in range(len(far)):
        place = (lax.axis_index("pairs") ^ (half + i)) ^ (lax.axis_index("pairs") & ~(half - 1))
        arrived[pl.ds(pl.multiple_of(place * stride, ROWS), stride), :] = far[i][...]
    eye = eye_mask(width)
    singles = None
    for p in range(arrived.shape[0] // stride):
        part = join_parts(
            arrived[pl.ds(p * stride + capacity * width, stride - capacity * width), :], orbitals
        )
        singles = part if singles is None else singles + part
    ids = lax.broadcasted_iota(jnp.int32, (orbitals, 1), 0)
    total = jnp.zeros((orbitals, width), F32)
    for s in range(per_device):
        copies[s].wait()
        coupling = jnp.zeros((width, width), F32)
        for k in range(0, count, 2):
            wide = jnp.concatenate([held[s, k], held[s, k + 1]], axis=1)
            scaled = []
            for m in (k, k + 1):
                first = pl.multiple_of(entry_index[m, s], ROWS)
                near = arrived[pl.ds(first, width), :]
                lifted = jnp.dot(held[s, m], near, preferred_element_type=F32)
                scaled.append((couplings[s, m] * lifted).astype(BF16))
            coupling += lax.dot_general(
                jnp.concatenate(scaled, axis=1), wide, (((1,), (1,)), ((), ())),
                preferred_element_type=F32,
            )
        old = state[s]
        energy = energies[pl.ds(s, 1), :]
        energy_c = to_column(energy, eye)
        proj = projector[pl.ds(s, 1), :]
        proj_c = to_column(proj, eye)
        left = jnp.sum(jnp.where(ids == ends[0, s], singles, 0.0), axis=0, keepdims=True)
        right = jnp.sum(jnp.where(ids == ends[1, s], singles, 0.0), axis=0, keepdims=True)
        residual = (
            integrals[s].astype(F32) + energy_c * old + old * energy - coupling
            + to_column(left, eye) * proj + proj_c * right
        )
        new = old - residual / (energy_c + energy)
        if last:
            out_a[s] = new
            out_b[s] = residual
        else:
            out_a[s] = new
            out_b[pl.ds(s * width, width), :] = new.astype(BF16)
            total += singles_terms(new, proj, ends[0, s], ends[1, s], orbitals, eye)
    if not last:
        tail = out_b.shape[0] - per_device * width
        out_b[pl.ds(per_device * width, tail), :] = tail_rows(total, tail)


def tail_size(orbitals):
    return -(-PARTS * orbitals // ROWS) * ROWS


def body(
    amplitudes, integrals, energies, intersections, couplings, projector, pair_orbitals, coupled, pair_slot,
):
    pair_count = lax.axis_size("pairs")
    per_device, width = amplitudes.shape[0], amplitudes.shape[1]
    total, neighbours = coupled.shape
    capacity = 1 + neighbours // pair_count
    orbitals = total // PAIRS_ORB
    tail = tail_size(orbitals)
    stride = capacity * width + tail
    params = pltpu.CompilerParams(vmem_limit_bytes=LIMIT)

    near = pair_count // 2 if pair_count <= 8 else pair_count
    ends = pair_orbitals.T
    payload, send_index, entry_index = pl.pallas_call(
        functools.partial(setup_kernel, capacity, stride, orbitals, near),
        out_shape=(
            jax.ShapeDtypeStruct((per_device * width + tail, width), BF16),
            jax.ShapeDtypeStruct((capacity, 128), jnp.int32),
            jax.ShapeDtypeStruct((neighbours, 128), jnp.int32),
        ),
        in_specs=[SMEM, HBM, HBM, HBM, HBM],
        out_specs=(VMEM, VMEM, VMEM),
        scratch_shapes=[
            pltpu.VMEM(amplitudes.shape, F32),
            pltpu.VMEM(projector.shape, F32),
            pltpu.VMEM((neighbours, total), jnp.int32),
            pltpu.VMEM((1, total), jnp.int32),
            pltpu.SemaphoreType.DMA((4,)),
        ],
        compiler_params=params,
        name="setup",
    )(ends, amplitudes, projector, coupled.T, pair_slot.reshape(1, total))
    entry_index = entry_index[:, :per_device]
    state = amplitudes
    sources = 1 + pair_count - near
    groups = [[i + j for j in range(near)] for i in range(0, pair_count, near)]
    for step in range(ITERS):
        last = step == ITERS - 1
        gathered = lax.all_gather(payload, "orb", axis=0, tiled=False)
        outgoing = pl.pallas_call(
            functools.partial(select_kernel, capacity, per_device, orbitals, width, near),
            out_shape=[jax.ShapeDtypeStruct((near, stride, width), BF16)]
            + [jax.ShapeDtypeStruct((stride, width), BF16)] * (sources - 1),
            in_specs=[SMEM, VMEM],
            out_specs=[VMEM] * sources,
            compiler_params=params,
            name="select",
        )(send_index, gathered)
        arrived = [
            lax.ppermute(outgoing[1 + i], "pairs", [(p, p ^ (near + i)) for p in range(pair_count)])
            for i in range(sources - 1)
        ]
        arrived = [
            lax.all_to_all(
                outgoing[0], "pairs", split_axis=0, concat_axis=0, axis_index_groups=groups, tiled=True
            )
        ] + arrived
        second = (
            jax.ShapeDtypeStruct(amplitudes.shape, F32)
            if last
            else jax.ShapeDtypeStruct((per_device * width + tail, width), BF16)
        )
        state, payload = pl.pallas_call(
            functools.partial(update_kernel, last, capacity, orbitals, sources),
            out_shape=(jax.ShapeDtypeStruct(amplitudes.shape, F32), second),
            in_specs=[SMEM, SMEM, SMEM] + [VMEM] * sources + [ANY, VMEM, VMEM, VMEM, VMEM],
            out_specs=(VMEM, VMEM),
            scratch_shapes=[
                pltpu.VMEM(intersections.shape, BF16),
                pltpu.VMEM((pair_count * stride, width), BF16),
                pltpu.SemaphoreType.DMA((per_device,)),
            ],
            compiler_params=params,
            name="update",
        )(
            entry_index, couplings, ends, *arrived, intersections, state, integrals, energies, projector,
        )
    return state, payload


def solution(mesh):
    split = ("pairs", "orb")
    return jax.shard_map(
        body,
        mesh=mesh,
        in_specs=(
            P(split, None, None),
            P(split, None, None),
            P(split, None),
            P(split, None, None, None),
            P(split, None),
            P(split, None),
            P(split, None),
            P(),
            P(),
        ),
        out_specs=(P(split, None, None), P(split, None, None)),
        check_vma=False,
    )
```

```python
import functools

import jax
import jax.numpy as jnp
from jax import lax
from jax.experimental import pallas as pl
from jax.experimental.pallas import tpu as pltpu
from jax.sharding import PartitionSpec as P

PAIRS_ORB = 32
ITERS = 2
ROWS = 16
PARTS = 3
EARLY = 20_000_000_000
CLOSE = 1_000_000_000

F32 = jnp.float32
BF16 = jnp.bfloat16
VMEM = pl.BlockSpec(memory_space=pltpu.VMEM)
SMEM = pl.BlockSpec(memory_space=pltpu.SMEM)
ANY = pl.BlockSpec(memory_space=pl.ANY)
HBM = pl.BlockSpec(memory_space=pltpu.HBM)
LIMIT = 16 * 1024 * 1024
SMALL = 8 * 1024 * 1024
WHOLE = 60 * 1024 * 1024


def eye_mask(width):
    rows = lax.broadcasted_iota(jnp.int32, (width, width), 0)
    cols = lax.broadcasted_iota(jnp.int32, (width, width), 1)
    return rows == cols


def to_row(column, eye):
    return jnp.sum(jnp.where(eye, column, 0.0), axis=0, keepdims=True)


def to_column(row, eye):
    return jnp.sum(jnp.where(eye, row, 0.0), axis=1, keepdims=True)


def split_parts(value):
    parts = []
    for _ in range(PARTS):
        part = value.astype(BF16)
        parts.append(part)
        value = value - part.astype(F32)
    return parts


def tail_rows(value, rows):
    parts = split_parts(value)
    missing = rows - sum(part.shape[0] for part in parts)
    if missing:
        parts.append(jnp.zeros((missing, value.shape[1]), BF16))
    return jnp.concatenate([part.astype(F32) for part in parts], axis=0).astype(BF16)


def join_parts(rows, orbitals):
    rows = rows.astype(F32)
    value = rows[:orbitals]
    for part in range(1, PARTS):
        value = value + rows[part * orbitals : (part + 1) * orbitals]
    return value


def singles_terms(state, projector_row, count, eye):
    projected = to_row(jnp.sum(state * projector_row, axis=1, keepdims=True), eye)
    return count * projected


def end_counts(orbitals, per_device, end):
    ids = lax.broadcasted_iota(jnp.int32, (orbitals, 1), 0)
    return [(ids == end(s)).astype(F32) for s in range(per_device)]


def fetch(pairs, sems):
    copies = [pltpu.make_async_copy(src, dst, sems.at[i]) for i, (src, dst) in enumerate(pairs)]
    for copy in copies:
        copy.start()
    return copies


def setup_kernel(
    capacity, orbitals,
    ends, state_hbm, projector_hbm, coupled_hbm, slot_hbm,
    payload, index,
    state, projector, coupled, slot, sems,
):
    copies = fetch(
        ((coupled_hbm, coupled), (slot_hbm, slot), (projector_hbm, projector), (state_hbm, state)), sems
    )
    per_device, width = state.shape[0], state.shape[1]
    count = slot.shape[1]
    pair_count, orb_count = lax.axis_size("pairs"), lax.axis_size("orb")
    pair_idx, orb_idx = lax.axis_index("pairs"), lax.axis_index("orb")
    group = orb_count * per_device
    lanes_out = index.shape[1]
    copies[0].wait()
    copies[1].wait()
    slots = slot[...]
    wanted = coupled[...]
    lanes = lax.broadcasted_iota(jnp.int32, (1, count), 1)
    members = lax.broadcasted_iota(jnp.int32, (group, 1), 0)
    pairs = jnp.sum(jnp.where(slots == pair_idx * group + members, lanes, 0), axis=1, keepdims=True)
    hits = jnp.zeros((group, count), F32)
    for g in range(group):
        hit = jnp.max((wanted == pairs[g : g + 1, :]).astype(F32), axis=0, keepdims=True)
        hits = jnp.where(members == g, hit, hits)
    slot_ids = lax.broadcasted_iota(jnp.int32, (count, lanes_out), 0)
    dest = lax.broadcasted_iota(jnp.int32, (count, lanes_out), 1)
    owner = (slot_ids // per_device == dest * orb_count + orb_idx) & (dest < pair_count)
    needed = jnp.dot(hits, owner.astype(F32), preferred_element_type=F32) > 0.5
    run = jnp.zeros((1, lanes_out), jnp.int32)
    picked = [jnp.zeros((1, lanes_out), jnp.int32) for _ in range(capacity)]
    for g in range(group):
        hit = needed[g : g + 1, :].astype(jnp.int32)
        for c in range(capacity):
            picked[c] = picked[c] + jnp.where((hit == 1) & (run == c), g, 0)
        run = run + hit
    for c, row in enumerate(picked):
        index[pl.ds(c, 1), :] = row

    eye = eye_mask(width)
    copies[2].wait()
    copies[3].wait()
    total = jnp.zeros((orbitals, width), F32)
    counts_a = end_counts(orbitals, per_device, lambda s: ends[0, s])
    counts_b = end_counts(orbitals, per_device, lambda s: ends[1, s])
    for s in range(per_device):
        block = state[s]
        payload[pl.ds(s * width, width), :] = block.astype(BF16)
        total += singles_terms(block, projector[pl.ds(s, 1), :], counts_a[s] + counts_b[s], eye)
    tail = payload.shape[0] - per_device * width
    payload[pl.ds(per_device * width, tail), :] = tail_rows(total, tail)


def tables_kernel(
    capacity, near,
    coupled_hbm, slot_hbm, couplings_hbm,
    index, coefficients,
    coupled, slot, couplings, sems,
):
    copies = fetch(((coupled_hbm, coupled), (slot_hbm, slot), (couplings_hbm, couplings)), sems)
    neighbours, count = coupled.shape
    per_device = couplings.shape[0]
    orb_count = lax.axis_size("orb")
    pair_idx, orb_idx = lax.axis_index("pairs"), lax.axis_index("orb")
    group = orb_count * per_device
    lanes_out = index.shape[1]
    for copy in copies:
        copy.wait()
    slots = slot[...]
    wanted = coupled[...]
    lanes = lax.broadcasted_iota(jnp.int32, (1, count), 1)
    eye = eye_mask(count)
    slots_c = jnp.sum(jnp.where(eye, slots, 0), axis=1, keepdims=True)
    first = (pair_idx * orb_count + orb_idx) * per_device
    entries = []
    mine = jnp.zeros((1, count), F32)
    for i in range(per_device):
        own = jnp.sum(jnp.where(lanes == first + i, wanted, 0), axis=1, keepdims=True)
        entries.append((own == lanes).astype(F32))
        mine = jnp.maximum(mine, jnp.max(entries[i], axis=0, keepdims=True))
    mine_c = to_column(mine, eye)
    before = (slots_c // group == slots // group) & (slots_c < slots)
    rank = jnp.sum(jnp.where(before, mine_c, 0.0), axis=0, keepdims=True).astype(jnp.int32)
    source = slots // group
    flip = source ^ pair_idx
    place = jnp.where(flip < near, source ^ (pair_idx & ~(near - 1)), flip) * capacity + rank
    place = place.astype(F32)
    ids = lax.broadcasted_iota(jnp.int32, (neighbours, 1), 0)
    square = eye_mask(neighbours)
    column = lax.broadcasted_iota(jnp.int32, (neighbours, lanes_out), 1)
    for i in range(per_device):
        found = jnp.sum(entries[i] * place, axis=1, keepdims=True).astype(jnp.int32)
        match = found == column
        index[pl.ds(i, 1), :] = jnp.sum(jnp.where(match, ids, 0), axis=0, keepdims=True)
        value = to_column(couplings[pl.ds(i, 1), :], square)
        coefficients[pl.ds(i, 1), :] = jnp.sum(jnp.where(match, value, 0.0), axis=0, keepdims=True)


def select_kernel(capacity, per_device, orbitals, width, mask, flips, index, gathered, *outs):
    blocks = per_device * width
    tail = gathered.shape[1] - blocks
    here = lax.axis_index("pairs")
    total = join_parts(gathered[0, pl.ds(blocks, tail), :], orbitals)
    for d in range(1, gathered.shape[0]):
        total += join_parts(gathered[d, pl.ds(blocks, tail), :], orbitals)
    rows = tail_rows(total, tail)
    for flip, out in zip(flips, outs):
        dest = (here & mask) ^ flip
        for c in range(capacity):
            j = index[c, dest]
            first = pl.multiple_of((j % per_device) * width, ROWS)
            out[pl.ds(c * width, width), :] = gathered[j // per_device, pl.ds(first, width), :]
        out[pl.ds(capacity * width, tail), :] = rows


def add_blocks(capacity, orbitals, index, coefficients, intersections, blocks, coupling, singles):
    per_device, width = intersections.shape[0], intersections.shape[2]
    slots = [(place * capacity + c, ref, c * width) for place, ref in blocks for c in range(capacity)]
    wide = [[] for _ in range(per_device)]
    scaled = [[] for _ in range(per_device)]
    empty = jnp.zeros((width, width), BF16)
    for p in range(0, len(slots), 2):
        part = slots[p : p + 2]
        mixing = [
            jnp.concatenate([intersections[s, index[s, lane]] for lane, _, _ in part], axis=1)
            for s in range(per_device)
        ]
        near = [ref[pl.ds(row, width), :] for _, ref, row in part]
        if len(part) == 2:
            near = jnp.concatenate(
                [jnp.concatenate([near[0], empty], axis=1), jnp.concatenate([empty, near[1]], axis=1)], axis=0
            )
        else:
            near = near[0]
        lifted = jnp.dot(jnp.concatenate(mixing, axis=0), near, preferred_element_type=F32)
        for s in range(per_device):
            wide[s].append(mixing[s])
            for i, (lane, _, _) in enumerate(part):
                block = lifted[s * width : (s + 1) * width, i * width : (i + 1) * width]
                scaled[s].append((coefficients[s, lane] * block).astype(BF16))
    for s in range(per_device):
        if slots:
            coupling[s] = coupling[s] + lax.dot_general(
                jnp.concatenate(scaled[s], axis=1), jnp.concatenate(wide[s], axis=1),
                (((1,), (1,)), ((), ())), preferred_element_type=F32,
            )
    for _, ref in blocks:
        tail = ref.shape[0] - capacity * width
        singles = singles + join_parts(ref[pl.ds(capacity * width, tail), :], orbitals)
    return singles


def gather_terms(capacity, orbitals, index, coefficients, intersections, near, far, first, before):
    per_device, width = intersections.shape[0], intersections.shape[2]
    coupling = [jnp.zeros((width, width), F32) for _ in range(per_device)]
    singles = jnp.zeros((orbitals, width), F32)
    if before is not None:
        coupling = [before[pl.ds(s * width, width), :] for s in range(per_device)]
        singles = before[pl.ds(per_device * width, orbitals), :]
    operands = (capacity, orbitals, index, coefficients, intersections)
    blocks = [(first + i, ref) for i, ref in enumerate(far)]
    count = 0 if near is None else near.shape[0]
    unit = min(count, 4)
    if count <= unit:
        blocks = [(i, near.at[i]) for i in range(count)] + blocks
    else:

        def step(i, carry):
            parts = list(carry[:-1])
            some = [(i * unit + u, near.at[i * unit + u]) for u in range(unit)]
            total = add_blocks(*operands, some, parts, carry[-1])
            return (*parts, total)

        *coupling, singles = lax.fori_loop(0, count // unit, step, (*coupling, singles))
    singles = add_blocks(*operands, blocks, coupling, singles)
    return coupling, singles


def terms_kernel(capacity, orbitals, has_before, has_near, first, index, coefficients, intersections, *refs):
    out = refs[-1]
    refs = list(refs[:-1])
    before = refs.pop(0) if has_before else None
    near = refs.pop(0) if has_near else None
    coupling, singles = gather_terms(
        capacity, orbitals, index, coefficients, intersections, near, refs, first, before
    )
    width = intersections.shape[2]
    for s, part in enumerate(coupling):
        out[pl.ds(s * width, width), :] = part
    out[pl.ds(len(coupling) * width, orbitals), :] = singles


def update_kernel(
    last, capacity, orbitals, first, far_count,
    index, coefficients, ends, intersections, before, *refs,
):
    far = refs[:far_count]
    state, integrals, energies, projector, out_a, out_b = refs[far_count:]
    per_device, width = state.shape[0], state.shape[1]
    coupling, singles = gather_terms(
        capacity, orbitals, index, coefficients, intersections, None, far, first, before
    )
    eye = eye_mask(width)
    total = jnp.zeros((orbitals, width), F32)
    counts_a = end_counts(orbitals, per_device, lambda s: ends[0, s])
    counts_b = end_counts(orbitals, per_device, lambda s: ends[1, s])
    for s in range(per_device):
        old = state[s]
        energy = energies[pl.ds(s, 1), :]
        energy_c = to_column(energy, eye)
        proj = projector[pl.ds(s, 1), :]
        proj_c = to_column(proj, eye)
        left = jnp.sum(counts_a[s] * singles, axis=0, keepdims=True)
        right = jnp.sum(counts_b[s] * singles, axis=0, keepdims=True)
        residual = (
            integrals[s].astype(F32) + energy_c * old + old * energy - coupling[s]
            + to_column(left, eye) * proj + proj_c * right
        )
        new = old - residual / (energy_c + energy)
        out_a[s] = new
        if last:
            out_b[s] = residual
        else:
            out_b[pl.ds(s * width, width), :] = new.astype(BF16)
            total += singles_terms(new, proj, counts_a[s] + counts_b[s], eye)
    if not last:
        tail = out_b.shape[0] - per_device * width
        out_b[pl.ds(per_device * width, tail), :] = tail_rows(total, tail)


def tail_size(orbitals):
    return -(-PARTS * orbitals // ROWS) * ROWS


def cost(flops):
    return pl.CostEstimate(flops=flops, bytes_accessed=0, transcendentals=0)


def body(
    amplitudes, integrals, energies, intersections, couplings, projector, pair_orbitals, coupled, pair_slot,
):
    pair_count = lax.axis_size("pairs")
    per_device, width = amplitudes.shape[0], amplitudes.shape[1]
    total, neighbours = coupled.shape
    capacity = 1 + neighbours // pair_count
    orbitals = total // PAIRS_ORB
    tail = tail_size(orbitals)
    stride = capacity * width + tail
    near = pair_count // 2 if pair_count <= 8 else pair_count
    lanes = -(-pair_count * capacity // 128) * 128
    ends = pair_orbitals.T
    small = pltpu.CompilerParams(vmem_limit_bytes=SMALL)
    params = pltpu.CompilerParams(vmem_limit_bytes=LIMIT)
    block_shape = jax.ShapeDtypeStruct((stride, width), BF16)
    terms_shape = jax.ShapeDtypeStruct((per_device * width + -(-orbitals // 8) * 8, width), F32)
    payload_shape = jax.ShapeDtypeStruct((per_device * width + tail, width), BF16)
    payload, send_index = pl.pallas_call(
        functools.partial(setup_kernel, capacity, orbitals),
        out_shape=(payload_shape, jax.ShapeDtypeStruct((8, lanes), jnp.int32)),
        in_specs=[SMEM, HBM, HBM, HBM, HBM],
        out_specs=(VMEM, VMEM),
        scratch_shapes=[
            pltpu.VMEM(amplitudes.shape, F32),
            pltpu.VMEM(projector.shape, F32),
            pltpu.VMEM((neighbours, total), jnp.int32),
            pltpu.VMEM((1, total), jnp.int32),
            pltpu.SemaphoreType.DMA((4,)),
        ],
        compiler_params=pltpu.CompilerParams(vmem_limit_bytes=WHOLE),
        name="setup",
    )(ends, amplitudes, projector, coupled.T, pair_slot.reshape(1, total))
    index, coefficients = pl.pallas_call(
        functools.partial(tables_kernel, capacity, near),
        out_shape=(
            jax.ShapeDtypeStruct((per_device, lanes), jnp.int32),
            jax.ShapeDtypeStruct((per_device, lanes), F32),
        ),
        in_specs=[HBM, HBM, HBM],
        out_specs=(VMEM, VMEM),
        scratch_shapes=[
            pltpu.VMEM((neighbours, total), jnp.int32),
            pltpu.VMEM((1, total), jnp.int32),
            pltpu.VMEM(couplings.shape, F32),
            pltpu.SemaphoreType.DMA((3,)),
        ],
        compiler_params=params,
        name="tables",
    )(coupled.T, pair_slot.reshape(1, total), couplings)

    def select(together, mask, flips, gathered):
        if not len(flips):
            return []

        def kernel(*refs):
            outs = [refs[2].at[i] for i in range(len(flips))] if together else refs[2:]
            select_kernel(capacity, per_device, orbitals, width, mask, list(flips), *refs[:2], *outs)

        shape = [block_shape] * len(flips)
        if together:
            shape = jax.ShapeDtypeStruct((len(flips), stride, width), BF16)
        return pl.pallas_call(
            kernel,
            out_shape=shape,
            in_specs=[SMEM, VMEM],
            out_specs=VMEM if together else [VMEM] * len(flips),
            compiler_params=small,
            name="select",
        )(send_index, gathered)

    def terms(before, close, far, first, flops):
        extra = [x for x in (before, close) if x is not None]
        return pl.pallas_call(
            functools.partial(
                terms_kernel, capacity, orbitals, before is not None, close is not None, first
            ),
            out_shape=terms_shape,
            in_specs=[SMEM, SMEM] + [VMEM] * (1 + len(extra) + len(far)),
            out_specs=VMEM,
            cost_estimate=cost(flops),
            compiler_params=params,
            name="terms",
        )(index, coefficients, intersections, *extra, *far)

    state = amplitudes
    groups = [[i + j for j in range(near)] for i in range(0, pair_count, near)]
    flips = range(near, pair_count)
    ends_of = [x for x in (len(flips) // 2,) if x > 0]
    early = ends_of[-1] if ends_of else 0
    for step in range(ITERS):
        last = step == ITERS - 1
        gathered = lax.all_gather(payload, "orb", axis=0, tiled=False)
        sent = select(False, ~0, flips, gathered)
        far = [
            lax.ppermute(block, "pairs", [(p, p ^ flip) for p in range(pair_count)])
            for flip, block in zip(flips, sent)
        ]
        outgoing = select(True, ~(near - 1), range(near), gathered)
        close = lax.all_to_all(
            outgoing, "pairs", split_axis=0, concat_axis=0, axis_index_groups=groups, tiled=True
        )
        partial, done = None, 0
        for stop in ends_of:
            partial = terms(partial, None, far[done:stop], near + done, EARLY)
            done = stop
        partial = terms(partial, close, [], 0, CLOSE)
        late = far[early:]
        second = jax.ShapeDtypeStruct(amplitudes.shape, F32) if last else payload_shape
        state, payload = pl.pallas_call(
            functools.partial(update_kernel, last, capacity, orbitals, near + early, len(late)),
            out_shape=(jax.ShapeDtypeStruct(amplitudes.shape, F32), second),
            in_specs=[SMEM, SMEM, SMEM] + [VMEM] * (6 + len(late)),
            out_specs=(VMEM, VMEM),
            compiler_params=params,
            name="update",
        )(
            index, coefficients, ends, intersections, partial, *late, state, integrals, energies, projector,
        )
    return state, payload


def solution(mesh):
    split = ("pairs", "orb")
    return jax.shard_map(
        body,
        mesh=mesh,
        in_specs=(
            P(split, None, None),
            P(split, None, None),
            P(split, None),
            P(split, None, None, None),
            P(split, None),
            P(split, None),
            P(split, None),
            P(),
            P(),
        ),
        out_specs=(P(split, None, None), P(split, None, None)),
        check_vma=False,
    )
```

```python
import functools

import jax
import jax.numpy as jnp
from jax import lax
from jax.experimental import pallas as pl
from jax.experimental.pallas import tpu as pltpu
from jax.sharding import PartitionSpec as P

PAIRS_ORB = 32
ITERS = 2
ROWS = 16
PARTS = 3
EARLY = 20_000_000_000
CLOSE = 1_000_000_000

F32 = jnp.float32
BF16 = jnp.bfloat16
VMEM = pl.BlockSpec(memory_space=pltpu.VMEM)
SMEM = pl.BlockSpec(memory_space=pltpu.SMEM)
ANY = pl.BlockSpec(memory_space=pl.ANY)
HBM = pl.BlockSpec(memory_space=pltpu.HBM)
LIMIT = 16 * 1024 * 1024
SMALL = 8 * 1024 * 1024
WHOLE = 60 * 1024 * 1024


def eye_mask(width):
    rows = lax.broadcasted_iota(jnp.int32, (width, width), 0)
    cols = lax.broadcasted_iota(jnp.int32, (width, width), 1)
    return rows == cols


def to_row(column, eye):
    return jnp.sum(jnp.where(eye, column, 0.0), axis=0, keepdims=True)


def to_column(row, eye):
    return jnp.sum(jnp.where(eye, row, 0.0), axis=1, keepdims=True)


def split_parts(value):
    parts = []
    for _ in range(PARTS):
        part = value.astype(BF16)
        parts.append(part)
        value = value - part.astype(F32)
    return parts


def tail_rows(value, rows):
    parts = split_parts(value)
    missing = rows - sum(part.shape[0] for part in parts)
    if missing:
        parts.append(jnp.zeros((missing, value.shape[1]), BF16))
    return jnp.concatenate([part.astype(F32) for part in parts], axis=0).astype(BF16)


def join_parts(rows, orbitals):
    rows = rows.astype(F32)
    value = rows[:orbitals]
    for part in range(1, PARTS):
        value = value + rows[part * orbitals : (part + 1) * orbitals]
    return value


def singles_terms(state, projector_row, count, eye):
    projected = to_row(jnp.sum(state * projector_row, axis=1, keepdims=True), eye)
    return count * projected


def end_counts(orbitals, per_device, end):
    ids = lax.broadcasted_iota(jnp.int32, (orbitals, 1), 0)
    return [(ids == end(s)).astype(F32) for s in range(per_device)]


def fetch(pairs, sems):
    copies = [pltpu.make_async_copy(src, dst, sems.at[i]) for i, (src, dst) in enumerate(pairs)]
    for copy in copies:
        copy.start()
    return copies


def setup_kernel(
    capacity, orbitals, near, mirrors,
    ends, state_hbm, projector_hbm, coupled_hbm, slot_hbm, couplings_hbm,
    payload, index, table, coefficients,
    state, projector, coupled, slot, couplings, sems,
):
    copies = fetch(
        (
            (coupled_hbm, coupled), (slot_hbm, slot), (projector_hbm, projector), (state_hbm, state),
            (couplings_hbm, couplings),
        ),
        sems,
    )
    per_device, width = state.shape[0], state.shape[1]
    count = slot.shape[1]
    pair_count, orb_count = lax.axis_size("pairs"), lax.axis_size("orb")
    pair_idx, orb_idx = lax.axis_index("pairs"), lax.axis_index("orb")
    group = orb_count * per_device
    lanes_out = index.shape[1]
    copies[0].wait()
    copies[1].wait()
    slots = slot[...]
    wanted = coupled[...]
    lanes = lax.broadcasted_iota(jnp.int32, (1, count), 1)
    members = lax.broadcasted_iota(jnp.int32, (group, 1), 0)
    slot_ids = lax.broadcasted_iota(jnp.int32, (count, lanes_out), 0)
    dest = lax.broadcasted_iota(jnp.int32, (count, lanes_out), 1)
    owner = (slot_ids // per_device == dest * orb_count + orb_idx) & (dest < pair_count)
    for m, flip in enumerate(mirrors):
        base = (pair_idx ^ flip) * group
        pairs = jnp.sum(jnp.where(slots == base + members, lanes, 0), axis=1, keepdims=True)
        hits = jnp.zeros((group, count), F32)
        for g in range(group):
            hit = jnp.max((wanted == pairs[g : g + 1, :]).astype(F32), axis=0, keepdims=True)
            hits = jnp.where(members == g, hit, hits)
        needed = jnp.dot(hits, owner.astype(F32), preferred_element_type=F32) > 0.5
        run = jnp.zeros((1, lanes_out), jnp.int32)
        picked = [jnp.zeros((1, lanes_out), jnp.int32) for _ in range(capacity)]
        for g in range(group):
            hit = needed[g : g + 1, :].astype(jnp.int32)
            for c in range(capacity):
                picked[c] = picked[c] + jnp.where((hit == 1) & (run == c), g, 0)
            run = run + hit
        for c, row in enumerate(picked):
            index[pl.ds(m * capacity + c, 1), :] = row

    eye = eye_mask(count)
    slots_c = jnp.sum(jnp.where(eye, slots, 0), axis=1, keepdims=True)
    first = (pair_idx * orb_count + orb_idx) * per_device
    entries = []
    mine = jnp.zeros((1, count), F32)
    for i in range(per_device):
        own = jnp.sum(jnp.where(lanes == first + i, wanted, 0), axis=1, keepdims=True)
        entries.append((own == lanes).astype(F32))
        mine = jnp.maximum(mine, jnp.max(entries[i], axis=0, keepdims=True))
    mine_c = to_column(mine, eye)
    before = (slots_c // group == slots // group) & (slots_c < slots)
    rank = jnp.sum(jnp.where(before, mine_c, 0.0), axis=0, keepdims=True).astype(jnp.int32)
    source = slots // group
    flip = source ^ pair_idx
    place = jnp.where(flip < near, source ^ (pair_idx & ~(near - 1)), flip) * capacity + rank
    place = place.astype(F32)
    neighbours = coupled.shape[0]
    ids = lax.broadcasted_iota(jnp.int32, (neighbours, 1), 0)
    square = eye_mask(neighbours)
    column = lax.broadcasted_iota(jnp.int32, (neighbours, lanes_out), 1)
    copies[4].wait()
    for i in range(per_device):
        found = jnp.sum(entries[i] * place, axis=1, keepdims=True).astype(jnp.int32)
        match = found == column
        table[pl.ds(i, 1), :] = jnp.sum(jnp.where(match, ids, 0), axis=0, keepdims=True)
        value = to_column(couplings[pl.ds(i, 1), :], square)
        coefficients[pl.ds(i, 1), :] = jnp.sum(jnp.where(match, value, 0.0), axis=0, keepdims=True)

    eye = eye_mask(width)
    copies[2].wait()
    copies[3].wait()
    total = jnp.zeros((orbitals, width), F32)
    counts_a = end_counts(orbitals, per_device, lambda s: ends[0, s])
    counts_b = end_counts(orbitals, per_device, lambda s: ends[1, s])
    for s in range(per_device):
        block = state[s]
        payload[pl.ds(s * width, width), :] = block.astype(BF16)
        total += singles_terms(block, projector[pl.ds(s, 1), :], counts_a[s] + counts_b[s], eye)
    tail = payload.shape[0] - per_device * width
    payload[pl.ds(per_device * width, tail), :] = tail_rows(total, tail)


def select_kernel(capacity, per_device, orbitals, width, dests, row, swap, index, gathered, outs):
    blocks = per_device * width
    tail = gathered.shape[1] - blocks
    total = join_parts(gathered[0, pl.ds(blocks, tail), :], orbitals)
    for d in range(1, gathered.shape[0]):
        total += join_parts(gathered[d, pl.ds(blocks, tail), :], orbitals)
    rows = tail_rows(total, tail)
    for dest, out in zip(dests, outs):
        for c in range(capacity):
            j = index[row + c, dest]
            first = pl.multiple_of((j % per_device) * width, ROWS)
            out[pl.ds(c * width, width), :] = gathered[(j // per_device) ^ swap, pl.ds(first, width), :]
        out[pl.ds(capacity * width, tail), :] = rows


def add_blocks(capacity, orbitals, index, coefficients, intersections, blocks, coupling, singles):
    per_device, width = intersections.shape[0], intersections.shape[2]
    slots = [(place * capacity + c, ref, c * width) for place, ref in blocks for c in range(capacity)]
    wide = [[] for _ in range(per_device)]
    scaled = [[] for _ in range(per_device)]
    empty = jnp.zeros((width, width), BF16)
    for p in range(0, len(slots), 2):
        part = slots[p : p + 2]
        mixing = [
            jnp.concatenate([intersections[s, index[s, lane]] for lane, _, _ in part], axis=1)
            for s in range(per_device)
        ]
        near = [ref[pl.ds(row, width), :] for _, ref, row in part]
        if len(part) == 2:
            near = jnp.concatenate(
                [jnp.concatenate([near[0], empty], axis=1), jnp.concatenate([empty, near[1]], axis=1)], axis=0
            )
        else:
            near = near[0]
        lifted = jnp.dot(jnp.concatenate(mixing, axis=0), near, preferred_element_type=F32)
        for s in range(per_device):
            wide[s].append(mixing[s])
            for i, (lane, _, _) in enumerate(part):
                block = lifted[s * width : (s + 1) * width, i * width : (i + 1) * width]
                scaled[s].append((coefficients[s, lane] * block).astype(BF16))
    for s in range(per_device):
        if slots:
            coupling[s] = coupling[s] + lax.dot_general(
                jnp.concatenate(scaled[s], axis=1), jnp.concatenate(wide[s], axis=1),
                (((1,), (1,)), ((), ())), preferred_element_type=F32,
            )
    for _, ref in blocks:
        tail = ref.shape[0] - capacity * width
        singles = singles + join_parts(ref[pl.ds(capacity * width, tail), :], orbitals)
    return singles


def gather_terms(capacity, orbitals, index, coefficients, intersections, every, places, blocks, before):
    per_device, width = intersections.shape[0], intersections.shape[2]
    coupling = [jnp.zeros((width, width), F32) for _ in range(per_device)]
    singles = jnp.zeros((orbitals, width), F32)
    if before is not None:
        coupling = [before[pl.ds(s * width, width), :] for s in range(per_device)]
        singles = before[pl.ds(per_device * width, orbitals), :]
    operands = (capacity, orbitals, index, coefficients, intersections)
    if every is not None:
        unit = min(every.shape[0], 4)

        def step(i, carry):
            parts = list(carry[:-1])
            some = [(i * unit + u, every.at[i * unit + u]) for u in range(unit)]
            total = add_blocks(*operands, some, parts, carry[-1])
            return (*parts, total)

        *coupling, singles = lax.fori_loop(0, every.shape[0] // unit, step, (*coupling, singles))
    singles = add_blocks(*operands, list(zip(places, blocks)), coupling, singles)
    return coupling, singles


def terms_kernel(
    capacity, orbitals, has_before, has_every, places, index, coefficients, intersections, *refs
):
    out = refs[-1]
    refs = list(refs[:-1])
    before = refs.pop(0) if has_before else None
    every = refs.pop(0) if has_every else None
    coupling, singles = gather_terms(
        capacity, orbitals, index, coefficients, intersections, every, places, refs, before
    )
    width = intersections.shape[2]
    for s, part in enumerate(coupling):
        out[pl.ds(s * width, width), :] = part
    out[pl.ds(len(coupling) * width, orbitals), :] = singles


def update_kernel(
    last, capacity, orbitals, places,
    index, coefficients, ends, intersections, before, *refs,
):
    blocks = refs[: len(places)]
    state, integrals, energies, projector, out_a, out_b = refs[len(places) :]
    per_device, width = state.shape[0], state.shape[1]
    coupling, singles = gather_terms(
        capacity, orbitals, index, coefficients, intersections, None, places, blocks, before
    )
    eye = eye_mask(width)
    total = jnp.zeros((orbitals, width), F32)
    counts_a = end_counts(orbitals, per_device, lambda s: ends[0, s])
    counts_b = end_counts(orbitals, per_device, lambda s: ends[1, s])
    for s in range(per_device):
        old = state[s]
        energy = energies[pl.ds(s, 1), :]
        energy_c = to_column(energy, eye)
        proj = projector[pl.ds(s, 1), :]
        proj_c = to_column(proj, eye)
        left = jnp.sum(counts_a[s] * singles, axis=0, keepdims=True)
        right = jnp.sum(counts_b[s] * singles, axis=0, keepdims=True)
        residual = (
            integrals[s].astype(F32) + energy_c * old + old * energy - coupling[s]
            + to_column(left, eye) * proj + proj_c * right
        )
        new = old - residual / (energy_c + energy)
        out_a[s] = new
        if last:
            out_b[s] = residual
        else:
            out_b[pl.ds(s * width, width), :] = new.astype(BF16)
            total += singles_terms(new, proj, counts_a[s] + counts_b[s], eye)
    if not last:
        tail = out_b.shape[0] - per_device * width
        out_b[pl.ds(per_device * width, tail), :] = tail_rows(total, tail)


def tail_size(orbitals):
    return -(-PARTS * orbitals // ROWS) * ROWS


def cost(flops):
    return pl.CostEstimate(flops=flops, bytes_accessed=0, transcendentals=0)


def body(
    amplitudes, integrals, energies, intersections, couplings, projector, pair_orbitals, coupled, pair_slot,
):
    pair_count = lax.axis_size("pairs")
    per_device, width = amplitudes.shape[0], amplitudes.shape[1]
    total, neighbours = coupled.shape
    capacity = 1 + neighbours // pair_count
    orbitals = total // PAIRS_ORB
    tail = tail_size(orbitals)
    stride = capacity * width + tail
    orb_count = lax.axis_size("orb")
    direct = pair_count in (4, 8) and orb_count == 4
    half = pair_count // 2
    mirrors = [0, half] if direct else [0]
    near = 1 if direct else pair_count
    lanes = -(-pair_count * capacity // 128) * 128
    ends = pair_orbitals.T
    small = pltpu.CompilerParams(vmem_limit_bytes=SMALL)
    params = pltpu.CompilerParams(vmem_limit_bytes=LIMIT)
    block_shape = jax.ShapeDtypeStruct((stride, width), BF16)
    terms_shape = jax.ShapeDtypeStruct((per_device * width + -(-orbitals // 8) * 8, width), F32)
    payload_shape = jax.ShapeDtypeStruct((per_device * width + tail, width), BF16)
    payload, send_index, index, coefficients = pl.pallas_call(
        functools.partial(setup_kernel, capacity, orbitals, near, mirrors),
        out_shape=(
            payload_shape,
            jax.ShapeDtypeStruct((-(-len(mirrors) * capacity // 8) * 8, lanes), jnp.int32),
            jax.ShapeDtypeStruct((per_device, lanes), jnp.int32),
            jax.ShapeDtypeStruct((per_device, lanes), F32),
        ),
        in_specs=[SMEM] + [HBM] * 5,
        out_specs=[VMEM] * 4,
        scratch_shapes=[
            pltpu.VMEM(amplitudes.shape, F32),
            pltpu.VMEM(projector.shape, F32),
            pltpu.VMEM((neighbours, total), jnp.int32),
            pltpu.VMEM((1, total), jnp.int32),
            pltpu.VMEM(couplings.shape, F32),
            pltpu.SemaphoreType.DMA((5,)),
        ],
        compiler_params=pltpu.CompilerParams(vmem_limit_bytes=WHOLE),
        name="setup",
    )(ends, amplitudes, projector, coupled.T, pair_slot.reshape(1, total), couplings)

    def join(*parts, after=()):
        def kernel(*refs):
            for i in range(len(parts)):
                refs[-1][i] = refs[i][...]

        return pl.pallas_call(
            kernel,
            out_shape=jax.ShapeDtypeStruct((len(parts), *payload_shape.shape), BF16),
            in_specs=[VMEM] * len(parts) + [ANY] * len(after),
            out_specs=VMEM,
            compiler_params=small,
            cost_estimate=cost(0),
            name="join",
        )(*parts, *after)

    def select(row, flips, gathered):
        def kernel(index, source, *refs):
            outs = refs[: len(flips)]
            here, swap = lax.axis_index("pairs"), 0
            if row:
                held, source, swap = source, refs[-1], lax.axis_index("orb") // 2 * 2
                for c in range(2):
                    for x in range(2):
                        source[2 * x + c] = held[c, x]
            dests = [here ^ flip for flip in flips]
            select_kernel(capacity, per_device, orbitals, width, dests, row, swap, index, source, outs)

        return pl.pallas_call(
            kernel,
            out_shape=[block_shape] * len(flips),
            in_specs=[SMEM, VMEM],
            out_specs=[VMEM] * len(flips),
            scratch_shapes=[pltpu.VMEM((4, *payload_shape.shape), BF16)] if row else [],
            compiler_params=small,
            cost_estimate=cost(0),
            name="select",
        )(send_index, gathered)

    def select_all(gathered):
        def kernel(index, source, out):
            outs = [out.at[i] for i in range(pair_count)]
            select_kernel(capacity, per_device, orbitals, width, range(pair_count), 0, 0, index, source, outs)

        return pl.pallas_call(
            kernel,
            out_shape=jax.ShapeDtypeStruct((pair_count, stride, width), BF16),
            in_specs=[SMEM, VMEM],
            out_specs=VMEM,
            compiler_params=small,
            name="select",
        )(send_index, gathered)

    def exchange(block, axis, flip):
        return lax.ppermute(block, axis, [(p, p ^ flip) for p in range(pair_count * orb_count if isinstance(axis, tuple) else lax.axis_size(axis))])

    def terms(before, every, places, blocks, flops):
        extra = [x for x in (before, every) if x is not None]
        return pl.pallas_call(
            functools.partial(
                terms_kernel, capacity, orbitals, before is not None, every is not None, places
            ),
            out_shape=terms_shape,
            in_specs=[SMEM, SMEM] + [VMEM] * (1 + len(extra) + len(blocks)),
            out_specs=VMEM,
            cost_estimate=cost(flops),
            compiler_params=params,
            name="terms",
        )(index, coefficients, intersections, *extra, *blocks)

    state = amplitudes
    for step in range(ITERS):
        last = step == ITERS - 1
        gathered = lax.all_gather(payload, "orb", axis=0, tiled=False)
        partial, places, late = None, [], []
        if direct:
            mirror = [exchange(payload, "pairs", half), exchange(payload, ("pairs", "orb"), half * orb_count + 2)]
            flips = [0, *range(half - 1, 0, -1)]
            cores = [[o, o + 1] for o in range(0, orb_count, 2)]
            sent = select(0, flips, gathered)
            arrived = [sent[0]] + [exchange(part, "pairs", flip) for flip, part in zip(flips[1:], sent[1:])]
            held = join(*mirror, after=arrived[:1])
            held = lax.all_gather(held, "orb", axis=0, axis_index_groups=cores)
            sent = select(capacity, flips, held)
            partial = terms(None, None, flips + [half], arrived + [sent[0]], EARLY)
            places = [half + flip for flip in flips[1:]]
            late = [exchange(part, "pairs", flip) for flip, part in zip(flips[1:], sent[1:])]
        else:
            outgoing = select_all(gathered)
            every = lax.all_to_all(outgoing, "pairs", split_axis=0, concat_axis=0, tiled=True)
            partial = terms(None, every, [], [], CLOSE)
        second = jax.ShapeDtypeStruct(amplitudes.shape, F32) if last else payload_shape
        state, payload = pl.pallas_call(
            functools.partial(update_kernel, last, capacity, orbitals, places),
            out_shape=(jax.ShapeDtypeStruct(amplitudes.shape, F32), second),
            in_specs=[SMEM, SMEM, SMEM] + [VMEM] * (6 + len(late)),
            out_specs=(VMEM, VMEM),
            compiler_params=params,
            name="update",
        )(
            index, coefficients, ends, intersections, partial, *late, state, integrals, energies, projector,
        )
    return state, payload


def solution(mesh):
    split = ("pairs", "orb")
    return jax.shard_map(
        body,
        mesh=mesh,
        in_specs=(
            P(split, None, None),
            P(split, None, None),
            P(split, None),
            P(split, None, None, None),
            P(split, None),
            P(split, None),
            P(split, None),
            P(),
            P(),
        ),
        out_specs=(P(split, None, None), P(split, None, None)),
        check_vma=False,
    )
```

```python
import functools

import jax
import jax.numpy as jnp
from jax import lax
from jax.experimental import pallas as pl
from jax.experimental.pallas import tpu as pltpu
from jax.sharding import PartitionSpec as P

PAIRS_ORB = 32
ITERS = 2
ROWS = 16
PARTS = 3
EARLY = 20_000_000_000
CLOSE = 1_000_000_000

F32 = jnp.float32
BF16 = jnp.bfloat16
VMEM = pl.BlockSpec(memory_space=pltpu.VMEM)
SMEM = pl.BlockSpec(memory_space=pltpu.SMEM)
ANY = pl.BlockSpec(memory_space=pl.ANY)
HBM = pl.BlockSpec(memory_space=pltpu.HBM)
LIMIT = 16 * 1024 * 1024
SMALL = 8 * 1024 * 1024
WHOLE = 60 * 1024 * 1024


def eye_mask(width):
    rows = lax.broadcasted_iota(jnp.int32, (width, width), 0)
    cols = lax.broadcasted_iota(jnp.int32, (width, width), 1)
    return rows == cols


def to_row(column, eye):
    return jnp.sum(jnp.where(eye, column, 0.0), axis=0, keepdims=True)


def to_column(row, eye):
    return jnp.sum(jnp.where(eye, row, 0.0), axis=1, keepdims=True)


def split_parts(value):
    parts = []
    for _ in range(PARTS):
        part = value.astype(BF16)
        parts.append(part)
        value = value - part.astype(F32)
    return parts


def tail_rows(value, rows):
    parts = split_parts(value)
    missing = rows - sum(part.shape[0] for part in parts)
    if missing:
        parts.append(jnp.zeros((missing, value.shape[1]), BF16))
    return jnp.concatenate([part.astype(F32) for part in parts], axis=0).astype(BF16)


def join_parts(rows, orbitals):
    rows = rows.astype(F32)
    value = rows[:orbitals]
    for part in range(1, PARTS):
        value = value + rows[part * orbitals : (part + 1) * orbitals]
    return value


def singles_terms(state, projector_row, count, eye):
    projected = to_row(jnp.sum(state * projector_row, axis=1, keepdims=True), eye)
    return count * projected


def end_counts(orbitals, per_device, end):
    ids = lax.broadcasted_iota(jnp.int32, (orbitals, 1), 0)
    return [(ids == end(s)).astype(F32) for s in range(per_device)]


def fetch(pairs, sems):
    copies = [pltpu.make_async_copy(src, dst, sems.at[i]) for i, (src, dst) in enumerate(pairs)]
    for copy in copies:
        copy.start()
    return copies


def setup_kernel(
    capacity, orbitals, near, mirrors, direct,
    ends_hbm, state_hbm, projector_hbm, coupled_hbm, slot_hbm, couplings_hbm,
    payload, index, table, coefficients,
    ends, state, projector, coupled, slot, couplings, sems,
):
    copies = fetch(
        (
            (coupled_hbm, coupled), (slot_hbm, slot), (projector_hbm, projector), (state_hbm, state),
            (couplings_hbm, couplings), (ends_hbm, ends),
        ),
        sems,
    )
    per_device, width = state.shape[0], state.shape[1]
    count = slot.shape[1]
    pair_count, orb_count = lax.axis_size("pairs"), lax.axis_size("orb")
    pair_idx, orb_idx = lax.axis_index("pairs"), lax.axis_index("orb")
    group = orb_count * per_device
    lanes_out = index.shape[1]
    copies[0].wait()
    copies[1].wait()
    slots = slot[...]
    wanted = coupled[...]
    lanes = lax.broadcasted_iota(jnp.int32, (1, count), 1)
    members = lax.broadcasted_iota(jnp.int32, (group, 1), 0)
    slot_ids = lax.broadcasted_iota(jnp.int32, (count, lanes_out), 0)
    column = lax.broadcasted_iota(jnp.int32, (count, lanes_out), 1)
    dest = column ^ pair_idx if direct else column
    owner = (slot_ids // per_device == dest * orb_count + orb_idx) & (column < pair_count)
    for m, flip in enumerate(mirrors):
        base = (pair_idx ^ flip) * group
        pairs = jnp.sum(jnp.where(slots == base + members, lanes, 0), axis=1, keepdims=True)
        hits = jnp.zeros((group, count), F32)
        for g in range(group):
            hit = jnp.max((wanted == pairs[g : g + 1, :]).astype(F32), axis=0, keepdims=True)
            hits = jnp.where(members == g, hit, hits)
        needed = jnp.dot(hits, owner.astype(F32), preferred_element_type=F32) > 0.5
        run = jnp.zeros((1, lanes_out), jnp.int32)
        picked = [jnp.zeros((1, lanes_out), jnp.int32) for _ in range(capacity)]
        for g in range(group):
            hit = needed[g : g + 1, :].astype(jnp.int32)
            for c in range(capacity):
                picked[c] = picked[c] + jnp.where((hit == 1) & (run == c), g, 0)
            run = run + hit
        for c, row in enumerate(picked):
            index[pl.ds(m * capacity + c, 1), :] = row

    eye = eye_mask(count)
    slots_c = jnp.sum(jnp.where(eye, slots, 0), axis=1, keepdims=True)
    first = (pair_idx * orb_count + orb_idx) * per_device
    entries = []
    mine = jnp.zeros((1, count), F32)
    for i in range(per_device):
        own = jnp.sum(jnp.where(lanes == first + i, wanted, 0), axis=1, keepdims=True)
        entries.append((own == lanes).astype(F32))
        mine = jnp.maximum(mine, jnp.max(entries[i], axis=0, keepdims=True))
    mine_c = to_column(mine, eye)
    before = (slots_c // group == slots // group) & (slots_c < slots)
    rank = jnp.sum(jnp.where(before, mine_c, 0.0), axis=0, keepdims=True).astype(jnp.int32)
    source = slots // group
    flip = source ^ pair_idx
    place = jnp.where(flip < near, source ^ (pair_idx & ~(near - 1)), flip) * capacity + rank
    place = place.astype(F32)
    neighbours = coupled.shape[0]
    ids = lax.broadcasted_iota(jnp.int32, (neighbours, 1), 0)
    square = eye_mask(neighbours)
    column = lax.broadcasted_iota(jnp.int32, (neighbours, lanes_out), 1)
    copies[4].wait()
    for i in range(per_device):
        found = jnp.sum(entries[i] * place, axis=1, keepdims=True).astype(jnp.int32)
        match = found == column
        table[pl.ds(i, 1), :] = jnp.sum(jnp.where(match, ids, 0), axis=0, keepdims=True)
        value = to_column(couplings[pl.ds(i, 1), :], square)
        coefficients[pl.ds(i, 1), :] = jnp.sum(jnp.where(match, value, 0.0), axis=0, keepdims=True)

    eye = eye_mask(width)
    copies[2].wait()
    copies[3].wait()
    copies[5].wait()
    total = jnp.zeros((orbitals, width), F32)
    counts_a = end_counts(orbitals, per_device, lambda s: ends[0, s])
    counts_b = end_counts(orbitals, per_device, lambda s: ends[1, s])
    for s in range(per_device):
        block = state[s]
        payload[pl.ds(s * width, width), :] = block.astype(BF16)
        total += singles_terms(block, projector[pl.ds(s, 1), :], counts_a[s] + counts_b[s], eye)
    tail = payload.shape[0] - per_device * width
    payload[pl.ds(per_device * width, tail), :] = tail_rows(total, tail)


def select_kernel(capacity, per_device, orbitals, width, lanes, row, swap, index, gathered, outs):
    blocks = per_device * width
    tail = gathered.shape[1] - blocks
    total = join_parts(gathered[0, pl.ds(blocks, tail), :], orbitals)
    for d in range(1, gathered.shape[0]):
        total += join_parts(gathered[d, pl.ds(blocks, tail), :], orbitals)
    rows = tail_rows(total, tail)
    for lane, out in zip(lanes, outs):
        for c in range(capacity):
            j = index[row + c, lane]
            first = pl.multiple_of((j % per_device) * width, ROWS)
            out[pl.ds(c * width, width), :] = gathered[(j // per_device) ^ swap, pl.ds(first, width), :]
        out[pl.ds(capacity * width, tail), :] = rows


def add_blocks(capacity, orbitals, index, coefficients, intersections, blocks, coupling, singles):
    per_device, width = intersections.shape[0], intersections.shape[2]
    slots = [(place * capacity + c, ref, c * width) for place, ref in blocks for c in range(capacity)]
    wide = [[] for _ in range(per_device)]
    scaled = [[] for _ in range(per_device)]
    empty = jnp.zeros((width, width), BF16)
    for p in range(0, len(slots), 2):
        part = slots[p : p + 2]
        mixing = [
            jnp.concatenate([intersections[s, index[s, lane]] for lane, _, _ in part], axis=1)
            for s in range(per_device)
        ]
        near = [ref[pl.ds(row, width), :] for _, ref, row in part]
        if len(part) == 2:
            near = jnp.concatenate(
                [jnp.concatenate([near[0], empty], axis=1), jnp.concatenate([empty, near[1]], axis=1)], axis=0
            )
        else:
            near = near[0]
        lifted = jnp.dot(jnp.concatenate(mixing, axis=0), near, preferred_element_type=F32)
        for s in range(per_device):
            wide[s].append(mixing[s])
            for i, (lane, _, _) in enumerate(part):
                block = lifted[s * width : (s + 1) * width, i * width : (i + 1) * width]
                scaled[s].append((coefficients[s, lane] * block).astype(BF16))
    for s in range(per_device):
        if slots:
            coupling[s] = coupling[s] + lax.dot_general(
                jnp.concatenate(scaled[s], axis=1), jnp.concatenate(wide[s], axis=1),
                (((1,), (1,)), ((), ())), preferred_element_type=F32,
            )
    for _, ref in blocks:
        tail = ref.shape[0] - capacity * width
        singles = singles + join_parts(ref[pl.ds(capacity * width, tail), :], orbitals)
    return singles


def gather_terms(capacity, orbitals, index, coefficients, intersections, every, places, blocks, before):
    per_device, width = intersections.shape[0], intersections.shape[2]
    coupling = [jnp.zeros((width, width), F32) for _ in range(per_device)]
    singles = jnp.zeros((orbitals, width), F32)
    if before is not None:
        coupling = [before[pl.ds(s * width, width), :] for s in range(per_device)]
        singles = before[pl.ds(per_device * width, orbitals), :]
    operands = (capacity, orbitals, index, coefficients, intersections)
    if every is not None:
        unit = min(every.shape[0], 4)

        def step(i, carry):
            parts = list(carry[:-1])
            some = [(i * unit + u, every.at[i * unit + u]) for u in range(unit)]
            total = add_blocks(*operands, some, parts, carry[-1])
            return (*parts, total)

        *coupling, singles = lax.fori_loop(0, every.shape[0] // unit, step, (*coupling, singles))
    singles = add_blocks(*operands, list(zip(places, blocks)), coupling, singles)
    return coupling, singles


def terms_kernel(
    capacity, orbitals, has_before, has_every, places, index, coefficients, intersections, *refs
):
    out = refs[-1]
    refs = list(refs[:-1])
    before = refs.pop(0) if has_before else None
    every = refs.pop(0) if has_every else None
    coupling, singles = gather_terms(
        capacity, orbitals, index, coefficients, intersections, every, places, refs, before
    )
    width = intersections.shape[2]
    for s, part in enumerate(coupling):
        out[pl.ds(s * width, width), :] = part
    out[pl.ds(len(coupling) * width, orbitals), :] = singles


def update_kernel(
    last, capacity, orbitals, places,
    index, coefficients, ends, intersections, before, *refs,
):
    blocks = refs[: len(places)]
    state, integrals, energies, projector, out_a, out_b = refs[len(places) :]
    per_device, width = state.shape[0], state.shape[1]
    coupling, singles = gather_terms(
        capacity, orbitals, index, coefficients, intersections, None, places, blocks, before
    )
    eye = eye_mask(width)
    total = jnp.zeros((orbitals, width), F32)
    counts_a = end_counts(orbitals, per_device, lambda s: ends[0, s])
    counts_b = end_counts(orbitals, per_device, lambda s: ends[1, s])
    for s in range(per_device):
        old = state[s]
        energy = energies[pl.ds(s, 1), :]
        energy_c = to_column(energy, eye)
        proj = projector[pl.ds(s, 1), :]
        proj_c = to_column(proj, eye)
        left = jnp.sum(counts_a[s] * singles, axis=0, keepdims=True)
        right = jnp.sum(counts_b[s] * singles, axis=0, keepdims=True)
        residual = (
            integrals[s].astype(F32) + energy_c * old + old * energy - coupling[s]
            + to_column(left, eye) * proj + proj_c * right
        )
        new = old - residual / (energy_c + energy)
        out_a[s] = new
        if last:
            out_b[s] = residual
        else:
            out_b[pl.ds(s * width, width), :] = new.astype(BF16)
            total += singles_terms(new, proj, counts_a[s] + counts_b[s], eye)
    if not last:
        tail = out_b.shape[0] - per_device * width
        out_b[pl.ds(per_device * width, tail), :] = tail_rows(total, tail)


def tail_size(orbitals):
    return -(-PARTS * orbitals // ROWS) * ROWS


def cost(flops):
    return pl.CostEstimate(flops=flops, bytes_accessed=0, transcendentals=0)


def body(
    amplitudes, integrals, energies, intersections, couplings, projector, pair_orbitals, coupled, pair_slot,
):
    pair_count = lax.axis_size("pairs")
    per_device, width = amplitudes.shape[0], amplitudes.shape[1]
    total, neighbours = coupled.shape
    capacity = 1 + neighbours // pair_count
    orbitals = total // PAIRS_ORB
    tail = tail_size(orbitals)
    stride = capacity * width + tail
    orb_count = lax.axis_size("orb")
    direct = pair_count in (4, 8) and orb_count == 4
    tables = VMEM if direct else SMEM
    half = pair_count // 2
    mirrors = [0, half] if direct else [0]
    near = 1 if direct else pair_count
    lanes = -(-pair_count * capacity // 128) * 128
    ends = pair_orbitals.T
    small = pltpu.CompilerParams(vmem_limit_bytes=SMALL)
    params = pltpu.CompilerParams(vmem_limit_bytes=LIMIT)
    block_shape = jax.ShapeDtypeStruct((stride, width), BF16)
    terms_shape = jax.ShapeDtypeStruct((per_device * width + -(-orbitals // 8) * 8, width), F32)
    payload_shape = jax.ShapeDtypeStruct((per_device * width + tail, width), BF16)
    payload, send_index, index, coefficients = pl.pallas_call(
        functools.partial(setup_kernel, capacity, orbitals, near, mirrors, direct),
        out_shape=(
            payload_shape,
            jax.ShapeDtypeStruct((-(-len(mirrors) * capacity // 8) * 8, lanes), jnp.int32),
            jax.ShapeDtypeStruct((per_device, lanes), jnp.int32),
            jax.ShapeDtypeStruct((per_device, lanes), F32),
        ),
        in_specs=[HBM] * 6,
        out_specs=[VMEM] * 4,
        scratch_shapes=[
            pltpu.VMEM(ends.shape, jnp.int32),
            pltpu.VMEM(amplitudes.shape, F32),
            pltpu.VMEM(projector.shape, F32),
            pltpu.VMEM((neighbours, total), jnp.int32),
            pltpu.VMEM((1, total), jnp.int32),
            pltpu.VMEM(couplings.shape, F32),
            pltpu.SemaphoreType.DMA((6,)),
        ],
        compiler_params=pltpu.CompilerParams(vmem_limit_bytes=WHOLE),
        name="setup",
    )(ends, amplitudes, projector, coupled.T, pair_slot.reshape(1, total), couplings)

    def join(*parts, after=()):
        def kernel(*refs):
            if len(parts) == 1:
                refs[-1][...] = refs[0][...]
            else:
                for i in range(len(parts)):
                    refs[-1][i] = refs[i][...]

        shape = payload_shape.shape if len(parts) == 1 else (len(parts), *payload_shape.shape)
        return pl.pallas_call(
            kernel,
            out_shape=jax.ShapeDtypeStruct(shape, BF16),
            in_specs=[VMEM] * len(parts) + [ANY] * len(after),
            out_specs=VMEM,
            compiler_params=small,
            cost_estimate=cost(0),
            name="join",
        )(*parts, *after)

    def select(row, flips, gathered):
        def kernel(index, source, *refs):
            outs, held = refs[: len(flips)], refs[-1]
            for c in range(2):
                for x in range(2):
                    held[2 * x + c] = source[c, x]
            swap = lax.axis_index("orb") // 2 * 2
            select_kernel(capacity, per_device, orbitals, width, flips, row, swap, index, held, outs)

        return pl.pallas_call(
            kernel,
            out_shape=[block_shape] * len(flips),
            in_specs=[VMEM, VMEM],
            out_specs=[VMEM] * len(flips),
            scratch_shapes=[pltpu.VMEM((4, *payload_shape.shape), BF16)],
            compiler_params=small,
            cost_estimate=cost(0),
            name="select",
        )(send_index, gathered)

    def select_all(gathered):
        def kernel(index, source, out):
            outs = [out.at[i] for i in range(pair_count)]
            select_kernel(capacity, per_device, orbitals, width, range(pair_count), 0, 0, index, source, outs)

        return pl.pallas_call(
            kernel,
            out_shape=jax.ShapeDtypeStruct((pair_count, stride, width), BF16),
            in_specs=[VMEM, VMEM],
            out_specs=VMEM,
            compiler_params=small,
            name="select",
        )(send_index, gathered)

    def exchange(block, axis, flip):
        return lax.ppermute(block, axis, [(p, p ^ flip) for p in range(pair_count * orb_count if isinstance(axis, tuple) else lax.axis_size(axis))])

    def terms(before, every, places, blocks, flops):
        extra = [x for x in (before, every) if x is not None]
        return pl.pallas_call(
            functools.partial(
                terms_kernel, capacity, orbitals, before is not None, every is not None, places
            ),
            out_shape=terms_shape,
            in_specs=[tables, tables] + [VMEM] * (1 + len(extra) + len(blocks)),
            out_specs=VMEM,
            cost_estimate=cost(flops),
            compiler_params=params,
            name="terms",
        )(index, coefficients, intersections, *extra, *blocks)

    state = amplitudes
    for step in range(ITERS):
        last = step == ITERS - 1
        partial, places, late = None, [], []
        if direct:
            mirror = exchange(payload, "pairs", half)
            flips = [0, *range(half - 1, 0, -1)]
            cores = [[o, o + 1] for o in range(0, orb_count, 2)]
            held = join(payload, exchange(payload, "orb", 2))
            held = lax.all_gather(held, "orb", axis=0, axis_index_groups=cores)
            sent = select(0, flips, held)
            arrived = [sent[0]] + [exchange(part, "pairs", flip) for flip, part in zip(flips[1:], sent[1:])]
            mirror = join(mirror, after=[held])
            held = join(mirror, exchange(mirror, "orb", 2), after=arrived[:1])
            held = lax.all_gather(held, "orb", axis=0, axis_index_groups=cores)
            sent = select(capacity, flips, held)
            partial = terms(None, None, flips + [half], arrived + [sent[0]], EARLY)
            places = [half + flip for flip in flips[1:]]
            late = [exchange(part, "pairs", flip) for flip, part in zip(flips[1:], sent[1:])]
        else:
            gathered = lax.all_gather(payload, "orb", axis=0, tiled=False)
            outgoing = select_all(gathered)
            every = lax.all_to_all(outgoing, "pairs", split_axis=0, concat_axis=0, tiled=True)
            partial = terms(None, every, [], [], CLOSE)
        second = jax.ShapeDtypeStruct(amplitudes.shape, F32) if last else payload_shape
        state, payload = pl.pallas_call(
            functools.partial(update_kernel, last, capacity, orbitals, places),
            out_shape=(jax.ShapeDtypeStruct(amplitudes.shape, F32), second),
            in_specs=[VMEM] * (9 + len(late)),
            out_specs=(VMEM, VMEM),
            compiler_params=params,
            name="update",
        )(
            index, coefficients, ends, intersections, partial, *late, state, integrals, energies, projector,
        )
    return state, payload


def solution(mesh):
    split = ("pairs", "orb")
    return jax.shard_map(
        body,
        mesh=mesh,
        in_specs=(
            P(split, None, None),
            P(split, None, None),
            P(split, None),
            P(split, None, None, None),
            P(split, None),
            P(split, None),
            P(split, None),
            P(),
            P(),
        ),
        out_specs=(P(split, None, None), P(split, None, None)),
        check_vma=False,
    )
```

```python
import functools

import jax
import jax.numpy as jnp
from jax import lax
from jax.experimental import pallas as pl
from jax.experimental.pallas import tpu as pltpu
from jax.sharding import PartitionSpec as P

PAIRS_ORB = 32
ITERS = 2
ROWS = 16
PARTS = 3
EARLY = 20_000_000_000
CLOSE = 1_000_000_000

F32 = jnp.float32
BF16 = jnp.bfloat16
VMEM = pl.BlockSpec(memory_space=pltpu.VMEM)
SMEM = pl.BlockSpec(memory_space=pltpu.SMEM)
ANY = pl.BlockSpec(memory_space=pl.ANY)
HBM = pl.BlockSpec(memory_space=pltpu.HBM)
LIMIT = 16 * 1024 * 1024
SMALL = 8 * 1024 * 1024
WHOLE = 60 * 1024 * 1024


def eye_mask(width):
    rows = lax.broadcasted_iota(jnp.int32, (width, width), 0)
    cols = lax.broadcasted_iota(jnp.int32, (width, width), 1)
    return rows == cols


def to_row(column, eye):
    return jnp.sum(jnp.where(eye, column, 0.0), axis=0, keepdims=True)


def to_column(row, eye):
    return jnp.sum(jnp.where(eye, row, 0.0), axis=1, keepdims=True)


def split_parts(value):
    parts = []
    for _ in range(PARTS):
        part = value.astype(BF16)
        parts.append(part)
        value = value - part.astype(F32)
    return parts


def tail_rows(value, rows):
    parts = split_parts(value)
    missing = rows - sum(part.shape[0] for part in parts)
    if missing:
        parts.append(jnp.zeros((missing, value.shape[1]), BF16))
    return jnp.concatenate([part.astype(F32) for part in parts], axis=0).astype(BF16)


def join_parts(rows, orbitals):
    rows = rows.astype(F32)
    value = rows[:orbitals]
    for part in range(1, PARTS):
        value = value + rows[part * orbitals : (part + 1) * orbitals]
    return value


def singles_terms(state, projector_row, count, eye):
    projected = to_row(jnp.sum(state * projector_row, axis=1, keepdims=True), eye)
    return count * projected


def end_counts(orbitals, per_device, end):
    ids = lax.broadcasted_iota(jnp.int32, (orbitals, 1), 0)
    return [(ids == end(s)).astype(F32) for s in range(per_device)]


def fetch(pairs, sems):
    copies = [pltpu.make_async_copy(src, dst, sems.at[i]) for i, (src, dst) in enumerate(pairs)]
    for copy in copies:
        copy.start()
    return copies


def setup_kernel(
    capacity, orbitals, near, mirrors, direct,
    ends_hbm, state_hbm, projector_hbm, coupled_hbm, slot_hbm, couplings_hbm,
    payload, index, table, coefficients,
    ends, state, projector, coupled, slot, couplings, sems,
):
    copies = fetch(
        (
            (coupled_hbm, coupled), (slot_hbm, slot), (projector_hbm, projector), (state_hbm, state),
            (couplings_hbm, couplings), (ends_hbm, ends),
        ),
        sems,
    )
    per_device, width = state.shape[0], state.shape[1]
    count = slot.shape[1]
    pair_count, orb_count = lax.axis_size("pairs"), lax.axis_size("orb")
    pair_idx, orb_idx = lax.axis_index("pairs"), lax.axis_index("orb")
    group = orb_count * per_device
    lanes_out = index.shape[1]
    copies[0].wait()
    copies[1].wait()
    slots = slot[...]
    wanted = coupled[...]
    lanes = lax.broadcasted_iota(jnp.int32, (1, count), 1)
    members = lax.broadcasted_iota(jnp.int32, (group, 1), 0)
    slot_ids = lax.broadcasted_iota(jnp.int32, (count, lanes_out), 0)
    column = lax.broadcasted_iota(jnp.int32, (count, lanes_out), 1)
    dest = column ^ pair_idx if direct else column
    owner = (slot_ids // per_device == dest * orb_count + orb_idx) & (column < pair_count)
    for m, flip in enumerate(mirrors):
        base = (pair_idx ^ flip) * group
        pairs = jnp.sum(jnp.where(slots == base + members, lanes, 0), axis=1, keepdims=True)
        hits = jnp.zeros((group, count), F32)
        for g in range(group):
            hit = jnp.max((wanted == pairs[g : g + 1, :]).astype(F32), axis=0, keepdims=True)
            hits = jnp.where(members == g, hit, hits)
        needed = jnp.dot(hits, owner.astype(F32), preferred_element_type=F32) > 0.5
        run = jnp.zeros((1, lanes_out), jnp.int32)
        picked = [jnp.zeros((1, lanes_out), jnp.int32) for _ in range(capacity)]
        for g in range(group):
            hit = needed[g : g + 1, :].astype(jnp.int32)
            for c in range(capacity):
                picked[c] = picked[c] + jnp.where((hit == 1) & (run == c), g, 0)
            run = run + hit
        for c, row in enumerate(picked):
            index[pl.ds(m * capacity + c, 1), :] = row

    eye = eye_mask(count)
    slots_c = jnp.sum(jnp.where(eye, slots, 0), axis=1, keepdims=True)
    first = (pair_idx * orb_count + orb_idx) * per_device
    entries = []
    mine = jnp.zeros((1, count), F32)
    for i in range(per_device):
        own = jnp.sum(jnp.where(lanes == first + i, wanted, 0), axis=1, keepdims=True)
        entries.append((own == lanes).astype(F32))
        mine = jnp.maximum(mine, jnp.max(entries[i], axis=0, keepdims=True))
    mine_c = to_column(mine, eye)
    before = (slots_c // group == slots // group) & (slots_c < slots)
    rank = jnp.sum(jnp.where(before, mine_c, 0.0), axis=0, keepdims=True).astype(jnp.int32)
    source = slots // group
    flip = source ^ pair_idx
    place = jnp.where(flip < near, source ^ (pair_idx & ~(near - 1)), flip) * capacity + rank
    place = place.astype(F32)
    neighbours = coupled.shape[0]
    ids = lax.broadcasted_iota(jnp.int32, (neighbours, 1), 0)
    square = eye_mask(neighbours)
    column = lax.broadcasted_iota(jnp.int32, (neighbours, lanes_out), 1)
    copies[4].wait()
    for i in range(per_device):
        found = jnp.sum(entries[i] * place, axis=1, keepdims=True).astype(jnp.int32)
        match = found == column
        table[pl.ds(i, 1), :] = jnp.sum(jnp.where(match, ids, 0), axis=0, keepdims=True)
        value = to_column(couplings[pl.ds(i, 1), :], square)
        coefficients[pl.ds(i, 1), :] = jnp.sum(jnp.where(match, value, 0.0), axis=0, keepdims=True)

    eye = eye_mask(width)
    copies[2].wait()
    copies[3].wait()
    copies[5].wait()
    total = jnp.zeros((orbitals, width), F32)
    counts_a = end_counts(orbitals, per_device, lambda s: ends[0, s])
    counts_b = end_counts(orbitals, per_device, lambda s: ends[1, s])
    for s in range(per_device):
        block = state[s]
        payload[pl.ds(s * width, width), :] = block.astype(BF16)
        total += singles_terms(block, projector[pl.ds(s, 1), :], counts_a[s] + counts_b[s], eye)
    tail = payload.shape[0] - per_device * width
    payload[pl.ds(per_device * width, tail), :] = tail_rows(total, tail)


def select_kernel(capacity, per_device, orbitals, width, lanes, row, swap, index, gathered, outs):
    blocks = per_device * width
    tail = gathered.shape[1] - blocks
    total = join_parts(gathered[0, pl.ds(blocks, tail), :], orbitals)
    for d in range(1, gathered.shape[0]):
        total += join_parts(gathered[d, pl.ds(blocks, tail), :], orbitals)
    rows = tail_rows(total, tail)
    for lane, out in zip(lanes, outs):
        for c in range(capacity):
            j = index[row + c, lane]
            first = pl.multiple_of((j % per_device) * width, ROWS)
            out[pl.ds(c * width, width), :] = gathered[(j // per_device) ^ swap, pl.ds(first, width), :]
        out[pl.ds(capacity * width, tail), :] = rows


def add_blocks(capacity, orbitals, index, coefficients, intersections, blocks, coupling, singles):
    per_device, width = intersections.shape[0], intersections.shape[2]
    slots = [(place * capacity + c, ref, c * width) for place, ref in blocks for c in range(capacity)]
    wide = [[] for _ in range(per_device)]
    scaled = [[] for _ in range(per_device)]
    empty = jnp.zeros((width, width), BF16)
    for p in range(0, len(slots), 2):
        part = slots[p : p + 2]
        mixing = [
            jnp.concatenate([intersections[s, index[s, lane]] for lane, _, _ in part], axis=1)
            for s in range(per_device)
        ]
        near = [ref[pl.ds(row, width), :] for _, ref, row in part]
        if len(part) == 2:
            near = jnp.concatenate(
                [jnp.concatenate([near[0], empty], axis=1), jnp.concatenate([empty, near[1]], axis=1)], axis=0
            )
        else:
            near = near[0]
        lifted = jnp.dot(jnp.concatenate(mixing, axis=0), near, preferred_element_type=F32)
        for s in range(per_device):
            wide[s].append(mixing[s])
            for i, (lane, _, _) in enumerate(part):
                block = lifted[s * width : (s + 1) * width, i * width : (i + 1) * width]
                scaled[s].append((coefficients[s, lane] * block).astype(BF16))
    for s in range(per_device):
        if slots:
            coupling[s] = coupling[s] + lax.dot_general(
                jnp.concatenate(scaled[s], axis=1), jnp.concatenate(wide[s], axis=1),
                (((1,), (1,)), ((), ())), preferred_element_type=F32,
            )
    for _, ref in blocks:
        tail = ref.shape[0] - capacity * width
        singles = singles + join_parts(ref[pl.ds(capacity * width, tail), :], orbitals)
    return singles


def gather_terms(capacity, orbitals, index, coefficients, intersections, every, places, blocks, before):
    per_device, width = intersections.shape[0], intersections.shape[2]
    coupling = [jnp.zeros((width, width), F32) for _ in range(per_device)]
    singles = jnp.zeros((orbitals, width), F32)
    if before is not None:
        coupling = [before[pl.ds(s * width, width), :] for s in range(per_device)]
        singles = before[pl.ds(per_device * width, orbitals), :]
    operands = (capacity, orbitals, index, coefficients, intersections)
    if every is not None:
        unit = min(every.shape[0], 4)

        def step(i, carry):
            parts = list(carry[:-1])
            some = [(i * unit + u, every.at[i * unit + u]) for u in range(unit)]
            total = add_blocks(*operands, some, parts, carry[-1])
            return (*parts, total)

        *coupling, singles = lax.fori_loop(0, every.shape[0] // unit, step, (*coupling, singles))
    singles = add_blocks(*operands, list(zip(places, blocks)), coupling, singles)
    return coupling, singles


def terms_kernel(
    capacity, orbitals, has_before, has_every, places, index, coefficients, intersections, *refs
):
    out = refs[-1]
    refs = list(refs[:-1])
    before = refs.pop(0) if has_before else None
    every = refs.pop(0) if has_every else None
    coupling, singles = gather_terms(
        capacity, orbitals, index, coefficients, intersections, every, places, refs, before
    )
    width = intersections.shape[2]
    for s, part in enumerate(coupling):
        out[pl.ds(s * width, width), :] = part
    out[pl.ds(len(coupling) * width, orbitals), :] = singles


def update_kernel(
    last, capacity, orbitals, places,
    index, coefficients, ends, intersections, before, *refs,
):
    blocks = refs[: len(places)]
    state, integrals, energies, projector, out_a, out_b = refs[len(places) : len(places) + 6]
    final = out_a, out_b
    if last:
        out_a, out_b, sems = refs[-3:]
    copies = []
    per_device, width = state.shape[0], state.shape[1]
    coupling, singles = gather_terms(
        capacity, orbitals, index, coefficients, intersections, None, places, blocks, before
    )
    eye = eye_mask(width)
    total = jnp.zeros((orbitals, width), F32)
    counts_a = end_counts(orbitals, per_device, lambda s: ends[0, s])
    counts_b = end_counts(orbitals, per_device, lambda s: ends[1, s])
    for s in range(per_device):
        old = state[s]
        energy = energies[pl.ds(s, 1), :]
        energy_c = to_column(energy, eye)
        proj = projector[pl.ds(s, 1), :]
        proj_c = to_column(proj, eye)
        left = jnp.sum(counts_a[s] * singles, axis=0, keepdims=True)
        right = jnp.sum(counts_b[s] * singles, axis=0, keepdims=True)
        residual = (
            integrals[s].astype(F32) + energy_c * old + old * energy - coupling[s]
            + to_column(left, eye) * proj + proj_c * right
        )
        new = old - residual / (energy_c + energy)
        out_a[s] = new
        if last:
            out_b[s] = residual
            for i in range(2):
                copies.append(pltpu.make_async_copy((out_a, out_b)[i].at[s], final[i].at[s], sems.at[i, s]))
                copies[-1].start()
        else:
            out_b[pl.ds(s * width, width), :] = new.astype(BF16)
            total += singles_terms(new, proj, counts_a[s] + counts_b[s], eye)
    for copy in copies:
        copy.wait()
    if not last:
        tail = out_b.shape[0] - per_device * width
        out_b[pl.ds(per_device * width, tail), :] = tail_rows(total, tail)


def tail_size(orbitals):
    return -(-PARTS * orbitals // ROWS) * ROWS


def cost(flops):
    return pl.CostEstimate(flops=flops, bytes_accessed=0, transcendentals=0)


def body(
    amplitudes, integrals, energies, intersections, couplings, projector, pair_orbitals, coupled, pair_slot,
):
    pair_count = lax.axis_size("pairs")
    per_device, width = amplitudes.shape[0], amplitudes.shape[1]
    total, neighbours = coupled.shape
    capacity = 1 + neighbours // pair_count
    orbitals = total // PAIRS_ORB
    tail = tail_size(orbitals)
    stride = capacity * width + tail
    orb_count = lax.axis_size("orb")
    direct = pair_count in (4, 8) and orb_count == 4
    tables = VMEM if direct else SMEM
    half = pair_count // 2
    mirrors = [0, half] if direct else [0]
    near = 1 if direct else pair_count
    lanes = -(-pair_count * capacity // 128) * 128
    ends = pair_orbitals.T
    small = pltpu.CompilerParams(vmem_limit_bytes=SMALL)
    params = pltpu.CompilerParams(vmem_limit_bytes=LIMIT)
    block_shape = jax.ShapeDtypeStruct((stride, width), BF16)
    terms_shape = jax.ShapeDtypeStruct((per_device * width + -(-orbitals // 8) * 8, width), F32)
    payload_shape = jax.ShapeDtypeStruct((per_device * width + tail, width), BF16)
    payload, send_index, index, coefficients = pl.pallas_call(
        functools.partial(setup_kernel, capacity, orbitals, near, mirrors, direct),
        out_shape=(
            payload_shape,
            jax.ShapeDtypeStruct((-(-len(mirrors) * capacity // 8) * 8, lanes), jnp.int32),
            jax.ShapeDtypeStruct((per_device, lanes), jnp.int32),
            jax.ShapeDtypeStruct((per_device, lanes), F32),
        ),
        in_specs=[HBM] * 6,
        out_specs=[VMEM] * 4,
        scratch_shapes=[
            pltpu.VMEM(ends.shape, jnp.int32),
            pltpu.VMEM(amplitudes.shape, F32),
            pltpu.VMEM(projector.shape, F32),
            pltpu.VMEM((neighbours, total), jnp.int32),
            pltpu.VMEM((1, total), jnp.int32),
            pltpu.VMEM(couplings.shape, F32),
            pltpu.SemaphoreType.DMA((6,)),
        ],
        compiler_params=small if direct else pltpu.CompilerParams(vmem_limit_bytes=WHOLE),
        name="setup",
    )(
        *[
            pltpu.with_memory_space_constraint(x, pltpu.HBM)
            for x in (ends, amplitudes, projector, coupled.T, pair_slot.reshape(1, total), couplings)
        ]
    )

    def join(*parts, after=()):
        def kernel(*refs):
            if len(parts) == 1:
                refs[-1][...] = refs[0][...]
            else:
                for i in range(len(parts)):
                    refs[-1][i] = refs[i][...]

        shape = payload_shape.shape if len(parts) == 1 else (len(parts), *payload_shape.shape)
        return pl.pallas_call(
            kernel,
            out_shape=jax.ShapeDtypeStruct(shape, BF16),
            in_specs=[VMEM] * len(parts) + [ANY] * len(after),
            out_specs=VMEM,
            compiler_params=small,
            cost_estimate=cost(0),
            name="join",
        )(*parts, *after)

    def select(row, flips, gathered):
        def kernel(index, source, *refs):
            outs, held = refs[: len(flips)], refs[-1]
            swap = 0
            if row:
                swap = lax.axis_index("orb") // 2 * 2
                for c in range(2):
                    for x in range(2):
                        held[2 * x + c] = source[c, x]
            else:
                held = source
            select_kernel(capacity, per_device, orbitals, width, flips, row, swap, index, held, outs)

        return pl.pallas_call(
            kernel,
            out_shape=[block_shape] * len(flips),
            in_specs=[VMEM, VMEM],
            out_specs=[VMEM] * len(flips),
            scratch_shapes=[pltpu.VMEM((4, *payload_shape.shape), BF16)],
            compiler_params=small,
            cost_estimate=cost(0),
            name="select",
        )(send_index, gathered)

    def select_all(gathered):
        def kernel(index, source, out):
            outs = [out.at[i] for i in range(pair_count)]
            select_kernel(capacity, per_device, orbitals, width, range(pair_count), 0, 0, index, source, outs)

        return pl.pallas_call(
            kernel,
            out_shape=jax.ShapeDtypeStruct((pair_count, stride, width), BF16),
            in_specs=[VMEM, VMEM],
            out_specs=VMEM,
            compiler_params=small,
            name="select",
        )(send_index, gathered)

    def exchange(block, axis, flip):
        return lax.ppermute(block, axis, [(p, p ^ flip) for p in range(pair_count * orb_count if isinstance(axis, tuple) else lax.axis_size(axis))])

    def terms(before, every, places, blocks, flops):
        extra = [x for x in (before, every) if x is not None]
        return pl.pallas_call(
            functools.partial(
                terms_kernel, capacity, orbitals, before is not None, every is not None, places
            ),
            out_shape=terms_shape,
            in_specs=[tables, tables] + [VMEM] * (1 + len(extra) + len(blocks)),
            out_specs=VMEM,
            cost_estimate=cost(flops),
            compiler_params=params,
            name="terms",
        )(index, coefficients, intersections, *extra, *blocks)

    state = amplitudes
    for step in range(ITERS):
        last = step == ITERS - 1
        partial, places, late = None, [], []
        if direct:
            mirror = exchange(payload, "pairs", half)
            flips = [0, *range(half - 1, 0, -1)]
            cores = [[o, o + 1] for o in range(0, orb_count, 2)]
            held = lax.all_gather(payload, "orb", axis=0, tiled=False)
            across = pair_count - 1
            order = [0, across, *flips[1:]]
            sent = select(0, order, held)
            arrived = [sent[0]] + [exchange(part, "pairs", flip) for flip, part in zip(order[1:], sent[1:])]
            mirror = join(mirror, after=sent[:1])
            held = join(mirror, exchange(mirror, "orb", 2), after=arrived[:1])
            held = lax.all_gather(held, "orb", axis=0, axis_index_groups=cores)
            close = [flip for flip in flips if flip + half != across]
            sent = select(capacity, close, held)
            partial = terms(None, None, [*order, half], arrived + [sent[0]], EARLY)
            places = [half + flip for flip in close[1:]]
            late = [exchange(part, "pairs", flip) for flip, part in zip(close[1:], sent[1:])]
        else:
            gathered = lax.all_gather(payload, "orb", axis=0, tiled=False)
            outgoing = select_all(gathered)
            every = lax.all_to_all(outgoing, "pairs", split_axis=0, concat_axis=0, tiled=True)
            partial = terms(None, every, [], [], CLOSE)
        second = jax.ShapeDtypeStruct(amplitudes.shape, F32) if last else payload_shape
        state, payload = pl.pallas_call(
            functools.partial(update_kernel, last, capacity, orbitals, places),
            out_shape=(jax.ShapeDtypeStruct(amplitudes.shape, F32), second),
            in_specs=[VMEM] * (9 + len(late)),
            out_specs=(HBM, HBM) if last else (VMEM, VMEM),
            scratch_shapes=[
                pltpu.VMEM(amplitudes.shape, F32),
                pltpu.VMEM(amplitudes.shape, F32),
                pltpu.SemaphoreType.DMA((2, per_device)),
            ]
            if last
            else [],
            compiler_params=params,
            name="update",
        )(
            index, coefficients, ends, intersections, partial, *late, state, integrals, energies, projector,
        )
    return state, payload


def solution(mesh):
    split = ("pairs", "orb")
    return jax.shard_map(
        body,
        mesh=mesh,
        in_specs=(
            P(split, None, None),
            P(split, None, None),
            P(split, None),
            P(split, None, None, None),
            P(split, None),
            P(split, None),
            P(split, None),
            P(),
            P(),
        ),
        out_specs=(P(split, None, None), P(split, None, None)),
        check_vma=False,
    )
```

```python
import functools

import jax
import jax.numpy as jnp
from jax import lax
from jax.experimental import pallas as pl
from jax.experimental.pallas import tpu as pltpu
from jax.sharding import PartitionSpec as P

PAIRS_ORB = 32
ITERS = 2
ROWS = 16
PARTS = 3
TERMS_COST = 20_000_000_000

F32 = jnp.float32
BF16 = jnp.bfloat16
VMEM = pl.BlockSpec(memory_space=pltpu.VMEM)
SMEM = pl.BlockSpec(memory_space=pltpu.SMEM)
ANY = pl.BlockSpec(memory_space=pl.ANY)
HBM = pl.BlockSpec(memory_space=pltpu.HBM)
LIMIT = 16 * 1024 * 1024
SMALL = 8 * 1024 * 1024
WHOLE = 60 * 1024 * 1024


def eye_mask(width):
    rows = lax.broadcasted_iota(jnp.int32, (width, width), 0)
    cols = lax.broadcasted_iota(jnp.int32, (width, width), 1)
    return rows == cols


def to_row(column, eye):
    return jnp.sum(jnp.where(eye, column, 0.0), axis=0, keepdims=True)


def to_column(row, eye):
    return jnp.sum(jnp.where(eye, row, 0.0), axis=1, keepdims=True)


def split_parts(value):
    parts = []
    for _ in range(PARTS):
        part = value.astype(BF16)
        parts.append(part)
        value = value - part.astype(F32)
    return parts


def tail_rows(value, rows):
    parts = split_parts(value)
    missing = rows - sum(part.shape[0] for part in parts)
    if missing:
        parts.append(jnp.zeros((missing, value.shape[1]), BF16))
    return jnp.concatenate([part.astype(F32) for part in parts], axis=0).astype(BF16)


def join_parts(rows, orbitals):
    rows = rows.astype(F32)
    value = rows[:orbitals]
    for part in range(1, PARTS):
        value = value + rows[part * orbitals : (part + 1) * orbitals]
    return value


def singles_terms(state, projector_row, count, eye):
    projected = to_row(jnp.sum(state * projector_row, axis=1, keepdims=True), eye)
    return count * projected


def end_counts(orbitals, per_device, end):
    ids = lax.broadcasted_iota(jnp.int32, (orbitals, 1), 0)
    return [(ids == end(s)).astype(F32) for s in range(per_device)]


def fetch(pairs, sems):
    copies = [pltpu.make_async_copy(src, dst, sems.at[i]) for i, (src, dst) in enumerate(pairs)]
    for copy in copies:
        copy.start()
    return copies


def setup_kernel(
    capacity, orbitals, near, mirrors, direct,
    ends_hbm, state_hbm, projector_hbm, coupled_hbm, slot_hbm, couplings_hbm,
    payload, index, table, coefficients,
    ends, state, projector, coupled, slot, couplings, sems,
):
    copies = fetch(
        (
            (coupled_hbm, coupled), (slot_hbm, slot), (projector_hbm, projector), (state_hbm, state),
            (couplings_hbm, couplings), (ends_hbm, ends),
        ),
        sems,
    )
    per_device, width = state.shape[0], state.shape[1]
    count = slot.shape[1]
    pair_count, orb_count = lax.axis_size("pairs"), lax.axis_size("orb")
    pair_idx, orb_idx = lax.axis_index("pairs"), lax.axis_index("orb")
    group = orb_count * per_device
    lanes_out = index.shape[1]
    copies[0].wait()
    copies[1].wait()
    slots = slot[...]
    wanted = coupled[...]
    lanes = lax.broadcasted_iota(jnp.int32, (1, count), 1)
    members = lax.broadcasted_iota(jnp.int32, (group, 1), 0)
    slot_ids = lax.broadcasted_iota(jnp.int32, (count, lanes_out), 0)
    column = lax.broadcasted_iota(jnp.int32, (count, lanes_out), 1)
    dest = column ^ pair_idx if direct else column
    owner = (slot_ids // per_device == dest * orb_count + orb_idx) & (column < pair_count)
    for m, flip in enumerate(mirrors):
        base = (pair_idx ^ flip) * group
        pairs = jnp.sum(jnp.where(slots == base + members, lanes, 0), axis=1, keepdims=True)
        hits = jnp.zeros((group, count), F32)
        for g in range(group):
            hit = jnp.max((wanted == pairs[g : g + 1, :]).astype(F32), axis=0, keepdims=True)
            hits = jnp.where(members == g, hit, hits)
        needed = jnp.dot(hits, owner.astype(F32), preferred_element_type=F32) > 0.5
        run = jnp.zeros((1, lanes_out), jnp.int32)
        picked = [jnp.zeros((1, lanes_out), jnp.int32) for _ in range(capacity)]
        for g in range(group):
            hit = needed[g : g + 1, :].astype(jnp.int32)
            for c in range(capacity):
                picked[c] = picked[c] + jnp.where((hit == 1) & (run == c), g, 0)
            run = run + hit
        for c, row in enumerate(picked):
            index[pl.ds(m * capacity + c, 1), :] = row

    eye = eye_mask(count)
    slots_c = jnp.sum(jnp.where(eye, slots, 0), axis=1, keepdims=True)
    first = (pair_idx * orb_count + orb_idx) * per_device
    entries = []
    mine = jnp.zeros((1, count), F32)
    for i in range(per_device):
        own = jnp.sum(jnp.where(lanes == first + i, wanted, 0), axis=1, keepdims=True)
        entries.append((own == lanes).astype(F32))
        mine = jnp.maximum(mine, jnp.max(entries[i], axis=0, keepdims=True))
    mine_c = to_column(mine, eye)
    before = (slots_c // group == slots // group) & (slots_c < slots)
    rank = jnp.sum(jnp.where(before, mine_c, 0.0), axis=0, keepdims=True).astype(jnp.int32)
    source = slots // group
    flip = source ^ pair_idx
    place = jnp.where(flip < near, source ^ (pair_idx & ~(near - 1)), flip) * capacity + rank
    place = place.astype(F32)
    neighbours = coupled.shape[0]
    ids = lax.broadcasted_iota(jnp.int32, (neighbours, 1), 0)
    square = eye_mask(neighbours)
    column = lax.broadcasted_iota(jnp.int32, (neighbours, lanes_out), 1)
    copies[4].wait()
    for i in range(per_device):
        found = jnp.sum(entries[i] * place, axis=1, keepdims=True).astype(jnp.int32)
        match = found == column
        table[pl.ds(i, 1), :] = jnp.sum(jnp.where(match, ids, 0), axis=0, keepdims=True)
        value = to_column(couplings[pl.ds(i, 1), :], square)
        coefficients[pl.ds(i, 1), :] = jnp.sum(jnp.where(match, value, 0.0), axis=0, keepdims=True)

    eye = eye_mask(width)
    copies[2].wait()
    copies[3].wait()
    copies[5].wait()
    total = jnp.zeros((orbitals, width), F32)
    counts_a = end_counts(orbitals, per_device, lambda s: ends[0, s])
    counts_b = end_counts(orbitals, per_device, lambda s: ends[1, s])
    for s in range(per_device):
        block = state[s]
        payload[pl.ds(s * width, width), :] = block.astype(BF16)
        total += singles_terms(block, projector[pl.ds(s, 1), :], counts_a[s] + counts_b[s], eye)
    tail = payload.shape[0] - per_device * width
    payload[pl.ds(per_device * width, tail), :] = tail_rows(total, tail)


def select_kernel(capacity, per_device, orbitals, width, lanes, row, swap, index, gathered, outs):
    blocks = per_device * width
    tail = gathered.shape[1] - blocks
    total = join_parts(gathered[0, pl.ds(blocks, tail), :], orbitals)
    for d in range(1, gathered.shape[0]):
        total += join_parts(gathered[d, pl.ds(blocks, tail), :], orbitals)
    rows = tail_rows(total, tail)
    for lane, out in zip(lanes, outs):
        for c in range(capacity):
            j = index[row + c, lane]
            first = pl.multiple_of((j % per_device) * width, ROWS)
            out[pl.ds(c * width, width), :] = gathered[(j // per_device) ^ swap, pl.ds(first, width), :]
        out[pl.ds(capacity * width, tail), :] = rows


def add_blocks(capacity, orbitals, index, coefficients, intersections, blocks, coupling, singles):
    per_device, width = intersections.shape[0], intersections.shape[2]
    slots = [(place * capacity + c, ref, c * width) for place, ref in blocks for c in range(capacity)]
    wide = [[] for _ in range(per_device)]
    scaled = [[] for _ in range(per_device)]
    empty = jnp.zeros((width, width), BF16)
    for p in range(0, len(slots), 2):
        part = slots[p : p + 2]
        mixing = [
            jnp.concatenate([intersections[s, index[s, lane]] for lane, _, _ in part], axis=1)
            for s in range(per_device)
        ]
        near = [ref[pl.ds(row, width), :] for _, ref, row in part]
        if len(part) == 2:
            near = jnp.concatenate(
                [jnp.concatenate([near[0], empty], axis=1), jnp.concatenate([empty, near[1]], axis=1)], axis=0
            )
        else:
            near = near[0]
        lifted = jnp.dot(jnp.concatenate(mixing, axis=0), near, preferred_element_type=F32)
        for s in range(per_device):
            wide[s].append(mixing[s])
            for i, (lane, _, _) in enumerate(part):
                block = lifted[s * width : (s + 1) * width, i * width : (i + 1) * width]
                scaled[s].append((coefficients[s, lane] * block).astype(BF16))
    for s in range(per_device):
        if slots:
            coupling[s] = coupling[s] + lax.dot_general(
                jnp.concatenate(scaled[s], axis=1), jnp.concatenate(wide[s], axis=1),
                (((1,), (1,)), ((), ())), preferred_element_type=F32,
            )
    for _, ref in blocks:
        tail = ref.shape[0] - capacity * width
        singles = singles + join_parts(ref[pl.ds(capacity * width, tail), :], orbitals)
    return singles


def gather_terms(capacity, orbitals, index, coefficients, intersections, every, places, blocks, before):
    per_device, width = intersections.shape[0], intersections.shape[2]
    coupling = [jnp.zeros((width, width), F32) for _ in range(per_device)]
    singles = jnp.zeros((orbitals, width), F32)
    if before is not None:
        coupling = [before[pl.ds(s * width, width), :] for s in range(per_device)]
        singles = before[pl.ds(per_device * width, orbitals), :]
    operands = (capacity, orbitals, index, coefficients, intersections)
    if every is not None:
        unit = min(every.shape[0], 4)

        def step(i, carry):
            parts = list(carry[:-1])
            some = [(i * unit + u, every.at[i * unit + u]) for u in range(unit)]
            total = add_blocks(*operands, some, parts, carry[-1])
            return (*parts, total)

        *coupling, singles = lax.fori_loop(0, every.shape[0] // unit, step, (*coupling, singles))
    singles = add_blocks(*operands, list(zip(places, blocks)), coupling, singles)
    return coupling, singles


def terms_kernel(capacity, orbitals, has_every, places, index, coefficients, intersections, *refs):
    refs, out = list(refs[:-1]), refs[-1]
    every = refs.pop(0) if has_every else None
    coupling, singles = gather_terms(
        capacity, orbitals, index, coefficients, intersections, every, places, refs, None
    )
    width = intersections.shape[2]
    for s, part in enumerate(coupling):
        out[pl.ds(s * width, width), :] = part
    out[pl.ds(len(coupling) * width, orbitals), :] = singles


def update_kernel(
    last, capacity, orbitals, places,
    index, coefficients, ends, intersections, before, *refs,
):
    blocks = refs[: len(places)]
    state, integrals, energies, projector, out_a, out_b = refs[len(places) : len(places) + 6]
    final = out_a, out_b
    if last:
        out_a, out_b, sems = refs[-3:]
    copies = []
    per_device, width = state.shape[0], state.shape[1]
    coupling, singles = gather_terms(
        capacity, orbitals, index, coefficients, intersections, None, places, blocks, before
    )
    eye = eye_mask(width)
    total = jnp.zeros((orbitals, width), F32)
    counts_a = end_counts(orbitals, per_device, lambda s: ends[0, s])
    counts_b = end_counts(orbitals, per_device, lambda s: ends[1, s])
    for s in range(per_device):
        old = state[s]
        energy = energies[pl.ds(s, 1), :]
        energy_c = to_column(energy, eye)
        proj = projector[pl.ds(s, 1), :]
        proj_c = to_column(proj, eye)
        left = jnp.sum(counts_a[s] * singles, axis=0, keepdims=True)
        right = jnp.sum(counts_b[s] * singles, axis=0, keepdims=True)
        residual = (
            integrals[s].astype(F32) + energy_c * old + old * energy - coupling[s]
            + to_column(left, eye) * proj + proj_c * right
        )
        new = old - residual / (energy_c + energy)
        out_a[s] = new
        if last:
            out_b[s] = residual
            for i in range(2):
                copies.append(pltpu.make_async_copy((out_a, out_b)[i].at[s], final[i].at[s], sems.at[i, s]))
                copies[-1].start()
        else:
            out_b[pl.ds(s * width, width), :] = new.astype(BF16)
            total += singles_terms(new, proj, counts_a[s] + counts_b[s], eye)
    for copy in copies:
        copy.wait()
    if not last:
        tail = out_b.shape[0] - per_device * width
        out_b[pl.ds(per_device * width, tail), :] = tail_rows(total, tail)


def tail_size(orbitals):
    return -(-PARTS * orbitals // ROWS) * ROWS


def cost(flops):
    return pl.CostEstimate(flops=flops, bytes_accessed=0, transcendentals=0)


def body(
    amplitudes, integrals, energies, intersections, couplings, projector, pair_orbitals, coupled, pair_slot,
):
    pair_count = lax.axis_size("pairs")
    per_device, width = amplitudes.shape[0], amplitudes.shape[1]
    total, neighbours = coupled.shape
    capacity = 1 + neighbours // pair_count
    orbitals = total // PAIRS_ORB
    tail = tail_size(orbitals)
    stride = capacity * width + tail
    orb_count = lax.axis_size("orb")
    direct = pair_count in (4, 8) and orb_count == 4
    tables = VMEM if direct else SMEM
    half = pair_count // 2
    mirrors = [0, half] if direct else [0]
    near = 1 if direct else pair_count
    lanes = -(-pair_count * capacity // 128) * 128
    ends = pair_orbitals.T
    small = pltpu.CompilerParams(vmem_limit_bytes=SMALL)
    params = pltpu.CompilerParams(vmem_limit_bytes=LIMIT)
    block_shape = jax.ShapeDtypeStruct((stride, width), BF16)
    terms_shape = jax.ShapeDtypeStruct((per_device * width + -(-orbitals // 8) * 8, width), F32)
    payload_shape = jax.ShapeDtypeStruct((per_device * width + tail, width), BF16)
    payload, send_index, index, coefficients = pl.pallas_call(
        functools.partial(setup_kernel, capacity, orbitals, near, mirrors, direct),
        out_shape=(
            payload_shape,
            jax.ShapeDtypeStruct((-(-len(mirrors) * capacity // 8) * 8, lanes), jnp.int32),
            jax.ShapeDtypeStruct((per_device, lanes), jnp.int32),
            jax.ShapeDtypeStruct((per_device, lanes), F32),
        ),
        in_specs=[HBM] * 6,
        out_specs=[VMEM] * 4,
        scratch_shapes=[
            pltpu.VMEM(ends.shape, jnp.int32),
            pltpu.VMEM(amplitudes.shape, F32),
            pltpu.VMEM(projector.shape, F32),
            pltpu.VMEM((neighbours, total), jnp.int32),
            pltpu.VMEM((1, total), jnp.int32),
            pltpu.VMEM(couplings.shape, F32),
            pltpu.SemaphoreType.DMA((6,)),
        ],
        compiler_params=small if direct else pltpu.CompilerParams(vmem_limit_bytes=WHOLE),
        name="setup",
    )(
        *[
            pltpu.with_memory_space_constraint(x, pltpu.HBM)
            for x in (ends, amplitudes, projector, coupled.T, pair_slot.reshape(1, total), couplings)
        ]
    )

    def join(*parts, after=()):
        def kernel(*refs):
            if len(parts) == 1:
                refs[-1][...] = refs[0][...]
            else:
                for i in range(len(parts)):
                    refs[-1][i] = refs[i][...]

        shape = payload_shape.shape if len(parts) == 1 else (len(parts), *payload_shape.shape)
        return pl.pallas_call(
            kernel,
            out_shape=jax.ShapeDtypeStruct(shape, BF16),
            in_specs=[VMEM] * len(parts) + [ANY] * len(after),
            out_specs=VMEM,
            compiler_params=small,
            cost_estimate=cost(0),
            name="join",
        )(*parts, *after)

    def select(row, flips, gathered):
        def kernel(index, source, *refs):
            outs, held = refs[: len(flips)], refs[-1]
            swap = 0
            if row:
                swap = lax.axis_index("orb") // 2 * 2
                for c in range(2):
                    for x in range(2):
                        held[2 * x + c] = source[c, x]
            else:
                held = source
            select_kernel(capacity, per_device, orbitals, width, flips, row, swap, index, held, outs)

        return pl.pallas_call(
            kernel,
            out_shape=[block_shape] * len(flips),
            in_specs=[VMEM, VMEM],
            out_specs=[VMEM] * len(flips),
            scratch_shapes=[pltpu.VMEM((4, *payload_shape.shape), BF16)],
            compiler_params=small,
            cost_estimate=cost(0),
            name="select",
        )(send_index, gathered)

    def select_all(gathered):
        def kernel(index, source, out):
            outs = [out.at[i] for i in range(pair_count)]
            select_kernel(capacity, per_device, orbitals, width, range(pair_count), 0, 0, index, source, outs)

        return pl.pallas_call(
            kernel,
            out_shape=jax.ShapeDtypeStruct((pair_count, stride, width), BF16),
            in_specs=[VMEM, VMEM],
            out_specs=VMEM,
            compiler_params=small,
            name="select",
        )(send_index, gathered)

    def exchange(block, axis, flip):
        return lax.ppermute(block, axis, [(p, p ^ flip) for p in range(lax.axis_size(axis))])

    def terms(every, places, blocks):
        extra = [] if every is None else [every]
        return pl.pallas_call(
            functools.partial(terms_kernel, capacity, orbitals, every is not None, places),
            out_shape=terms_shape,
            in_specs=[tables, tables] + [VMEM] * (1 + len(extra) + len(blocks)),
            out_specs=VMEM,
            cost_estimate=cost(TERMS_COST),
            compiler_params=params,
            name="terms",
        )(index, coefficients, intersections, *extra, *blocks)

    state = amplitudes
    for step in range(ITERS):
        last = step == ITERS - 1
        places, late = [], []
        if direct:
            mirror = exchange(payload, "pairs", half)
            flips = [0, *range(half - 1, 0, -1)]
            cores = [[o, o + 1] for o in range(0, orb_count, 2)]
            held = lax.all_gather(payload, "orb", axis=0, tiled=False)
            across = pair_count - 1
            order = [0, half - 1, across, *range(half - 2, 0, -1)]
            sent = select(0, order, held)
            arrived = [sent[0]] + [exchange(part, "pairs", flip) for flip, part in zip(order[1:], sent[1:])]
            mirror = join(mirror, after=sent[:1])
            held = join(mirror, exchange(mirror, "orb", 2), after=arrived[:1])
            held = lax.all_gather(held, "orb", axis=0, axis_index_groups=cores)
            close = [flip for flip in flips if flip + half != across]
            sent = select(capacity, close, held)
            partial = terms(None, [*order, half], arrived + [sent[0]])
            places = [half + flip for flip in close[1:]]
            late = [exchange(part, "pairs", flip) for flip, part in zip(close[1:], sent[1:])]
        else:
            gathered = lax.all_gather(payload, "orb", axis=0, tiled=False)
            outgoing = select_all(gathered)
            every = lax.all_to_all(outgoing, "pairs", split_axis=0, concat_axis=0, tiled=True)
            partial = terms(every, [], [])
        second = jax.ShapeDtypeStruct(amplitudes.shape, F32) if last else payload_shape
        state, payload = pl.pallas_call(
            functools.partial(update_kernel, last, capacity, orbitals, places),
            out_shape=(jax.ShapeDtypeStruct(amplitudes.shape, F32), second),
            in_specs=[VMEM] * (9 + len(late)),
            out_specs=(HBM, HBM) if last else (VMEM, VMEM),
            scratch_shapes=[
                pltpu.VMEM(amplitudes.shape, F32),
                pltpu.VMEM(amplitudes.shape, F32),
                pltpu.SemaphoreType.DMA((2, per_device)),
            ]
            if last
            else [],
            compiler_params=params,
            name="update",
        )(
            index, coefficients, ends, intersections, partial, *late, state, integrals, energies, projector,
        )
    return state, payload


def solution(mesh):
    split = ("pairs", "orb")
    return jax.shard_map(
        body,
        mesh=mesh,
        in_specs=(
            P(split, None, None),
            P(split, None, None),
            P(split, None),
            P(split, None, None, None),
            P(split, None),
            P(split, None),
            P(split, None),
            P(),
            P(),
        ),
        out_specs=(P(split, None, None), P(split, None, None)),
        check_vma=False,
    )
```

```python
import functools

import jax
import jax.numpy as jnp
from jax import lax
from jax.experimental import pallas as pl
from jax.experimental.pallas import tpu as pltpu
from jax.sharding import PartitionSpec as P

PAIRS_ORB = 32
ITERS = 2
ROWS = 16
PARTS = 3
TERMS_COST = 20_000_000_000

F32 = jnp.float32
BF16 = jnp.bfloat16
VMEM = pl.BlockSpec(memory_space=pltpu.VMEM)
SMEM = pl.BlockSpec(memory_space=pltpu.SMEM)
ANY = pl.BlockSpec(memory_space=pl.ANY)
HBM = pl.BlockSpec(memory_space=pltpu.HBM)
LIMIT = 16 * 1024 * 1024
SMALL = 8 * 1024 * 1024
WHOLE = 60 * 1024 * 1024


def eye_mask(width):
    rows = lax.broadcasted_iota(jnp.int32, (width, width), 0)
    cols = lax.broadcasted_iota(jnp.int32, (width, width), 1)
    return rows == cols


def to_row(column, eye):
    return jnp.sum(jnp.where(eye, column, 0.0), axis=0, keepdims=True)


def to_column(row, eye):
    return jnp.sum(jnp.where(eye, row, 0.0), axis=1, keepdims=True)


def split_parts(value):
    parts = []
    for _ in range(PARTS):
        part = value.astype(BF16)
        parts.append(part)
        value = value - part.astype(F32)
    return parts


def tail_rows(value, rows):
    parts = split_parts(value)
    missing = rows - sum(part.shape[0] for part in parts)
    if missing:
        parts.append(jnp.zeros((missing, value.shape[1]), BF16))
    return jnp.concatenate([part.astype(F32) for part in parts], axis=0).astype(BF16)


def join_parts(rows, orbitals):
    rows = rows.astype(F32)
    value = rows[:orbitals]
    for part in range(1, PARTS):
        value = value + rows[part * orbitals : (part + 1) * orbitals]
    return value


def singles_terms(state, projector_row, count, eye):
    projected = to_row(jnp.sum(state * projector_row, axis=1, keepdims=True), eye)
    return count * projected


def end_counts(orbitals, per_device, end):
    ids = lax.broadcasted_iota(jnp.int32, (orbitals, 1), 0)
    return [(ids == end(s)).astype(F32) for s in range(per_device)]


def fetch(pairs, sems):
    copies = [pltpu.make_async_copy(src, dst, sems.at[i]) for i, (src, dst) in enumerate(pairs)]
    for copy in copies:
        copy.start()
    return copies


def setup_kernel(
    capacity, orbitals, near, mirrors, direct,
    ends_hbm, state_hbm, projector_hbm, coupled_hbm, slot_hbm, couplings_hbm,
    payload, index, table, coefficients,
    ends, state, projector, coupled, slot, couplings, sems,
):
    copies = fetch(
        (
            (coupled_hbm, coupled), (slot_hbm, slot), (projector_hbm, projector), (state_hbm, state),
            (couplings_hbm, couplings), (ends_hbm, ends),
        ),
        sems,
    )
    per_device, width = state.shape[0], state.shape[1]
    count = slot.shape[1]
    pair_count, orb_count = lax.axis_size("pairs"), lax.axis_size("orb")
    pair_idx, orb_idx = lax.axis_index("pairs"), lax.axis_index("orb")
    group = orb_count * per_device
    lanes_out = index.shape[1]
    copies[0].wait()
    copies[1].wait()
    slots = slot[...]
    wanted = coupled[...]
    lanes = lax.broadcasted_iota(jnp.int32, (1, count), 1)
    members = lax.broadcasted_iota(jnp.int32, (group, 1), 0)
    slot_ids = lax.broadcasted_iota(jnp.int32, (count, lanes_out), 0)
    column = lax.broadcasted_iota(jnp.int32, (count, lanes_out), 1)
    dest = column ^ pair_idx if direct else column
    owner = (slot_ids // per_device == dest * orb_count + orb_idx) & (column < pair_count)
    for m, flip in enumerate(mirrors):
        base = (pair_idx ^ flip) * group
        pairs = jnp.sum(jnp.where(slots == base + members, lanes, 0), axis=1, keepdims=True)
        hits = jnp.zeros((group, count), F32)
        for g in range(group):
            hit = jnp.max((wanted == pairs[g : g + 1, :]).astype(F32), axis=0, keepdims=True)
            hits = jnp.where(members == g, hit, hits)
        needed = jnp.dot(hits, owner.astype(F32), preferred_element_type=F32) > 0.5
        run = jnp.zeros((1, lanes_out), jnp.int32)
        picked = [jnp.zeros((1, lanes_out), jnp.int32) for _ in range(capacity)]
        for g in range(group):
            hit = needed[g : g + 1, :].astype(jnp.int32)
            for c in range(capacity):
                picked[c] = picked[c] + jnp.where((hit == 1) & (run == c), g, 0)
            run = run + hit
        for c, row in enumerate(picked):
            index[pl.ds(m * capacity + c, 1), :] = row

    eye = eye_mask(count)
    slots_c = jnp.sum(jnp.where(eye, slots, 0), axis=1, keepdims=True)
    first = (pair_idx * orb_count + orb_idx) * per_device
    entries = []
    mine = jnp.zeros((1, count), F32)
    for i in range(per_device):
        own = jnp.sum(jnp.where(lanes == first + i, wanted, 0), axis=1, keepdims=True)
        entries.append((own == lanes).astype(F32))
        mine = jnp.maximum(mine, jnp.max(entries[i], axis=0, keepdims=True))
    mine_c = to_column(mine, eye)
    before = (slots_c // group == slots // group) & (slots_c < slots)
    rank = jnp.sum(jnp.where(before, mine_c, 0.0), axis=0, keepdims=True).astype(jnp.int32)
    source = slots // group
    flip = source ^ pair_idx
    place = jnp.where(flip < near, source ^ (pair_idx & ~(near - 1)), flip) * capacity + rank
    place = place.astype(F32)
    neighbours = coupled.shape[0]
    ids = lax.broadcasted_iota(jnp.int32, (neighbours, 1), 0)
    square = eye_mask(neighbours)
    column = lax.broadcasted_iota(jnp.int32, (neighbours, lanes_out), 1)
    copies[4].wait()
    for i in range(per_device):
        found = jnp.sum(entries[i] * place, axis=1, keepdims=True).astype(jnp.int32)
        match = found == column
        table[pl.ds(i, 1), :] = jnp.sum(jnp.where(match, ids, 0), axis=0, keepdims=True)
        value = to_column(couplings[pl.ds(i, 1), :], square)
        coefficients[pl.ds(i, 1), :] = jnp.sum(jnp.where(match, value, 0.0), axis=0, keepdims=True)

    eye = eye_mask(width)
    copies[2].wait()
    copies[3].wait()
    copies[5].wait()
    total = jnp.zeros((orbitals, width), F32)
    counts_a = end_counts(orbitals, per_device, lambda s: ends[0, s])
    counts_b = end_counts(orbitals, per_device, lambda s: ends[1, s])
    for s in range(per_device):
        block = state[s]
        payload[pl.ds(s * width, width), :] = block.astype(BF16)
        total += singles_terms(block, projector[pl.ds(s, 1), :], counts_a[s] + counts_b[s], eye)
    tail = payload.shape[0] - per_device * width
    payload[pl.ds(per_device * width, tail), :] = tail_rows(total, tail)


def select_kernel(capacity, per_device, orbitals, width, lanes, row, swap, index, gathered, outs):
    blocks = per_device * width
    tail = gathered.shape[1] - blocks
    total = join_parts(gathered[0, pl.ds(blocks, tail), :], orbitals)
    for d in range(1, gathered.shape[0]):
        total += join_parts(gathered[d, pl.ds(blocks, tail), :], orbitals)
    rows = tail_rows(total, tail)
    for lane, out in zip(lanes, outs):
        for c in range(capacity):
            j = index[row + c, lane]
            first = pl.multiple_of((j % per_device) * width, ROWS)
            out[pl.ds(c * width, width), :] = gathered[(j // per_device) ^ swap, pl.ds(first, width), :]
        out[pl.ds(capacity * width, tail), :] = rows


def add_blocks(capacity, orbitals, index, coefficients, intersections, blocks, coupling, singles):
    per_device, width = intersections.shape[0], intersections.shape[2]
    slots = [(place * capacity + c, ref, c * width) for place, ref in blocks for c in range(capacity)]
    wide = [[] for _ in range(per_device)]
    scaled = [[] for _ in range(per_device)]
    empty = jnp.zeros((width, width), BF16)
    for p in range(0, len(slots), 2):
        part = slots[p : p + 2]
        mixing = [
            jnp.concatenate([intersections[s, index[s, lane]] for lane, _, _ in part], axis=1)
            for s in range(per_device)
        ]
        near = [ref[pl.ds(row, width), :] for _, ref, row in part]
        if len(part) == 2:
            near = jnp.concatenate(
                [jnp.concatenate([near[0], empty], axis=1), jnp.concatenate([empty, near[1]], axis=1)], axis=0
            )
        else:
            near = near[0]
        lifted = jnp.dot(jnp.concatenate(mixing, axis=0), near, preferred_element_type=F32)
        for s in range(per_device):
            wide[s].append(mixing[s])
            for i, (lane, _, _) in enumerate(part):
                block = lifted[s * width : (s + 1) * width, i * width : (i + 1) * width]
                scaled[s].append((coefficients[s, lane] * block).astype(BF16))
    for s in range(per_device):
        if slots:
            coupling[s] = coupling[s] + lax.dot_general(
                jnp.concatenate(scaled[s], axis=1), jnp.concatenate(wide[s], axis=1),
                (((1,), (1,)), ((), ())), preferred_element_type=F32,
            )
    for _, ref in blocks:
        tail = ref.shape[0] - capacity * width
        singles = singles + join_parts(ref[pl.ds(capacity * width, tail), :], orbitals)
    return singles


def gather_terms(capacity, orbitals, index, coefficients, intersections, every, places, blocks, before):
    per_device, width = intersections.shape[0], intersections.shape[2]
    coupling = [jnp.zeros((width, width), F32) for _ in range(per_device)]
    singles = jnp.zeros((orbitals, width), F32)
    if before is not None:
        coupling = [before[pl.ds(s * width, width), :] for s in range(per_device)]
        singles = before[pl.ds(per_device * width, orbitals), :]
    operands = (capacity, orbitals, index, coefficients, intersections)
    if every is not None:
        unit = min(every.shape[0], 4)

        def step(i, carry):
            parts = list(carry[:-1])
            some = [(i * unit + u, every.at[i * unit + u]) for u in range(unit)]
            total = add_blocks(*operands, some, parts, carry[-1])
            return (*parts, total)

        *coupling, singles = lax.fori_loop(0, every.shape[0] // unit, step, (*coupling, singles))
    singles = add_blocks(*operands, list(zip(places, blocks)), coupling, singles)
    return coupling, singles


def add_ready(capacity, orbitals, wide, rows, blocks, coupling, singles):
    per_device, width = wide.shape[0], wide.shape[1]
    slots = [(ref, c * width) for ref in blocks for c in range(capacity)]
    scaled = [[] for _ in range(per_device)]
    empty = jnp.zeros((width, width), BF16)
    for p in range(0, len(slots), 2):
        near = [ref[pl.ds(row, width), :] for ref, row in slots[p : p + 2]]
        lanes = pl.ds(p * width, len(near) * width)
        if len(near) == 2:
            near = jnp.concatenate(
                [jnp.concatenate([near[0], empty], axis=1), jnp.concatenate([empty, near[1]], axis=1)], axis=0
            )
        else:
            near = near[0]
        mixing = jnp.concatenate([wide[s, :, lanes] for s in range(per_device)], axis=0)
        lifted = jnp.dot(mixing, near, preferred_element_type=F32)
        for s in range(per_device):
            block = lifted[s * width : (s + 1) * width]
            scaled[s].append((rows[pl.ds(s, 1), lanes] * block).astype(BF16))
    for s in range(per_device):
        coupling[s] = coupling[s] + lax.dot_general(
            jnp.concatenate(scaled[s], axis=1), wide[s], (((1,), (1,)), ((), ())), preferred_element_type=F32
        )
    for ref in blocks:
        tail = ref.shape[0] - capacity * width
        singles = singles + join_parts(ref[pl.ds(capacity * width, tail), :], orbitals)
    return singles


def terms_kernel(capacity, orbitals, has_every, places, later, index, coefficients, intersections, *refs):
    refs = list(refs)
    if later:
        rows, wide = refs.pop(), refs.pop()
        per_device, width = intersections.shape[0], intersections.shape[2]
        for j, lane in enumerate([place * capacity + c for place in later for c in range(capacity)]):
            lanes = pl.ds(j * width, width)
            for s in range(per_device):
                wide[s, :, lanes] = intersections[s, index[s, lane]]
                rows[pl.ds(s, 1), lanes] = jnp.full((1, width), coefficients[s, lane], F32)
    out = refs.pop()
    every = refs.pop(0) if has_every else None
    coupling, singles = gather_terms(
        capacity, orbitals, index, coefficients, intersections, every, places, refs, None
    )
    width = intersections.shape[2]
    for s, part in enumerate(coupling):
        out[pl.ds(s * width, width), :] = part
    out[pl.ds(len(coupling) * width, orbitals), :] = singles


def update_kernel(
    last, capacity, orbitals, count,
    ends, before, *refs,
):
    if count:
        wide, rows, refs = refs[0], refs[1], refs[2:]
    blocks = refs[:count]
    state, integrals, energies, projector, out_a, out_b = refs[count : count + 6]
    final = out_a, out_b
    if last:
        out_a, out_b, sems = refs[-3:]
    copies = []
    per_device, width = state.shape[0], state.shape[1]
    coupling = [before[pl.ds(s * width, width), :] for s in range(per_device)]
    singles = before[pl.ds(per_device * width, orbitals), :]
    if count:
        singles = add_ready(capacity, orbitals, wide, rows, blocks, coupling, singles)
    eye = eye_mask(width)
    total = jnp.zeros((orbitals, width), F32)
    counts_a = end_counts(orbitals, per_device, lambda s: ends[0, s])
    counts_b = end_counts(orbitals, per_device, lambda s: ends[1, s])
    for s in range(per_device):
        old = state[s]
        energy = energies[pl.ds(s, 1), :]
        energy_c = to_column(energy, eye)
        proj = projector[pl.ds(s, 1), :]
        proj_c = to_column(proj, eye)
        left = jnp.sum(counts_a[s] * singles, axis=0, keepdims=True)
        right = jnp.sum(counts_b[s] * singles, axis=0, keepdims=True)
        residual = (
            integrals[s].astype(F32) + energy_c * old + old * energy - coupling[s]
            + to_column(left, eye) * proj + proj_c * right
        )
        new = old - residual / (energy_c + energy)
        out_a[s] = new
        if last:
            out_b[s] = residual
            for i in range(2):
                copies.append(pltpu.make_async_copy((out_a, out_b)[i].at[s], final[i].at[s], sems.at[i, s]))
                copies[-1].start()
        else:
            out_b[pl.ds(s * width, width), :] = new.astype(BF16)
            total += singles_terms(new, proj, counts_a[s] + counts_b[s], eye)
    for copy in copies:
        copy.wait()
    if not last:
        tail = out_b.shape[0] - per_device * width
        out_b[pl.ds(per_device * width, tail), :] = tail_rows(total, tail)


def tail_size(orbitals):
    return -(-PARTS * orbitals // ROWS) * ROWS


def cost(flops):
    return pl.CostEstimate(flops=flops, bytes_accessed=0, transcendentals=0)


def body(
    amplitudes, integrals, energies, intersections, couplings, projector, pair_orbitals, coupled, pair_slot,
):
    pair_count = lax.axis_size("pairs")
    per_device, width = amplitudes.shape[0], amplitudes.shape[1]
    total, neighbours = coupled.shape
    capacity = 1 + neighbours // pair_count
    orbitals = total // PAIRS_ORB
    tail = tail_size(orbitals)
    stride = capacity * width + tail
    orb_count = lax.axis_size("orb")
    direct = pair_count in (4, 8) and orb_count == 4
    tables = VMEM if direct else SMEM
    half = pair_count // 2
    mirrors = [0, half] if direct else [0]
    near = 1 if direct else pair_count
    lanes = -(-pair_count * capacity // 128) * 128
    ends = pair_orbitals.T
    small = pltpu.CompilerParams(vmem_limit_bytes=SMALL)
    params = pltpu.CompilerParams(vmem_limit_bytes=LIMIT)
    block_shape = jax.ShapeDtypeStruct((stride, width), BF16)
    terms_shape = jax.ShapeDtypeStruct((per_device * width + -(-orbitals // 8) * 8, width), F32)
    payload_shape = jax.ShapeDtypeStruct((per_device * width + tail, width), BF16)
    payload, send_index, index, coefficients = pl.pallas_call(
        functools.partial(setup_kernel, capacity, orbitals, near, mirrors, direct),
        out_shape=(
            payload_shape,
            jax.ShapeDtypeStruct((-(-len(mirrors) * capacity // 8) * 8, lanes), jnp.int32),
            jax.ShapeDtypeStruct((per_device, lanes), jnp.int32),
            jax.ShapeDtypeStruct((per_device, lanes), F32),
        ),
        in_specs=[HBM] * 6,
        out_specs=[VMEM] * 4,
        scratch_shapes=[
            pltpu.VMEM(ends.shape, jnp.int32),
            pltpu.VMEM(amplitudes.shape, F32),
            pltpu.VMEM(projector.shape, F32),
            pltpu.VMEM((neighbours, total), jnp.int32),
            pltpu.VMEM((1, total), jnp.int32),
            pltpu.VMEM(couplings.shape, F32),
            pltpu.SemaphoreType.DMA((6,)),
        ],
        compiler_params=small if direct else pltpu.CompilerParams(vmem_limit_bytes=WHOLE),
        name="setup",
    )(
        *[
            pltpu.with_memory_space_constraint(x, pltpu.HBM)
            for x in (ends, amplitudes, projector, coupled.T, pair_slot.reshape(1, total), couplings)
        ]
    )

    def join(*parts, after=()):
        def kernel(*refs):
            if len(parts) == 1:
                refs[-1][...] = refs[0][...]
            else:
                for i in range(len(parts)):
                    refs[-1][i] = refs[i][...]

        shape = payload_shape.shape if len(parts) == 1 else (len(parts), *payload_shape.shape)
        return pl.pallas_call(
            kernel,
            out_shape=jax.ShapeDtypeStruct(shape, BF16),
            in_specs=[VMEM] * len(parts) + [ANY] * len(after),
            out_specs=VMEM,
            compiler_params=small,
            cost_estimate=cost(0),
            name="join",
        )(*parts, *after)

    def select(row, flips, gathered):
        def kernel(index, source, *refs):
            outs, held = refs[: len(flips)], refs[-1]
            swap = 0
            if row:
                swap = lax.axis_index("orb") // 2 * 2
                for c in range(2):
                    for x in range(2):
                        held[2 * x + c] = source[c, x]
            else:
                held = source
            select_kernel(capacity, per_device, orbitals, width, flips, row, swap, index, held, outs)

        return pl.pallas_call(
            kernel,
            out_shape=[block_shape] * len(flips),
            in_specs=[VMEM, VMEM],
            out_specs=[VMEM] * len(flips),
            scratch_shapes=[pltpu.VMEM((4, *payload_shape.shape), BF16)],
            compiler_params=small,
            cost_estimate=cost(0),
            name="select",
        )(send_index, gathered)

    def select_all(gathered):
        def kernel(index, source, out):
            outs = [out.at[i] for i in range(pair_count)]
            select_kernel(capacity, per_device, orbitals, width, range(pair_count), 0, 0, index, source, outs)

        return pl.pallas_call(
            kernel,
            out_shape=jax.ShapeDtypeStruct((pair_count, stride, width), BF16),
            in_specs=[VMEM, VMEM],
            out_specs=VMEM,
            compiler_params=small,
            name="select",
        )(send_index, gathered)

    def exchange(block, axis, flip):
        return lax.ppermute(block, axis, [(p, p ^ flip) for p in range(lax.axis_size(axis))])

    def terms(every, places, blocks, later):
        span = len(later) * capacity * width
        ready = [jax.ShapeDtypeStruct((per_device, width, span), BF16), jax.ShapeDtypeStruct((per_device, span), F32)]
        shapes = [terms_shape, *(ready if later else [])]
        extra = [] if every is None else [every]
        return pl.pallas_call(
            functools.partial(terms_kernel, capacity, orbitals, every is not None, places, later),
            out_shape=shapes,
            in_specs=[tables, tables] + [VMEM] * (1 + len(extra) + len(blocks)),
            out_specs=[VMEM] * len(shapes),
            cost_estimate=cost(TERMS_COST),
            compiler_params=params,
            name="terms",
        )(index, coefficients, intersections, *extra, *blocks)

    state = amplitudes
    for step in range(ITERS):
        last = step == ITERS - 1
        late = []
        if direct:
            mirror = exchange(payload, "pairs", half)
            flips = [0, *range(half - 1, 0, -1)]
            cores = [[o, o + 1] for o in range(0, orb_count, 2)]
            held = lax.all_gather(payload, "orb", axis=0, tiled=False)
            across = pair_count - 1
            order = [0, half - 1, across, *range(half - 2, 0, -1)]
            sent = select(0, order, held)
            arrived = [sent[0]] + [exchange(part, "pairs", flip) for flip, part in zip(order[1:], sent[1:])]
            mirror = join(mirror, after=sent[:1])
            held = join(mirror, exchange(mirror, "orb", 2), after=arrived[:1])
            held = lax.all_gather(held, "orb", axis=0, axis_index_groups=cores)
            close = [flip for flip in flips if flip + half != across]
            sent = select(capacity, close, held)
            later = [half + flip for flip in close[1:]]
            partial = terms(None, [*order, half], arrived + [sent[0]], later)
            late = [exchange(part, "pairs", flip) for flip, part in zip(close[1:], sent[1:])]
        else:
            gathered = lax.all_gather(payload, "orb", axis=0, tiled=False)
            outgoing = select_all(gathered)
            every = lax.all_to_all(outgoing, "pairs", split_axis=0, concat_axis=0, tiled=True)
            partial = terms(every, [], [], [])
        second = jax.ShapeDtypeStruct(amplitudes.shape, F32) if last else payload_shape
        state, payload = pl.pallas_call(
            functools.partial(update_kernel, last, capacity, orbitals, len(late)),
            out_shape=(jax.ShapeDtypeStruct(amplitudes.shape, F32), second),
            in_specs=[VMEM] * (5 + len(partial) + len(late)),
            out_specs=(HBM, HBM) if last else (VMEM, VMEM),
            scratch_shapes=[
                pltpu.VMEM(amplitudes.shape, F32),
                pltpu.VMEM(amplitudes.shape, F32),
                pltpu.SemaphoreType.DMA((2, per_device)),
            ]
            if last
            else [],
            compiler_params=params,
            name="update",
        )(
            ends, *partial, *late, state, integrals, energies, projector,
        )
    return state, payload


def solution(mesh):
    split = ("pairs", "orb")
    return jax.shard_map(
        body,
        mesh=mesh,
        in_specs=(
            P(split, None, None),
            P(split, None, None),
            P(split, None),
            P(split, None, None, None),
            P(split, None),
            P(split, None),
            P(split, None),
            P(),
            P(),
        ),
        out_specs=(P(split, None, None), P(split, None, None)),
        check_vma=False,
    )
```

```python
import functools

import jax
import jax.numpy as jnp
from jax import lax
from jax.experimental import pallas as pl
from jax.experimental.pallas import tpu as pltpu
from jax.sharding import PartitionSpec as P

PAIRS_ORB = 32
ITERS = 2
ROWS = 16
PARTS = 3
TERMS_COST = 20_000_000_000

F32 = jnp.float32
BF16 = jnp.bfloat16
VMEM = pl.BlockSpec(memory_space=pltpu.VMEM)
SMEM = pl.BlockSpec(memory_space=pltpu.SMEM)
ANY = pl.BlockSpec(memory_space=pl.ANY)
HBM = pl.BlockSpec(memory_space=pltpu.HBM)
LIMIT = 16 * 1024 * 1024
SMALL = 8 * 1024 * 1024
WHOLE = 60 * 1024 * 1024


def eye_mask(width):
    rows = lax.broadcasted_iota(jnp.int32, (width, width), 0)
    cols = lax.broadcasted_iota(jnp.int32, (width, width), 1)
    return rows == cols


def to_row(column, eye):
    return jnp.sum(jnp.where(eye, column, 0.0), axis=0, keepdims=True)


def to_column(row, eye):
    return jnp.sum(jnp.where(eye, row, 0.0), axis=1, keepdims=True)


def split_parts(value):
    parts = []
    for _ in range(PARTS):
        part = value.astype(BF16)
        parts.append(part)
        value = value - part.astype(F32)
    return parts


def tail_rows(value, rows):
    parts = split_parts(value)
    missing = rows - sum(part.shape[0] for part in parts)
    if missing:
        parts.append(jnp.zeros((missing, value.shape[1]), BF16))
    return jnp.concatenate([part.astype(F32) for part in parts], axis=0).astype(BF16)


def join_parts(rows, orbitals):
    rows = rows.astype(F32)
    value = rows[:orbitals]
    for part in range(1, PARTS):
        value = value + rows[part * orbitals : (part + 1) * orbitals]
    return value


def singles_terms(state, projector_row, count, eye):
    projected = to_row(jnp.sum(state * projector_row, axis=1, keepdims=True), eye)
    return count * projected


def end_counts(orbitals, per_device, end):
    ids = lax.broadcasted_iota(jnp.int32, (orbitals, 1), 0)
    return [(ids == end(s)).astype(F32) for s in range(per_device)]


def fetch(pairs, sems):
    copies = [pltpu.make_async_copy(src, dst, sems.at[i]) for i, (src, dst) in enumerate(pairs)]
    for copy in copies:
        copy.start()
    return copies


def setup_kernel(
    capacity, orbitals, near, mirrors, direct,
    ends_hbm, state_hbm, projector_hbm, coupled_hbm, slot_hbm, couplings_hbm,
    payload, index, table, coefficients,
    ends, state, projector, coupled, slot, couplings, sems,
):
    copies = fetch(
        (
            (coupled_hbm, coupled), (slot_hbm, slot), (projector_hbm, projector), (state_hbm, state),
            (couplings_hbm, couplings), (ends_hbm, ends),
        ),
        sems,
    )
    per_device, width = state.shape[0], state.shape[1]
    count = slot.shape[1]
    pair_count, orb_count = lax.axis_size("pairs"), lax.axis_size("orb")
    pair_idx, orb_idx = lax.axis_index("pairs"), lax.axis_index("orb")
    group = orb_count * per_device
    lanes_out = index.shape[1]
    copies[0].wait()
    copies[1].wait()
    slots = slot[...]
    wanted = coupled[...]
    lanes = lax.broadcasted_iota(jnp.int32, (1, count), 1)
    members = lax.broadcasted_iota(jnp.int32, (group, 1), 0)
    slot_ids = lax.broadcasted_iota(jnp.int32, (count, lanes_out), 0)
    column = lax.broadcasted_iota(jnp.int32, (count, lanes_out), 1)
    dest = column ^ pair_idx if direct else column
    owner = (slot_ids // per_device == dest * orb_count + orb_idx) & (column < pair_count)
    for m, flip in enumerate(mirrors):
        base = (pair_idx ^ flip) * group
        pairs = jnp.sum(jnp.where(slots == base + members, lanes, 0), axis=1, keepdims=True)
        hits = jnp.zeros((group, count), F32)
        for g in range(group):
            hit = jnp.max((wanted == pairs[g : g + 1, :]).astype(F32), axis=0, keepdims=True)
            hits = jnp.where(members == g, hit, hits)
        needed = jnp.dot(hits, owner.astype(F32), preferred_element_type=F32) > 0.5
        run = jnp.zeros((1, lanes_out), jnp.int32)
        picked = [jnp.zeros((1, lanes_out), jnp.int32) for _ in range(capacity)]
        for g in range(group):
            hit = needed[g : g + 1, :].astype(jnp.int32)
            for c in range(capacity):
                picked[c] = picked[c] + jnp.where((hit == 1) & (run == c), g, 0)
            run = run + hit
        for c, row in enumerate(picked):
            index[pl.ds(m * capacity + c, 1), :] = row

    eye = eye_mask(count)
    slots_c = jnp.sum(jnp.where(eye, slots, 0), axis=1, keepdims=True)
    first = (pair_idx * orb_count + orb_idx) * per_device
    entries = []
    mine = jnp.zeros((1, count), F32)
    for i in range(per_device):
        own = jnp.sum(jnp.where(lanes == first + i, wanted, 0), axis=1, keepdims=True)
        entries.append((own == lanes).astype(F32))
        mine = jnp.maximum(mine, jnp.max(entries[i], axis=0, keepdims=True))
    mine_c = to_column(mine, eye)
    before = (slots_c // group == slots // group) & (slots_c < slots)
    rank = jnp.sum(jnp.where(before, mine_c, 0.0), axis=0, keepdims=True).astype(jnp.int32)
    source = slots // group
    flip = source ^ pair_idx
    place = jnp.where(flip < near, source ^ (pair_idx & ~(near - 1)), flip) * capacity + rank
    place = place.astype(F32)
    neighbours = coupled.shape[0]
    ids = lax.broadcasted_iota(jnp.int32, (neighbours, 1), 0)
    square = eye_mask(neighbours)
    column = lax.broadcasted_iota(jnp.int32, (neighbours, lanes_out), 1)
    copies[4].wait()
    for i in range(per_device):
        found = jnp.sum(entries[i] * place, axis=1, keepdims=True).astype(jnp.int32)
        match = found == column
        table[pl.ds(i, 1), :] = jnp.sum(jnp.where(match, ids, 0), axis=0, keepdims=True)
        value = to_column(couplings[pl.ds(i, 1), :], square)
        coefficients[pl.ds(i, 1), :] = jnp.sum(jnp.where(match, value, 0.0), axis=0, keepdims=True)

    eye = eye_mask(width)
    copies[2].wait()
    copies[3].wait()
    copies[5].wait()
    total = jnp.zeros((orbitals, width), F32)
    counts_a = end_counts(orbitals, per_device, lambda s: ends[0, s])
    counts_b = end_counts(orbitals, per_device, lambda s: ends[1, s])
    for s in range(per_device):
        block = state[s]
        payload[pl.ds(s * width, width), :] = block.astype(BF16)
        total += singles_terms(block, projector[pl.ds(s, 1), :], counts_a[s] + counts_b[s], eye)
    tail = payload.shape[0] - per_device * width
    payload[pl.ds(per_device * width, tail), :] = tail_rows(total, tail)


def select_kernel(capacity, per_device, orbitals, width, lanes, row, swap, index, gathered, outs):
    blocks = per_device * width
    tail = gathered.shape[1] - blocks
    total = join_parts(gathered[0, pl.ds(blocks, tail), :], orbitals)
    for d in range(1, gathered.shape[0]):
        total += join_parts(gathered[d, pl.ds(blocks, tail), :], orbitals)
    rows = tail_rows(total, tail)
    for lane, out in zip(lanes, outs):
        for c in range(capacity):
            j = index[row + c, lane]
            first = pl.multiple_of((j % per_device) * width, ROWS)
            out[pl.ds(c * width, width), :] = gathered[(j // per_device) ^ swap, pl.ds(first, width), :]
        out[pl.ds(capacity * width, tail), :] = rows


def add_blocks(capacity, orbitals, index, coefficients, intersections, blocks, coupling, singles):
    per_device, width = intersections.shape[0], intersections.shape[2]
    slots = [(place * capacity + c, ref, c * width) for place, ref in blocks for c in range(capacity)]
    wide = [[] for _ in range(per_device)]
    scaled = [[] for _ in range(per_device)]
    empty = jnp.zeros((width, width), BF16)
    for p in range(0, len(slots), 2):
        part = slots[p : p + 2]
        mixing = [
            jnp.concatenate([intersections[s, index[s, lane]] for lane, _, _ in part], axis=1)
            for s in range(per_device)
        ]
        near = [ref[pl.ds(row, width), :] for _, ref, row in part]
        if len(part) == 2:
            near = jnp.concatenate(
                [jnp.concatenate([near[0], empty], axis=1), jnp.concatenate([empty, near[1]], axis=1)], axis=0
            )
        else:
            near = near[0]
        lifted = jnp.dot(jnp.concatenate(mixing, axis=0), near, preferred_element_type=F32)
        for s in range(per_device):
            wide[s].append(mixing[s])
            for i, (lane, _, _) in enumerate(part):
                block = lifted[s * width : (s + 1) * width, i * width : (i + 1) * width]
                scaled[s].append((coefficients[s, lane] * block).astype(BF16))
    for s in range(per_device):
        if slots:
            coupling[s] = coupling[s] + lax.dot_general(
                jnp.concatenate(scaled[s], axis=1), jnp.concatenate(wide[s], axis=1),
                (((1,), (1,)), ((), ())), preferred_element_type=F32,
            )
    for _, ref in blocks:
        tail = ref.shape[0] - capacity * width
        singles = singles + join_parts(ref[pl.ds(capacity * width, tail), :], orbitals)
    return singles


def gather_terms(capacity, orbitals, index, coefficients, intersections, every, places, blocks, before):
    per_device, width = intersections.shape[0], intersections.shape[2]
    coupling = [jnp.zeros((width, width), F32) for _ in range(per_device)]
    singles = jnp.zeros((orbitals, width), F32)
    if before is not None:
        coupling = [before[pl.ds(s * width, width), :] for s in range(per_device)]
        singles = before[pl.ds(per_device * width, orbitals), :]
    operands = (capacity, orbitals, index, coefficients, intersections)
    if every is not None:
        unit = min(every.shape[0], 4)

        def step(i, carry):
            parts = list(carry[:-1])
            some = [(i * unit + u, every.at[i * unit + u]) for u in range(unit)]
            total = add_blocks(*operands, some, parts, carry[-1])
            return (*parts, total)

        *coupling, singles = lax.fori_loop(0, every.shape[0] // unit, step, (*coupling, singles))
    singles = add_blocks(*operands, list(zip(places, blocks)), coupling, singles)
    return coupling, singles


def add_ready(capacity, orbitals, wide, rows, blocks, coupling, singles):
    per_device, width = wide.shape[0], wide.shape[1]
    slots = [(ref, c * width) for ref in blocks for c in range(capacity)]
    scaled = [[] for _ in range(per_device)]
    empty = jnp.zeros((width, width), BF16)
    for p in range(0, len(slots), 2):
        near = [ref[pl.ds(row, width), :] for ref, row in slots[p : p + 2]]
        lanes = pl.ds(p * width, len(near) * width)
        if len(near) == 2:
            near = jnp.concatenate(
                [jnp.concatenate([near[0], empty], axis=1), jnp.concatenate([empty, near[1]], axis=1)], axis=0
            )
        else:
            near = near[0]
        mixing = jnp.concatenate([wide[s, :, lanes] for s in range(per_device)], axis=0)
        lifted = jnp.dot(mixing, near, preferred_element_type=F32)
        for s in range(per_device):
            block = lifted[s * width : (s + 1) * width]
            scaled[s].append((rows[pl.ds(s, 1), lanes] * block).astype(BF16))
    for s in range(per_device):
        coupling[s] = coupling[s] + lax.dot_general(
            jnp.concatenate(scaled[s], axis=1), wide[s], (((1,), (1,)), ((), ())), preferred_element_type=F32
        )
    for ref in blocks:
        tail = ref.shape[0] - capacity * width
        singles = singles + join_parts(ref[pl.ds(capacity * width, tail), :], orbitals)
    return singles


def terms_kernel(capacity, orbitals, has_every, places, later, index, coefficients, intersections, *refs):
    refs = list(refs)
    if later:
        rows, wide = refs.pop(), refs.pop()
        per_device, width = intersections.shape[0], intersections.shape[2]
        for j, lane in enumerate([place * capacity + c for place in later for c in range(capacity)]):
            lanes = pl.ds(j * width, width)
            for s in range(per_device):
                wide[s, :, lanes] = intersections[s, index[s, lane]]
                rows[pl.ds(s, 1), lanes] = jnp.full((1, width), coefficients[s, lane], F32)
    out = refs.pop()
    every = refs.pop(0) if has_every else None
    coupling, singles = gather_terms(
        capacity, orbitals, index, coefficients, intersections, every, places, refs, None
    )
    width = intersections.shape[2]
    for s, part in enumerate(coupling):
        out[pl.ds(s * width, width), :] = part
    out[pl.ds(len(coupling) * width, orbitals), :] = singles


def update_kernel(
    last, capacity, orbitals, count,
    ends, before, *refs,
):
    if count:
        wide, rows, refs = refs[0], refs[1], refs[2:]
    blocks = refs[:count]
    state, integrals, energies, projector, out_a, out_b = refs[count : count + 6]
    final = out_a, out_b
    if last:
        out_a, out_b, sems = refs[-3:]
    copies = []
    per_device, width = state.shape[0], state.shape[1]
    coupling = [before[pl.ds(s * width, width), :] for s in range(per_device)]
    singles = before[pl.ds(per_device * width, orbitals), :]
    if count:
        singles = add_ready(capacity, orbitals, wide, rows, blocks, coupling, singles)
    eye = eye_mask(width)
    total = jnp.zeros((orbitals, width), F32)
    counts_a = end_counts(orbitals, per_device, lambda s: ends[0, s])
    counts_b = end_counts(orbitals, per_device, lambda s: ends[1, s])
    for s in range(per_device):
        old = state[s]
        energy = energies[pl.ds(s, 1), :]
        energy_c = to_column(energy, eye)
        proj = projector[pl.ds(s, 1), :]
        proj_c = to_column(proj, eye)
        left = jnp.sum(counts_a[s] * singles, axis=0, keepdims=True)
        right = jnp.sum(counts_b[s] * singles, axis=0, keepdims=True)
        residual = (
            integrals[s].astype(F32) + energy_c * old + old * energy - coupling[s]
            + to_column(left, eye) * proj + proj_c * right
        )
        new = old - residual / (energy_c + energy)
        out_a[s] = new
        if last:
            out_b[s] = residual
            for i in range(2):
                copies.append(pltpu.make_async_copy((out_a, out_b)[i].at[s], final[i].at[s], sems.at[i, s]))
                copies[-1].start()
        else:
            out_b[pl.ds(s * width, width), :] = new.astype(BF16)
            total += singles_terms(new, proj, counts_a[s] + counts_b[s], eye)
    for copy in copies:
        copy.wait()
    if not last:
        tail = out_b.shape[0] - per_device * width
        out_b[pl.ds(per_device * width, tail), :] = tail_rows(total, tail)


def tail_size(orbitals):
    return -(-PARTS * orbitals // ROWS) * ROWS


def cost(flops):
    return pl.CostEstimate(flops=flops, bytes_accessed=0, transcendentals=0)


def body(
    amplitudes, integrals, energies, intersections, couplings, projector, pair_orbitals, coupled, pair_slot,
):
    pair_count = lax.axis_size("pairs")
    per_device, width = amplitudes.shape[0], amplitudes.shape[1]
    total, neighbours = coupled.shape
    capacity = 1 + neighbours // pair_count
    orbitals = total // PAIRS_ORB
    tail = tail_size(orbitals)
    stride = capacity * width + tail
    orb_count = lax.axis_size("orb")
    direct = pair_count in (4, 8) and orb_count == 4
    tables = VMEM if direct else SMEM
    half = pair_count // 2
    mirrors = [0, half] if direct else [0]
    near = 1 if direct else pair_count
    lanes = -(-pair_count * capacity // 128) * 128
    ends = pair_orbitals.T
    small = pltpu.CompilerParams(vmem_limit_bytes=SMALL)
    params = pltpu.CompilerParams(vmem_limit_bytes=LIMIT)
    block_shape = jax.ShapeDtypeStruct((stride, width), BF16)
    terms_shape = jax.ShapeDtypeStruct((per_device * width + -(-orbitals // 8) * 8, width), F32)
    payload_shape = jax.ShapeDtypeStruct((per_device * width + tail, width), BF16)
    payload, send_index, index, coefficients = pl.pallas_call(
        functools.partial(setup_kernel, capacity, orbitals, near, mirrors, direct),
        out_shape=(
            payload_shape,
            jax.ShapeDtypeStruct((-(-len(mirrors) * capacity // 8) * 8, lanes), jnp.int32),
            jax.ShapeDtypeStruct((per_device, lanes), jnp.int32),
            jax.ShapeDtypeStruct((per_device, lanes), F32),
        ),
        in_specs=[HBM] * 6,
        out_specs=[VMEM] * 4,
        scratch_shapes=[
            pltpu.VMEM(ends.shape, jnp.int32),
            pltpu.VMEM(amplitudes.shape, F32),
            pltpu.VMEM(projector.shape, F32),
            pltpu.VMEM((neighbours, total), jnp.int32),
            pltpu.VMEM((1, total), jnp.int32),
            pltpu.VMEM(couplings.shape, F32),
            pltpu.SemaphoreType.DMA((6,)),
        ],
        compiler_params=small if direct else pltpu.CompilerParams(vmem_limit_bytes=WHOLE),
        name="setup",
    )(
        *[
            pltpu.with_memory_space_constraint(x, pltpu.HBM)
            for x in (ends, amplitudes, projector, coupled.T, pair_slot.reshape(1, total), couplings)
        ]
    )

    def join(*parts, after=()):
        def kernel(*refs):
            if len(parts) == 1:
                refs[-1][...] = refs[0][...]
            else:
                for i in range(len(parts)):
                    refs[-1][i] = refs[i][...]

        shape = payload_shape.shape if len(parts) == 1 else (len(parts), *payload_shape.shape)
        return pl.pallas_call(
            kernel,
            out_shape=jax.ShapeDtypeStruct(shape, BF16),
            in_specs=[VMEM] * len(parts) + [ANY] * len(after),
            out_specs=VMEM,
            compiler_params=small,
            cost_estimate=cost(0),
            name="join",
        )(*parts, *after)

    def select(row, flips, gathered):
        def kernel(index, source, *refs):
            outs, held = refs[: len(flips)], refs[-1]
            swap = 0
            if row:
                swap = lax.axis_index("orb") // 2 * 2
                for c in range(2):
                    for x in range(2):
                        held[2 * x + c] = source[c, x]
            else:
                held = source
            select_kernel(capacity, per_device, orbitals, width, flips, row, swap, index, held, outs)

        return pl.pallas_call(
            kernel,
            out_shape=[block_shape] * len(flips),
            in_specs=[VMEM, VMEM],
            out_specs=[VMEM] * len(flips),
            scratch_shapes=[pltpu.VMEM((4, *payload_shape.shape), BF16)],
            compiler_params=small,
            cost_estimate=cost(0),
            name="select",
        )(send_index, gathered)

    def select_all(gathered):
        def kernel(index, source, out):
            outs = [out.at[i] for i in range(pair_count)]
            select_kernel(capacity, per_device, orbitals, width, range(pair_count), 0, 0, index, source, outs)

        return pl.pallas_call(
            kernel,
            out_shape=jax.ShapeDtypeStruct((pair_count, stride, width), BF16),
            in_specs=[VMEM, VMEM],
            out_specs=VMEM,
            compiler_params=small,
            name="select",
        )(send_index, gathered)

    def exchange(block, axis, flip):
        return lax.ppermute(block, axis, [(p, p ^ flip) for p in range(lax.axis_size(axis))])

    def terms(every, places, blocks, later):
        span = len(later) * capacity * width
        ready = [jax.ShapeDtypeStruct((per_device, width, span), BF16), jax.ShapeDtypeStruct((per_device, span), F32)]
        shapes = [terms_shape, *(ready if later else [])]
        extra = [] if every is None else [every]
        return pl.pallas_call(
            functools.partial(terms_kernel, capacity, orbitals, every is not None, places, later),
            out_shape=shapes,
            in_specs=[tables, tables] + [VMEM] * (1 + len(extra) + len(blocks)),
            out_specs=[VMEM] * len(shapes),
            cost_estimate=cost(TERMS_COST),
            compiler_params=params,
            name="terms",
        )(index, coefficients, intersections, *extra, *blocks)

    state = amplitudes
    for step in range(ITERS):
        last = step == ITERS - 1
        late = []
        if direct:
            mirror = exchange(payload, "pairs", half)
            flips = [0, *range(half - 1, 0, -1)]
            cores = [[o, o + 1] for o in range(0, orb_count, 2)]
            held = lax.all_gather(payload, "orb", axis=0, tiled=False)
            across = pair_count - 1
            order = [0, half - 1, across, *range(1, half - 1)]
            sent = select(0, order, held)
            arrived = [sent[0]] + [exchange(part, "pairs", flip) for flip, part in zip(order[1:], sent[1:])]
            mirror = join(mirror, after=sent[:1])
            held = join(mirror, exchange(mirror, "orb", 2), after=arrived[:1])
            held = lax.all_gather(held, "orb", axis=0, axis_index_groups=cores)
            close = [flip for flip in flips if flip + half != across]
            sent = select(capacity, close, held)
            later = [half + flip for flip in close[1:]]
            partial = terms(None, [*order, half], arrived + [sent[0]], later)
            late = [exchange(part, "pairs", flip) for flip, part in zip(close[1:], sent[1:])]
        else:
            gathered = lax.all_gather(payload, "orb", axis=0, tiled=False)
            outgoing = select_all(gathered)
            every = lax.all_to_all(outgoing, "pairs", split_axis=0, concat_axis=0, tiled=True)
            partial = terms(every, [], [], [])
        second = jax.ShapeDtypeStruct(amplitudes.shape, F32) if last else payload_shape
        state, payload = pl.pallas_call(
            functools.partial(update_kernel, last, capacity, orbitals, len(late)),
            out_shape=(jax.ShapeDtypeStruct(amplitudes.shape, F32), second),
            in_specs=[VMEM] * (5 + len(partial) + len(late)),
            out_specs=(HBM, HBM) if last else (VMEM, VMEM),
            scratch_shapes=[
                pltpu.VMEM(amplitudes.shape, F32),
                pltpu.VMEM(amplitudes.shape, F32),
                pltpu.SemaphoreType.DMA((2, per_device)),
            ]
            if last
            else [],
            compiler_params=params,
            name="update",
        )(
            ends, *partial, *late, state, integrals, energies, projector,
        )
    return state, payload


def solution(mesh):
    split = ("pairs", "orb")
    return jax.shard_map(
        body,
        mesh=mesh,
        in_specs=(
            P(split, None, None),
            P(split, None, None),
            P(split, None),
            P(split, None, None, None),
            P(split, None),
            P(split, None),
            P(split, None),
            P(),
            P(),
        ),
        out_specs=(P(split, None, None), P(split, None, None)),
        check_vma=False,
    )
```

```python
import functools

import jax
import jax.numpy as jnp
from jax import lax
from jax.experimental import pallas as pl
from jax.experimental.pallas import tpu as pltpu
from jax.sharding import PartitionSpec as P

PAIRS_ORB = 32
ITERS = 2
ROWS = 16
PARTS = 3
TERMS_COST = 20_000_000_000

F32 = jnp.float32
BF16 = jnp.bfloat16
VMEM = pl.BlockSpec(memory_space=pltpu.VMEM)
SMEM = pl.BlockSpec(memory_space=pltpu.SMEM)
ANY = pl.BlockSpec(memory_space=pl.ANY)
HBM = pl.BlockSpec(memory_space=pltpu.HBM)
LIMIT = 16 * 1024 * 1024
SMALL = 8 * 1024 * 1024
WHOLE = 60 * 1024 * 1024


def eye_mask(width):
    rows = lax.broadcasted_iota(jnp.int32, (width, width), 0)
    cols = lax.broadcasted_iota(jnp.int32, (width, width), 1)
    return rows == cols


def to_row(column, eye):
    return jnp.sum(jnp.where(eye, column, 0.0), axis=0, keepdims=True)


def to_column(row, eye):
    return jnp.sum(jnp.where(eye, row, 0.0), axis=1, keepdims=True)


def split_parts(value):
    parts = []
    for _ in range(PARTS):
        part = value.astype(BF16)
        parts.append(part)
        value = value - part.astype(F32)
    return parts


def tail_rows(value, rows):
    parts = split_parts(value)
    missing = rows - sum(part.shape[0] for part in parts)
    if missing:
        parts.append(jnp.zeros((missing, value.shape[1]), BF16))
    return jnp.concatenate([part.astype(F32) for part in parts], axis=0).astype(BF16)


def join_parts(rows, orbitals):
    rows = rows.astype(F32)
    value = rows[:orbitals]
    for part in range(1, PARTS):
        value = value + rows[part * orbitals : (part + 1) * orbitals]
    return value


def singles_terms(state, projector_row, count, eye):
    projected = to_row(jnp.sum(state * projector_row, axis=1, keepdims=True), eye)
    return count * projected


def end_counts(orbitals, per_device, end):
    ids = lax.broadcasted_iota(jnp.int32, (orbitals, 1), 0)
    return [(ids == end(s)).astype(F32) for s in range(per_device)]


def fetch(pairs, sems):
    copies = [pltpu.make_async_copy(src, dst, sems.at[i]) for i, (src, dst) in enumerate(pairs)]
    for copy in copies:
        copy.start()
    return copies


def setup_kernel(
    capacity, orbitals, near, mirrors, direct,
    ends_hbm, state_hbm, projector_hbm, coupled_hbm, slot_hbm, couplings_hbm,
    payload, index, table, coefficients,
    ends, state, projector, coupled, slot, couplings, sems,
):
    copies = fetch(
        (
            (coupled_hbm, coupled), (slot_hbm, slot), (projector_hbm, projector), (state_hbm, state),
            (couplings_hbm, couplings), (ends_hbm, ends),
        ),
        sems,
    )
    per_device, width = state.shape[0], state.shape[1]
    count = slot.shape[1]
    pair_count, orb_count = lax.axis_size("pairs"), lax.axis_size("orb")
    pair_idx, orb_idx = lax.axis_index("pairs"), lax.axis_index("orb")
    group = orb_count * per_device
    lanes_out = index.shape[1]
    copies[0].wait()
    copies[1].wait()
    slots = slot[...]
    wanted = coupled[...]
    lanes = lax.broadcasted_iota(jnp.int32, (1, count), 1)
    members = lax.broadcasted_iota(jnp.int32, (group, 1), 0)
    slot_ids = lax.broadcasted_iota(jnp.int32, (count, lanes_out), 0)
    column = lax.broadcasted_iota(jnp.int32, (count, lanes_out), 1)
    dest = column ^ pair_idx if direct else column
    owner = (slot_ids // per_device == dest * orb_count + orb_idx) & (column < pair_count)
    for m, flip in enumerate(mirrors):
        base = (pair_idx ^ flip) * group
        pairs = jnp.sum(jnp.where(slots == base + members, lanes, 0), axis=1, keepdims=True)
        hits = jnp.zeros((group, count), F32)
        for g in range(group):
            hit = jnp.max((wanted == pairs[g : g + 1, :]).astype(F32), axis=0, keepdims=True)
            hits = jnp.where(members == g, hit, hits)
        needed = jnp.dot(hits, owner.astype(F32), preferred_element_type=F32) > 0.5
        run = jnp.zeros((1, lanes_out), jnp.int32)
        picked = [jnp.zeros((1, lanes_out), jnp.int32) for _ in range(capacity)]
        for g in range(group):
            hit = needed[g : g + 1, :].astype(jnp.int32)
            for c in range(capacity):
                picked[c] = picked[c] + jnp.where((hit == 1) & (run == c), g, 0)
            run = run + hit
        for c, row in enumerate(picked):
            index[pl.ds(m * capacity + c, 1), :] = row

    eye = eye_mask(count)
    slots_c = jnp.sum(jnp.where(eye, slots, 0), axis=1, keepdims=True)
    first = (pair_idx * orb_count + orb_idx) * per_device
    entries = []
    mine = jnp.zeros((1, count), F32)
    for i in range(per_device):
        own = jnp.sum(jnp.where(lanes == first + i, wanted, 0), axis=1, keepdims=True)
        entries.append((own == lanes).astype(F32))
        mine = jnp.maximum(mine, jnp.max(entries[i], axis=0, keepdims=True))
    mine_c = to_column(mine, eye)
    before = (slots_c // group == slots // group) & (slots_c < slots)
    rank = jnp.sum(jnp.where(before, mine_c, 0.0), axis=0, keepdims=True).astype(jnp.int32)
    source = slots // group
    flip = source ^ pair_idx
    place = jnp.where(flip < near, source ^ (pair_idx & ~(near - 1)), flip) * capacity + rank
    place = place.astype(F32)
    neighbours = coupled.shape[0]
    ids = lax.broadcasted_iota(jnp.int32, (neighbours, 1), 0)
    square = eye_mask(neighbours)
    column = lax.broadcasted_iota(jnp.int32, (neighbours, lanes_out), 1)
    copies[4].wait()
    for i in range(per_device):
        found = jnp.sum(entries[i] * place, axis=1, keepdims=True).astype(jnp.int32)
        match = found == column
        table[pl.ds(i, 1), :] = jnp.sum(jnp.where(match, ids, 0), axis=0, keepdims=True)
        value = to_column(couplings[pl.ds(i, 1), :], square)
        coefficients[pl.ds(i, 1), :] = jnp.sum(jnp.where(match, value, 0.0), axis=0, keepdims=True)

    eye = eye_mask(width)
    copies[2].wait()
    copies[3].wait()
    copies[5].wait()
    total = jnp.zeros((orbitals, width), F32)
    counts_a = end_counts(orbitals, per_device, lambda s: ends[0, s])
    counts_b = end_counts(orbitals, per_device, lambda s: ends[1, s])
    for s in range(per_device):
        block = state[s]
        payload[pl.ds(s * width, width), :] = block.astype(BF16)
        total += singles_terms(block, projector[pl.ds(s, 1), :], counts_a[s] + counts_b[s], eye)
    tail = payload.shape[0] - per_device * width
    payload[pl.ds(per_device * width, tail), :] = tail_rows(total, tail)


def select_kernel(capacity, per_device, orbitals, width, lanes, row, swap, index, gathered, outs):
    blocks = per_device * width
    tail = gathered.shape[1] - blocks
    total = join_parts(gathered[0, pl.ds(blocks, tail), :], orbitals)
    for d in range(1, gathered.shape[0]):
        total += join_parts(gathered[d, pl.ds(blocks, tail), :], orbitals)
    rows = tail_rows(total, tail)
    for lane, out in zip(lanes, outs):
        for c in range(capacity):
            j = index[row + c, lane]
            first = pl.multiple_of((j % per_device) * width, ROWS)
            out[pl.ds(c * width, width), :] = gathered[(j // per_device) ^ swap, pl.ds(first, width), :]
        out[pl.ds(capacity * width, tail), :] = rows


def add_blocks(capacity, orbitals, index, coefficients, intersections, blocks, coupling, singles):
    per_device, width = intersections.shape[0], intersections.shape[2]
    slots = [(place * capacity + c, ref, c * width) for place, ref in blocks for c in range(capacity)]
    wide = [[] for _ in range(per_device)]
    scaled = [[] for _ in range(per_device)]
    empty = jnp.zeros((width, width), BF16)
    for p in range(0, len(slots), 2):
        part = slots[p : p + 2]
        mixing = [
            jnp.concatenate([intersections[s, index[s, lane]] for lane, _, _ in part], axis=1)
            for s in range(per_device)
        ]
        near = [ref[pl.ds(row, width), :] for _, ref, row in part]
        if len(part) == 2:
            near = jnp.concatenate(
                [jnp.concatenate([near[0], empty], axis=1), jnp.concatenate([empty, near[1]], axis=1)], axis=0
            )
        else:
            near = near[0]
        lifted = jnp.dot(jnp.concatenate(mixing, axis=0), near, preferred_element_type=F32)
        for s in range(per_device):
            wide[s].append(mixing[s])
            for i, (lane, _, _) in enumerate(part):
                block = lifted[s * width : (s + 1) * width, i * width : (i + 1) * width]
                scaled[s].append((coefficients[s, lane] * block).astype(BF16))
    for s in range(per_device):
        if slots:
            coupling[s] = coupling[s] + lax.dot_general(
                jnp.concatenate(scaled[s], axis=1), jnp.concatenate(wide[s], axis=1),
                (((1,), (1,)), ((), ())), preferred_element_type=F32,
            )
    for _, ref in blocks:
        tail = ref.shape[0] - capacity * width
        singles = singles + join_parts(ref[pl.ds(capacity * width, tail), :], orbitals)
    return singles


def gather_terms(capacity, orbitals, index, coefficients, intersections, every, places, blocks, before):
    per_device, width = intersections.shape[0], intersections.shape[2]
    coupling = [jnp.zeros((width, width), F32) for _ in range(per_device)]
    singles = jnp.zeros((orbitals, width), F32)
    if before is not None:
        coupling = [before[pl.ds(s * width, width), :] for s in range(per_device)]
        singles = before[pl.ds(per_device * width, orbitals), :]
    operands = (capacity, orbitals, index, coefficients, intersections)
    if every is not None:
        unit = min(every.shape[0], 4)

        def step(i, carry):
            parts = list(carry[:-1])
            some = [(i * unit + u, every.at[i * unit + u]) for u in range(unit)]
            total = add_blocks(*operands, some, parts, carry[-1])
            return (*parts, total)

        *coupling, singles = lax.fori_loop(0, every.shape[0] // unit, step, (*coupling, singles))
    singles = add_blocks(*operands, list(zip(places, blocks)), coupling, singles)
    return coupling, singles


def add_ready(capacity, orbitals, wide, rows, blocks, coupling, singles):
    per_device, width = wide.shape[0], wide.shape[1]
    slots = [(ref, c * width) for ref in blocks for c in range(capacity)]
    scaled = [[] for _ in range(per_device)]
    empty = jnp.zeros((width, width), BF16)
    for p in range(0, len(slots), 2):
        near = [ref[pl.ds(row, width), :] for ref, row in slots[p : p + 2]]
        lanes = pl.ds(p * width, len(near) * width)
        if len(near) == 2:
            near = jnp.concatenate(
                [jnp.concatenate([near[0], empty], axis=1), jnp.concatenate([empty, near[1]], axis=1)], axis=0
            )
        else:
            near = near[0]
        mixing = jnp.concatenate([wide[s, :, lanes] for s in range(per_device)], axis=0)
        lifted = jnp.dot(mixing, near, preferred_element_type=F32)
        for s in range(per_device):
            block = lifted[s * width : (s + 1) * width]
            scaled[s].append((rows[pl.ds(s, 1), lanes] * block).astype(BF16))
    for s in range(per_device):
        coupling[s] = coupling[s] + lax.dot_general(
            jnp.concatenate(scaled[s], axis=1), wide[s], (((1,), (1,)), ((), ())), preferred_element_type=F32
        )
    for ref in blocks:
        tail = ref.shape[0] - capacity * width
        singles = singles + join_parts(ref[pl.ds(capacity * width, tail), :], orbitals)
    return singles


def terms_kernel(capacity, orbitals, has_every, places, later, index, coefficients, intersections, *refs):
    refs = list(refs)
    if later:
        rows, wide = refs.pop(), refs.pop()
        per_device, width = intersections.shape[0], intersections.shape[2]
        for j, lane in enumerate([place * capacity + c for place in later for c in range(capacity)]):
            lanes = pl.ds(j * width, width)
            for s in range(per_device):
                wide[s, :, lanes] = intersections[s, index[s, lane]]
                rows[pl.ds(s, 1), lanes] = jnp.full((1, width), coefficients[s, lane], F32)
    out = refs.pop()
    every = refs.pop(0) if has_every else None
    coupling, singles = gather_terms(
        capacity, orbitals, index, coefficients, intersections, every, places, refs, None
    )
    width = intersections.shape[2]
    for s, part in enumerate(coupling):
        out[pl.ds(s * width, width), :] = part
    out[pl.ds(len(coupling) * width, orbitals), :] = singles


def update_kernel(
    last, capacity, orbitals, count,
    ends, before, *refs,
):
    if count:
        wide, rows, refs = refs[0], refs[1], refs[2:]
    blocks = refs[:count]
    state, integrals, energies, projector, out_a, out_b = refs[count : count + 6]
    final = out_a, out_b
    if last:
        out_a, out_b, sems = refs[-3:]
    copies = []
    per_device, width = state.shape[0], state.shape[1]
    coupling = [before[pl.ds(s * width, width), :] for s in range(per_device)]
    singles = before[pl.ds(per_device * width, orbitals), :]
    if count:
        singles = add_ready(capacity, orbitals, wide, rows, blocks, coupling, singles)
    eye = eye_mask(width)
    total = jnp.zeros((orbitals, width), F32)
    counts_a = end_counts(orbitals, per_device, lambda s: ends[0, s])
    counts_b = end_counts(orbitals, per_device, lambda s: ends[1, s])
    for s in range(per_device):
        old = state[s]
        energy = energies[pl.ds(s, 1), :]
        energy_c = to_column(energy, eye)
        proj = projector[pl.ds(s, 1), :]
        proj_c = to_column(proj, eye)
        left = jnp.sum(counts_a[s] * singles, axis=0, keepdims=True)
        right = jnp.sum(counts_b[s] * singles, axis=0, keepdims=True)
        residual = (
            integrals[s].astype(F32) + energy_c * old + old * energy - coupling[s]
            + to_column(left, eye) * proj + proj_c * right
        )
        new = old - residual / (energy_c + energy)
        out_a[s] = new
        if last:
            out_b[s] = residual
            for i in range(2):
                copies.append(pltpu.make_async_copy((out_a, out_b)[i].at[s], final[i].at[s], sems.at[i, s]))
                copies[-1].start()
        else:
            out_b[pl.ds(s * width, width), :] = new.astype(BF16)
            total += singles_terms(new, proj, counts_a[s] + counts_b[s], eye)
    for copy in copies:
        copy.wait()
    if not last:
        tail = out_b.shape[0] - per_device * width
        out_b[pl.ds(per_device * width, tail), :] = tail_rows(total, tail)


def tail_size(orbitals):
    return -(-PARTS * orbitals // ROWS) * ROWS


def cost(flops):
    return pl.CostEstimate(flops=flops, bytes_accessed=0, transcendentals=0)


def body(
    amplitudes, integrals, energies, intersections, couplings, projector, pair_orbitals, coupled, pair_slot,
):
    pair_count = lax.axis_size("pairs")
    per_device, width = amplitudes.shape[0], amplitudes.shape[1]
    total, neighbours = coupled.shape
    capacity = 1 + neighbours // pair_count
    orbitals = total // PAIRS_ORB
    tail = tail_size(orbitals)
    stride = capacity * width + tail
    orb_count = lax.axis_size("orb")
    direct = pair_count in (4, 8) and orb_count == 4
    tables = VMEM if direct else SMEM
    half = pair_count // 2
    mirrors = [0, half] if direct else [0]
    near = 1 if direct else pair_count
    lanes = -(-pair_count * capacity // 128) * 128
    ends = pair_orbitals.T
    small = pltpu.CompilerParams(vmem_limit_bytes=SMALL)
    params = pltpu.CompilerParams(vmem_limit_bytes=LIMIT)
    block_shape = jax.ShapeDtypeStruct((stride, width), BF16)
    terms_shape = jax.ShapeDtypeStruct((per_device * width + -(-orbitals // 8) * 8, width), F32)
    payload_shape = jax.ShapeDtypeStruct((per_device * width + tail, width), BF16)
    payload, send_index, index, coefficients = pl.pallas_call(
        functools.partial(setup_kernel, capacity, orbitals, near, mirrors, direct),
        out_shape=(
            payload_shape,
            jax.ShapeDtypeStruct((-(-len(mirrors) * capacity // 8) * 8, lanes), jnp.int32),
            jax.ShapeDtypeStruct((per_device, lanes), jnp.int32),
            jax.ShapeDtypeStruct((per_device, lanes), F32),
        ),
        in_specs=[HBM] * 6,
        out_specs=[VMEM] * 4,
        scratch_shapes=[
            pltpu.VMEM(ends.shape, jnp.int32),
            pltpu.VMEM(amplitudes.shape, F32),
            pltpu.VMEM(projector.shape, F32),
            pltpu.VMEM((neighbours, total), jnp.int32),
            pltpu.VMEM((1, total), jnp.int32),
            pltpu.VMEM(couplings.shape, F32),
            pltpu.SemaphoreType.DMA((6,)),
        ],
        compiler_params=small if direct else pltpu.CompilerParams(vmem_limit_bytes=WHOLE),
        name="setup",
    )(
        *[
            pltpu.with_memory_space_constraint(x, pltpu.HBM)
            for x in (ends, amplitudes, projector, coupled.T, pair_slot.reshape(1, total), couplings)
        ]
    )

    def join(*parts, after=()):
        def kernel(*refs):
            if len(parts) == 1:
                refs[-1][...] = refs[0][...]
            else:
                for i in range(len(parts)):
                    refs[-1][i] = refs[i][...]

        shape = payload_shape.shape if len(parts) == 1 else (len(parts), *payload_shape.shape)
        return pl.pallas_call(
            kernel,
            out_shape=jax.ShapeDtypeStruct(shape, BF16),
            in_specs=[VMEM] * len(parts) + [ANY] * len(after),
            out_specs=VMEM,
            compiler_params=small,
            cost_estimate=cost(0),
            name="join",
        )(*parts, *after)

    def select(row, flips, gathered):
        def kernel(index, source, *refs):
            outs, held = refs[: len(flips)], refs[-1]
            swap = 0
            if row:
                swap = lax.axis_index("orb") // 2 * 2
                for c in range(2):
                    for x in range(2):
                        held[2 * x + c] = source[c, x]
            else:
                held = source
            select_kernel(capacity, per_device, orbitals, width, flips, row, swap, index, held, outs)

        return pl.pallas_call(
            kernel,
            out_shape=[block_shape] * len(flips),
            in_specs=[VMEM, VMEM],
            out_specs=[VMEM] * len(flips),
            scratch_shapes=[pltpu.VMEM((4, *payload_shape.shape), BF16)],
            compiler_params=small,
            cost_estimate=cost(0),
            name="select",
        )(send_index, gathered)

    def select_all(gathered):
        def kernel(index, source, out):
            outs = [out.at[i] for i in range(pair_count)]
            select_kernel(capacity, per_device, orbitals, width, range(pair_count), 0, 0, index, source, outs)

        return pl.pallas_call(
            kernel,
            out_shape=jax.ShapeDtypeStruct((pair_count, stride, width), BF16),
            in_specs=[VMEM, VMEM],
            out_specs=VMEM,
            compiler_params=small,
            name="select",
        )(send_index, gathered)

    def exchange(block, axis, flip):
        return lax.ppermute(block, axis, [(p, p ^ flip) for p in range(lax.axis_size(axis))])

    def terms(every, places, blocks, later):
        span = len(later) * capacity * width
        ready = [jax.ShapeDtypeStruct((per_device, width, span), BF16), jax.ShapeDtypeStruct((per_device, span), F32)]
        shapes = [terms_shape, *(ready if later else [])]
        extra = [] if every is None else [every]
        return pl.pallas_call(
            functools.partial(terms_kernel, capacity, orbitals, every is not None, places, later),
            out_shape=shapes,
            in_specs=[tables, tables] + [VMEM] * (1 + len(extra) + len(blocks)),
            out_specs=[VMEM] * len(shapes),
            cost_estimate=cost(TERMS_COST),
            compiler_params=params,
            name="terms",
        )(index, coefficients, intersections, *extra, *blocks)

    state = amplitudes
    for step in range(ITERS):
        last = step == ITERS - 1
        late = []
        if direct:
            mirror = exchange(payload, "pairs", half)
            flips = list(range(half))
            cores = [[o, o + 1] for o in range(0, orb_count, 2)]
            held = lax.all_gather(payload, "orb", axis=0, tiled=False)
            across = pair_count - 1
            order = [0, half - 1, across, *range(1, half - 1)]
            sent = select(0, order, held)
            arrived = [sent[0]] + [exchange(part, "pairs", flip) for flip, part in zip(order[1:], sent[1:])]
            mirror = join(mirror, after=sent[:1])
            held = join(mirror, exchange(mirror, "orb", 2), after=arrived[:1])
            held = lax.all_gather(held, "orb", axis=0, axis_index_groups=cores)
            close = [flip for flip in flips if flip + half != across]
            sent = select(capacity, close, held)
            later = [half + flip for flip in close[1:]]
            partial = terms(None, [*order, half], arrived + [sent[0]], later)
            late = [exchange(part, "pairs", flip) for flip, part in zip(close[1:], sent[1:])]
        else:
            gathered = lax.all_gather(payload, "orb", axis=0, tiled=False)
            outgoing = select_all(gathered)
            every = lax.all_to_all(outgoing, "pairs", split_axis=0, concat_axis=0, tiled=True)
            partial = terms(every, [], [], [])
        second = jax.ShapeDtypeStruct(amplitudes.shape, F32) if last else payload_shape
        state, payload = pl.pallas_call(
            functools.partial(update_kernel, last, capacity, orbitals, len(late)),
            out_shape=(jax.ShapeDtypeStruct(amplitudes.shape, F32), second),
            in_specs=[VMEM] * (5 + len(partial) + len(late)),
            out_specs=(HBM, HBM) if last else (VMEM, VMEM),
            scratch_shapes=[
                pltpu.VMEM(amplitudes.shape, F32),
                pltpu.VMEM(amplitudes.shape, F32),
                pltpu.SemaphoreType.DMA((2, per_device)),
            ]
            if last
            else [],
            compiler_params=params,
            name="update",
        )(
            ends, *partial, *late, state, integrals, energies, projector,
        )
    return state, payload


def solution(mesh):
    split = ("pairs", "orb")
    return jax.shard_map(
        body,
        mesh=mesh,
        in_specs=(
            P(split, None, None),
            P(split, None, None),
            P(split, None),
            P(split, None, None, None),
            P(split, None),
            P(split, None),
            P(split, None),
            P(),
            P(),
        ),
        out_specs=(P(split, None, None), P(split, None, None)),
        check_vma=False,
    )
```
